128 devices in a mesh: row: 8 (over z, x_hi), col: 16 (over y, x_lo, core).
Axes of the slice: x: 4 (x_hi: 2, x_lo: 2; x = x_hi * 2 + x_lo), y: 4, z: 4, core: 2. Of those that a mesh axis runs over, the one named last changes fastest.
Arguments:
- tokens: bfloat16 [16384, 1024], P(('row', 'col')), may hold values from -6 to 6
- cotangent: bfloat16 [16384, 1024], P(('row', 'col')), may hold values from -6 to 6
- deal_order: int32 [8, 2048], P('row'), may hold values from 0 to 2047, as said below
- lengths: int32 [8, 4], P('row'), may hold values from 1 to 1024, 2048 in all within a row
- routes: int32 [16384, 8], P(('row', 'col')), may hold values from 0 to 31, all different within a row; in each aligned block of 128 rows (0 to 127, 128 to 255, ...) at most 64 rows name the same one
- route_gates: float32 [16384, 8], P(('row', 'col')), may hold values from 0.25 to 0.75
- gain_first: float32 [1024], replicated, may hold values from 0.1 to 1.9
- gain_second: float32 [1024], replicated, may hold values from 0.1 to 1.9
- gain_query: float32 [64], replicated, may hold values from 0.1 to 1.9
- gain_key: float32 [64], replicated, may hold values from 0.1 to 1.9
- weight_qkv: float32 [1024, 2048], P('row', 'col'), may hold values from -0.1875 to 0.1875
- weight_out: float32 [1024, 1024], P('row', 'col'), may hold values from -1.5 to 1.5
- weight_gate: float32 [1024, 32, 512], P('row', 'col'), may hold values from -0.1875 to 0.1875
- weight_up: float32 [1024, 32, 512], P('row', 'col'), may hold values from -0.1875 to 0.1875
- weight_down: float32 [1024, 32, 512], P('row', 'col'), may hold values from -0.25 to 0.25
Outputs:
- block_out: bfloat16 [16384, 1024], P(('row', 'col'))
- input_grad: bfloat16 [16384, 1024], P(('row', 'col'))
- grad_first: float32 [1024], replicated
- grad_second: float32 [1024], replicated
- grad_query: float32 [64], replicated
- grad_key: float32 [64], replicated
- grad_qkv: float32 [1024, 2048], P('row', 'col')
- grad_out: float32 [1024, 1024], P('row', 'col')
- grad_gate: float32 [1024, 32, 512], P('row', 'col')
- grad_up: float32 [1024, 32, 512], P('row', 'col')
- grad_down: float32 [1024, 32, 512], P('row', 'col')
The draws below stay inside these ranges and needn't reach their ends.
Inputs may be any that keep to these rules, and one draw needn't show every extreme that they name: `deal_order`: each row is a permutation of 0 to 2047. With the slots and the given rows of a group cut into 16 blocks of 128, every block of slots takes exactly 8 rows of every block of given rows. `routes`: within the rows of one device no expert is named more than 64 times; some device names some expert exactly 64 times. `lengths`: each row sums to 2048.
All inputs are finite; a program needn't handle non-finite values.
Results may differ from the reference program's by a relative error of at most 0.025.
Values may be sent and summed in bfloat16 or wider, within the bound.
No kernel may reach another device: no remote copies, remote signals or barrier semaphores. Data moves between devices by JAX's collectives and lax.ppermute only.
A program may use at most 128 MiB of HBM per device.

```python
import math
from functools import partial
import jax
import jax.numpy as jnp
import numpy as np
from jax import lax

D = 1024
HEADS = 16
KV_HEADS = 8
HEAD_DIM = 64
EXPERTS = 32
FF = 512
TOP = 8
TOK_DEV = 128
SEQ_GROUP = 4
GROUP_TOK = 2048
TOKENS = 16384
CAP = 64
N_ROW = 8
N_COL = 16


def shuffle_row(subkey):
    return jax.random.permutation(subkey, TOK_DEV)


def deal_group(group_key):
    share = TOK_DEV // N_COL
    subkeys = jax.random.split(group_key, 2 * N_COL)
    local = jax.vmap(shuffle_row)(subkeys[:N_COL])
    anchor = local + (jnp.arange(N_COL, dtype=jnp.int32) * TOK_DEV)[:, None]
    bundled = anchor.reshape(N_COL, N_COL, share).transpose(1, 0, 2).reshape(N_COL, TOK_DEV)
    mixing = jax.vmap(shuffle_row)(subkeys[N_COL:])
    return jnp.take_along_axis(bundled, mixing, axis=1).reshape(GROUP_TOK)


def draw_deal_order(key, part):
    key = jax.random.fold_in(key, 11)
    return jax.vmap(deal_group)(jax.random.split(key, N_ROW)).astype(jnp.int32)


def shard_levels(key, shape, cuts, low, top_value):
    loudness = 1.0
    for axis_at, parts in cuts:
        draws = jax.random.uniform(jax.random.fold_in(jax.random.fold_in(key, 6), axis_at), (parts,), jnp.float32, low / len(cuts), top_value / len(cuts))
        loudness = loudness * jnp.repeat(jnp.exp(draws), shape[axis_at] // parts).reshape((-1,) + (1,) * (len(shape) - 1 - axis_at))
    return loudness


def length_profile(count, total, most, slope):
    loads = [(1 << 20) // math.isqrt(grade ** slope) + 1 for grade in range(2, count + 1)]
    spare, counts = total - most - (count - 1), [1] * (count - 1)
    while spare > 0:
        movable = [i for i in range(count - 1) if counts[i] < most]
        mass, budget = sum([loads[i] for i in movable]), spare
        for i in movable:
            extra = min(most - counts[i], max(1, budget * loads[i] // mass), spare)
            counts[i] = counts[i] + extra
            spare = spare - extra
    return np.array([most] + counts)


def uneven(own_key, number_of, total, most, lean):
    if number_of == 2:
        one = jax.random.randint(own_key, (), max(1, total - most), min(most, total - 1) + 1)
        return jnp.stack([one, total - one])
    sizes = jnp.asarray(length_profile(number_of, total, most, lean), jnp.int32)
    pairs = (number_of - 1) // 2
    giver, receiver = sizes[1:1 + 2 * pairs:2], sizes[2:2 + 2 * pairs:2]
    room = jnp.minimum(giver - 1, most - receiver)
    passed = jax.random.randint(jax.random.fold_in(own_key, 1), (pairs,), 0, 1 << 20) % (room + 1)
    sizes = sizes.at[1:1 + 2 * pairs:2].set(giver - passed).at[2:2 + 2 * pairs:2].set(receiver + passed)
    return sizes[jax.random.permutation(jax.random.fold_in(own_key, 2), number_of)]


def shared_out(key, own, number, rows, count, top, most, slope):
    sequence = jax.random.permutation(key, count)
    packed, common = load_shares(count, rows * top, most, slope, True), load_shares(count, rows * top, most, slope, False)
    places = jnp.arange(count)

    def named(sizes, rotation):
        used = int((sizes > 0).sum())
        fixed = max(1, used // 4)
        moved = fixed + (places - fixed + rotation * (used - fixed)) % max(1, count - fixed)
        return jnp.zeros((count,), jnp.int32).at[sequence[jnp.where(places < fixed, places, moved)]].set(jnp.asarray(sizes, jnp.int32))

    sizes = jnp.where(number % 4 == 0, named(packed, number // 4), named(common, number - number // 4 - 1))
    mixed = jax.random.permutation(jax.random.fold_in(own, 3), count)
    giver, sink = mixed[0:count // 2 * 2:2], mixed[1:count // 2 * 2:2]
    slack = jnp.minimum(sizes[giver] - 1, most - sizes[sink]) // 2
    slack = jnp.where((giver == sequence[0]) | (sink == sequence[0]) | (sizes[sink] == 0), 0, jnp.maximum(slack, 0))
    moved = jax.random.randint(jax.random.fold_in(own, 4), (count // 2,), 0, 1 << 20) % (slack + 1)
    sizes = sizes.at[giver].add(-moved).at[sink].add(moved)
    members = jnp.searchsorted(jnp.cumsum(sizes), jnp.arange(rows * top), side="right").astype(jnp.int32)
    grid = members.reshape(top, rows).T
    grid = grid[jax.random.permutation(jax.random.fold_in(own, 1), rows)]
    rotation = jax.random.randint(jax.random.fold_in(own, 2), (rows, 1), 0, top)
    return jnp.take_along_axis(grid, (jnp.arange(top)[None, :] + rotation) % top, axis=1)


def load_shares(number_of, total, most, lean, full):
    portions = [(1 << 20) // math.isqrt(standing ** lean) + 1 for standing in range(1, number_of + 1)]
    largest = most if full else min(most, max(-(-total // number_of), total * portions[0] // sum(portions)))
    least = 1 if total - largest >= number_of - 1 else 0
    given, rest = [largest] + [least] * (number_of - 1), total - largest - least * (number_of - 1)
    while rest > 0:
        candidates = [i for i in range(1, number_of) if given[i] < largest] or [i for i in range(1, number_of) if given[i] < most]
        pool, budget = sum([portions[i] for i in candidates]), rest
        for i in candidates:
            addition = min(most - given[i], max(1, budget * portions[i] // pool), rest)
            given[i] = given[i] + addition
            rest = rest - addition
    return np.array(given)


def scatter_about(own_key, dims, spread, reach, cuts=(), kind=jnp.bfloat16):
    values = spread * jax.random.normal(own_key, dims, jnp.float32)
    if cuts:
        values = values * shard_levels(own_key, dims, cuts, -0.22, 0.18)
    return jnp.clip(values, -reach, reach).astype(kind)


def setup_inputs(seed: int = 0) -> dict:
    seeds = jax.random.split(jax.random.key(seed), 16)
    tokens = scatter_about(seeds[0], (TOKENS, D), 1.0, 6.0, ((0, 128),))
    cotangent = scatter_about(seeds[1], (TOKENS, D), 1.0, 6.0, ((0, 128),))
    deal_order = draw_deal_order(jax.random.fold_in(seeds[15], 71), 0)
    lengths = jax.vmap(lambda own: uneven(own, SEQ_GROUP, GROUP_TOK, GROUP_TOK // 2, 2))(jax.random.split(seeds[3], N_ROW)).reshape((N_ROW, SEQ_GROUP)).astype(jnp.int32)
    routes_keys = jax.random.split(jax.random.fold_in(seeds[4], 1), TOKENS // TOK_DEV)
    routes_turns = jax.random.permutation(jax.random.fold_in(seeds[4], 3), TOKENS // TOK_DEV)
    routes = jax.vmap(lambda own, number: shared_out(jax.random.fold_in(seeds[4], 2), own, number, TOK_DEV, EXPERTS, TOP, CAP, 1))(routes_keys, routes_turns).reshape((TOKENS, TOP))
    route_gates = jnp.clip(0.25 + 0.5 * jax.random.uniform(seeds[5], (TOKENS, TOP), jnp.float32) ** shard_levels(seeds[5], (TOKENS, TOP), ((0, 128),), -0.2, 0.2), 0.25, 0.75)
    gain_first = jnp.clip(1.0 + 0.18 * jax.random.normal(seeds[6], (D,), jnp.float32), 0.1, 1.9)
    gain_second = jnp.clip(1.0 + 0.18 * jax.random.normal(seeds[7], (D,), jnp.float32), 0.1, 1.9)
    gain_query = jnp.clip(1.0 + 0.18 * jax.random.normal(seeds[8], (HEAD_DIM,), jnp.float32), 0.1, 1.9)
    gain_key = jnp.clip(1.0 + 0.18 * jax.random.normal(seeds[9], (HEAD_DIM,), jnp.float32), 0.1, 1.9)
    weight_qkv = scatter_about(seeds[10], (D, 4 * KV_HEADS * HEAD_DIM), D ** -0.5, 0.1875, ((0, 8), (1, 16)), jnp.float32)
    weight_out = scatter_about(seeds[11], (D, HEADS * HEAD_DIM), (HEADS * HEAD_DIM // 64) ** -0.5, 1.5, ((0, 8), (1, 16)), jnp.float32)
    weight_gate = scatter_about(seeds[12], (D, EXPERTS, FF), D ** -0.5, 0.1875, ((0, 8), (1, 16)), jnp.float32)
    weight_up = scatter_about(seeds[13], (D, EXPERTS, FF), D ** -0.5, 0.1875, ((0, 8), (1, 16)), jnp.float32)
    weight_down = scatter_about(seeds[14], (D, EXPERTS, FF), FF ** -0.5, 0.25, ((0, 8), (1, 16)), jnp.float32)
    return {"tokens": tokens, "cotangent": cotangent, "deal_order": deal_order, "lengths": lengths, "routes": routes, "route_gates": route_gates, "gain_first": gain_first, "gain_second": gain_second, "gain_query": gain_query, "gain_key": gain_key, "weight_qkv": weight_qkv, "weight_out": weight_out, "weight_gate": weight_gate, "weight_up": weight_up, "weight_down": weight_down}


@jax.custom_vjp
def low(v):
    return lax.optimization_barrier(v.astype(jnp.bfloat16)).astype(jnp.float32)

@jax.custom_vjp
def low_back(v):
    return v

def low_keep(v):
    return (low(v), None)

def low_pass(kept, grad):
    return (grad,)

def back_keep(v):
    return (v, None)

def back_low(kept, grad):
    return (low(grad),)
low.defvjp(low_keep, low_pass)
low_back.defvjp(back_keep, back_low)
EPS_WIDE = 1e-05
EPS_HEAD = 1e-06
THETA = 10000.0
MASKED = -1e+30

def product(left, right):
    return jnp.dot(left, right, precision=lax.Precision.HIGHEST, preferred_element_type=jnp.float32)

def norm_rows(values, scales, epsilon):
    factor = lax.rsqrt(lax.optimization_barrier(jnp.mean(values * values, axis=-1, keepdims=True)) + epsilon)
    return values * factor * scales

def rotary(values, cosine_table, sine_table):
    middle = values.shape[-1] // 2
    leading = values[..., :middle]
    trailing = values[..., middle:]
    return jnp.concatenate([leading * cosine_table - trailing * sine_table, trailing * cosine_table + leading * sine_table], axis=-1)

def tables(lengths_row, amount, head_width):
    finish = jnp.cumsum(lengths_row)
    starts = finish - lengths_row
    positions = jnp.arange(amount, dtype=jnp.int32)
    segment = lax.optimization_barrier(jnp.sum((positions[:, None] >= finish[None, :]).astype(jnp.int32), axis=1))
    labels = jnp.arange(lengths_row.shape[0], dtype=jnp.int32)
    anchor = lax.optimization_barrier(jnp.sum(jnp.where(segment[:, None] == labels[None, :], starts[None, :], 0), axis=1))
    offset = (positions - anchor).astype(jnp.float32)
    frequency = THETA ** (-jnp.arange(head_width // 2, dtype=jnp.float32) * 2.0 / head_width)
    angles = offset[:, None] * frequency[None, :]
    return (segment, jnp.cos(angles), jnp.sin(angles))

def attend_group(normed_rows, lengths_row, weight_qkv, weight_out, gain_query, gain_key):
    amount = normed_rows.shape[0]
    segment, cosine_table, sine_table = tables(lengths_row, amount, HEAD_DIM)
    raw = low_back(product(normed_rows, low(weight_qkv))).reshape(amount, KV_HEADS, 4, HEAD_DIM)
    turn_cos = cosine_table[:, None, :]
    turn_sin = sine_table[:, None, :]
    query = raw[:, :, 0:2, :].reshape(amount, HEADS, HEAD_DIM)
    query = low(rotary(norm_rows(query, gain_query, EPS_HEAD), turn_cos, turn_sin))
    keys = low(rotary(norm_rows(raw[:, :, 2, :], gain_key, EPS_HEAD), turn_cos, turn_sin))
    values = low(raw[:, :, 3, :])
    keys = jnp.repeat(keys, 2, axis=1)
    values = jnp.repeat(values, 2, axis=1)
    same = segment[:, None] == segment[None, :]

    def one_head(operands):
        head_query, head_keys, head_values = operands
        scores = low_back(product(head_query, head_keys.T) * HEAD_DIM ** (-0.5))
        scores = jnp.where(same, scores, MASKED)
        highest = lax.optimization_barrier(jnp.max(scores, axis=1, keepdims=True))
        weights = jnp.exp(scores - highest)
        probs = weights / lax.optimization_barrier(jnp.sum(weights, axis=1, keepdims=True))
        return low(low_back(product(low(probs), head_values)))
    heads_out = lax.map(jax.checkpoint(one_head), (query.transpose(1, 0, 2), keys.transpose(1, 0, 2), values.transpose(1, 0, 2)))
    joined = heads_out.transpose(1, 0, 2).reshape(amount, HEADS * HEAD_DIM)
    return low_back(product(joined, low(weight_out).T))

def layer(tokens_full, gain_first, gain_second, gain_query, gain_key, weight_qkv, weight_out, weight_gate, weight_up, weight_down, deal_order=None, inverse=None, lengths=None, combine=None):
    grouped = tokens_full.reshape(N_ROW, GROUP_TOK, D)
    dealt = jnp.take_along_axis(grouped, deal_order[:, :, None], axis=1)
    gate_stack = weight_gate.transpose(1, 0, 2)
    up_stack = weight_up.transpose(1, 0, 2)
    down_stack = weight_down.transpose(1, 0, 2)

    def group_layer(operands):
        rows_in, lengths_row, shares = operands
        normed_rows = low(norm_rows(rows_in, gain_first, EPS_WIDE))
        hidden = rows_in + attend_group(normed_rows, lengths_row, weight_qkv, weight_out, gain_query, gain_key)
        middle = low(norm_rows(hidden, gain_second, EPS_WIDE))

        def expert_step(running, pieces):
            gate_cols, up_cols, down_cols, share_col = pieces
            entry = low_back(middle)
            gate_pre = low_back(product(entry, low(gate_cols)))
            up_pre = low_back(product(entry, low(up_cols)))
            inner = low(jax.nn.silu(gate_pre) * up_pre)
            result = low(low_back(product(inner, low(down_cols).T)))
            return (running + share_col[:, None] * result, None)
        mixed, _ = lax.scan(jax.checkpoint(expert_step), jnp.zeros_like(hidden), (gate_stack, up_stack, down_stack, shares.T))
        return hidden + mixed
    outcome = lax.map(jax.checkpoint(group_layer), (dealt, lengths, combine.reshape(N_ROW, GROUP_TOK, EXPERTS)))
    given = jnp.take_along_axis(outcome, inverse[:, :, None], axis=1)
    return given.reshape(N_ROW * GROUP_TOK, D)

def reference(tokens, cotangent, deal_order, lengths, routes, route_gates, gain_first, gain_second, gain_query, gain_key, weight_qkv, weight_out, weight_gate, weight_up, weight_down):
    inverse = jnp.argsort(deal_order, axis=1).astype(jnp.int32)
    labels = jnp.arange(EXPERTS, dtype=jnp.int32)
    gates_full = route_gates.astype(jnp.float32)
    combine = lax.optimization_barrier(jnp.sum(jnp.where(routes[:, :, None] == labels[None, None, :], gates_full[:, :, None], jnp.float32(0.0)), axis=1))
    bound = partial(layer, deal_order=deal_order, inverse=inverse, lengths=lengths, combine=combine)
    output, pull = jax.vjp(bound, tokens.astype(jnp.float32), gain_first, gain_second, gain_query, gain_key, weight_qkv, weight_out, weight_gate, weight_up, weight_down)
    grads = pull(cotangent.astype(jnp.float32))
    return (output.astype(jnp.bfloat16), grads[0].astype(jnp.bfloat16), grads[1], grads[2], grads[3], grads[4], grads[5], grads[6], grads[7], grads[8], grads[9])
```

```python
from functools import partial

import jax
import jax.numpy as jnp
import numpy as np
from jax import lax
from jax.experimental import pallas as pl
from jax.experimental.pallas import tpu as pltpu
from jax.sharding import PartitionSpec as P

D = 1024
HEAD = 64
EXPERTS = 32
FF = 512
TOP = 8
TOK = 128
GROUP = 2048
PLANE = 1024
EPS_WIDE = 1e-05
EPS_HEAD = 1e-06
THETA = 10000.0
LOG2E = 1.4426950408889634
LN2 = 0.6931471805599453
QSCALE = LOG2E * HEAD**-0.5
APART = -256.0
BF = jnp.bfloat16
F32 = jnp.float32
NT = (((1,), (1,)), ((), ()))
TN = (((0,), (0,)), ((), ()))
HIGH = lax.Precision.HIGHEST


def params(mib=48):
    return pltpu.CompilerParams(vmem_limit_bytes=mib * 2**20)


def dot(a, b, dims=None):
    if dims is None:
        dims = (((1,), (0,)), ((), ()))
    return lax.dot_general(a, b, dims, preferred_element_type=F32)


def sds(shape, kind):
    return jax.ShapeDtypeStruct(shape, kind)


def whole(*shape):
    return pl.BlockSpec(shape, lambda *_: (0,) * len(shape))


def together(*values):
    return lax.optimization_barrier(values)


AHEAD = (1, 3, 2)


def step_pair(v, axis):
    if axis == "row":
        route = [(i, i ^ 1) for i in range(8)]
    else:
        route = [(i, i ^ 2) for i in range(16)]
    return lax.ppermute(v, axis, route)


def step_ring(v, axis, d):
    if axis == "row":
        route = [(i, (i + 2 * d) % 8) for i in range(8)]
    else:
        route = [(i, (i + 4 * d) % 16) for i in range(16)]
    return lax.ppermute(v, axis, route)


def step_core(v):
    return lax.ppermute(v, "col", [(i, i ^ 1) for i in range(16)])


def place(axis):
    i = lax.axis_index(axis)
    if axis == "col":
        i = i // 2
    return i // 2, i % 2


def gather_first(v, axis):
    h = v.shape[0] // 2
    va, vb = v[:h], v[h:]
    ax = step_pair(va, axis)
    by = [step_ring(vb, axis, d) for d in AHEAD]
    ax, *by = together(ax, *by)
    pa = jnp.stack([ax, va])
    pb = jnp.stack(by + [vb])
    return pa, pb


def gather_second(pa, pb, axis):
    bx = step_pair(pb, axis)
    ay = [step_ring(pa, axis, d) for d in AHEAD]
    return ay + [pa], [bx, pb]


def gather_plain(v, axis):
    pair = jnp.stack([step_pair(v, axis), v])
    return [step_ring(pair, axis, d) for d in AHEAD] + [pair]


def scatter_pieces(send_a, keep_a, send_b, axis):
    ra = step_pair(send_a, axis)
    rb = [step_ring(send_b[i], axis, d) for i, d in enumerate(AHEAD)]
    ra, *rb = together(ra, *rb)
    kind = send_a.dtype
    qa = [(keep_a[i].astype(F32) + ra[i].astype(F32)).astype(kind) for i in range(4)]

    def total(i):
        t = send_b[3][i].astype(F32)
        for r in rb:
            t = t + r[i].astype(F32)
        return t.astype(kind)

    qb = [total(0), total(1)]
    sa = [step_ring(qa[i], axis, d) for i, d in enumerate(AHEAD)]
    sb = step_pair(qb[0], axis)
    return sa + [qa[3]], [sb, qb[1]]


def added(terms):
    t = terms[0].astype(F32)
    for r in terms[1:]:
        t = t + r.astype(F32)
    return t


def sum_all(v):
    for k in (0, 1, 2, 3):
        v = v + lax.ppermute(v, "col", [(i, i ^ (1 << k)) for i in range(16)])
    for k in (0, 1, 2):
        v = v + lax.ppermute(v, "row", [(i, i ^ (1 << k)) for i in range(8)])
    return v


def head_sums():
    i = np.arange(256) // HEAD
    return jnp.asarray((i[:, None] == i[None, :]) / HEAD, BF)


def spread():
    s = np.zeros((256, 512), np.float32)
    for h in range(4):
        for i in range(64):
            s[h * 64 + i, h * 128 + i] = 1.0
    return jnp.asarray(s, BF)


def exact_sums(v, sums):
    hi = v.astype(BF)
    lo = (v - hi.astype(F32)).astype(BF)
    return dot(hi, sums) + dot(lo, sums)


def half_turn(v, lane):
    back = jnp.concatenate([pltpu.roll(v[:, :128], 96, 1), pltpu.roll(v[:, 128:], 96, 1)], 1)
    ahead = jnp.concatenate([pltpu.roll(v[:, :128], 32, 1), pltpu.roll(v[:, 128:], 32, 1)], 1)
    return jnp.where(lane % 64 < 32, -back, ahead)


def wide_tables(c, s, lane):
    c = jnp.where(lane < 192, jnp.concatenate([c, c], 1), 1.0)
    s = jnp.where(lane < 192, jnp.concatenate([s, s], 1), 0.0)
    return c, s


def heads_kernel(x_ref, w_ref, g_ref, c_ref, s_ref, seg_ref, bd_ref, sp_ref,
                 q0_ref, q1_ref, k_ref, v_ref, raw_ref, f_ref):
    x = x_ref[...]
    xf = x.astype(F32)
    f = lax.rsqrt(jnp.mean(xf * xf, axis=1, keepdims=True) + EPS_WIDE)
    raw = dot(x, w_ref[...]) * f
    raw_ref[...] = raw
    f_ref[...] = f
    rows = raw.shape[0]
    lane = lax.broadcasted_iota(jnp.int32, (rows, 256), 1)
    fac = jnp.where(lane < 192, lax.rsqrt(exact_sums(raw * raw, bd_ref[...]) + EPS_HEAD), 1.0)
    h = raw * fac * g_ref[...]
    c, s = wide_tables(c_ref[...], s_ref[...], lane)
    t = h * c + half_turn(h, lane) * s
    t = jnp.where(lane < 128, t * QSCALE, t).astype(BF)
    wide = dot(t, sp_ref[...])
    l1 = lax.broadcasted_iota(jnp.int32, (rows, 128), 1)
    seg = seg_ref[...]
    inseg = (l1 >= 64) & (l1 < 68)
    same = (l1 - 64) == seg
    aug_q = jnp.where(inseg & jnp.logical_not(same), APART, 0.0)
    aug_k = jnp.where((inseg & same) | ((l1 >= 68) & (l1 < 71)), 1.0, 0.0)
    aug_v = jnp.where((l1 >= 64) & (l1 < 67), 1.0, 0.0)
    q0_ref[...] = (wide[:, 0:128] + aug_q).astype(BF)
    q1_ref[...] = (wide[:, 128:256] + aug_q).astype(BF)
    k_ref[...] = (wide[:, 256:384] + aug_k).astype(BF)
    v_ref[...] = (wide[:, 384:512] + aug_v).astype(BF)


def project_heads(x, w, gains, cos, sin, seg):
    t = 512
    rows = lambda m: pl.BlockSpec((t, m), lambda i: (i, 0))
    return pl.pallas_call(
        heads_kernel,
        grid=(GROUP // t,),
        in_specs=[rows(D), whole(D, 256), whole(1, 256), rows(128), rows(128), rows(1),
                  whole(256, 256), whole(256, 512)],
        out_specs=[rows(128)] * 4 + [rows(256), rows(1)],
        out_shape=[sds((GROUP, 128), BF)] * 4 + [sds((GROUP, 256), F32), sds((GROUP, 1), F32)],
        compiler_params=params(),
        name="project_heads",
    )(x, w, gains, cos, sin, seg, head_sums(), spread())


CHUNK = 512


def attend_kernel(s_ref, q0_ref, q1_ref, k_ref, v_ref, o_ref, l_ref):
    q = jnp.concatenate([q0_ref[...], q1_ref[...]], 0)
    acc = jnp.zeros((256, 128), F32)
    for j in range(GROUP // CHUNK):
        rows = pl.ds(j * CHUNK, CHUNK)
        s = dot(q, k_ref[rows, :], NT)
        p = jnp.exp2(s).astype(BF)
        acc = acc + dot(p, v_ref[rows, :])
    total = acc[:, 64:65]
    o = acc / total
    l_ref[0] = jnp.log2(total)
    lane = lax.broadcasted_iota(jnp.int32, (128, 128), 1)
    o_ref[0] = jnp.where(lane < 64, o[:128], pltpu.roll(o[128:], 64, 1)).astype(BF)


MINE = pl.BlockSpec((128, 128), lambda j, s: (2 * j + s[0], 0))


def block3(n, m):
    return pl.BlockSpec((1, n, m), lambda j, s: (j, 0, 0))


def attend(marks, q0, q1, k, v):
    return pl.pallas_call(
        attend_kernel,
        grid_spec=pltpu.PrefetchScalarGridSpec(
            num_scalar_prefetch=1,
            grid=(8,),
            in_specs=[MINE, MINE, whole(GROUP, 128), whole(GROUP, 128)],
            out_specs=[block3(128, 128), block3(256, 1)],
        ),
        out_shape=[sds((8, 128, 128), BF), sds((8, 256, 1), F32)],
        compiler_params=params(),
        name="attend",
    )(marks, q0, q1, k, v)


def three(v):
    hi = v.astype(BF).astype(F32)
    mid = (v - hi).astype(BF).astype(F32)
    return hi, mid, v - hi - mid


def attend_back_kernel(s_ref, q0_ref, q1_ref, k_ref, v_ref, o_ref, l_ref, g_ref,
                       dq_ref, own_ref, other_ref, dk_ref, dv_ref):
    @pl.when(pl.program_id(0) == 0)
    def _():
        dk_ref[...] = jnp.zeros_like(dk_ref)
        dv_ref[...] = jnp.zeros_like(dv_ref)

    lane = lax.broadcasted_iota(jnp.int32, (256, 128), 1)
    q = jnp.concatenate([q0_ref[...], q1_ref[...]], 0)
    h0, h1, h2 = three(l_ref[0])
    ql = jnp.where(lane == 68, -h0, jnp.where(lane == 69, -h1, jnp.where(lane == 70, -h2, q.astype(F32))))
    ql = ql.astype(BF)
    g = g_ref[0].astype(F32)
    o = o_ref[0].astype(F32)
    g = jnp.concatenate([g, pltpu.roll(g, 64, 1)], 0)
    o = jnp.concatenate([o, pltpu.roll(o, 64, 1)], 0)
    g = jnp.where(lane < 64, g, 0.0)
    centre = jnp.sum(g * o, axis=1, keepdims=True)
    c0, c1, c2 = three(centre)
    gl = jnp.where(lane == 64, -c0, jnp.where(lane == 65, -c1, jnp.where(lane == 66, -c2, g)))
    gl = gl.astype(BF)
    gb = g.astype(BF)
    dq = jnp.zeros((256, 128), F32)
    for j in range(GROUP // CHUNK):
        rows = pl.ds(j * CHUNK, CHUNK)
        k = k_ref[rows, :]
        st = dot(k, ql, NT)
        pt = jnp.exp2(st)
        gt = dot(v_ref[rows, :], gl, NT)
        ds = (pt * gt).astype(BF)
        dv_ref[rows, :] += dot(pt.astype(BF), gb)
        dk_ref[rows, :] += dot(ds, q)
        dq = dq + dot(ds, k, TN)
    dq_ref[0] = dq

    @pl.when(pl.program_id(0) == 7)
    def _():
        core = s_ref[0]
        low = lax.broadcasted_iota(jnp.int32, (128, 128), 1) < 64

        def block(j, c):
            rows = pl.ds(pl.multiple_of((2 * j + c) * 128, 128), 128)
            return jnp.where(low, dk_ref[rows, :] * LN2, pltpu.roll(dv_ref[rows, :], 64, 1))

        for j in range(8):
            own_ref[j] = block(j, core)
            other_ref[j] = block(j, 1 - core).astype(BF)


def attend_back(marks, q0, q1, k, v, o, l, g):
    return pl.pallas_call(
        attend_back_kernel,
        grid_spec=pltpu.PrefetchScalarGridSpec(
            num_scalar_prefetch=1,
            grid=(8,),
            in_specs=[MINE, MINE, whole(GROUP, 128), whole(GROUP, 128), block3(128, 128), block3(256, 1),
                      block3(128, 128)],
            out_specs=[block3(256, 128), whole(8, 128, 128), whole(8, 128, 128)],
            scratch_shapes=[pltpu.VMEM((GROUP, 128), F32)] * 2,
        ),
        out_shape=[sds((8, 256, 128), F32), sds((8, 128, 128), F32), sds((8, 128, 128), BF)],
        compiler_params=params(),
        name="attend_back",
    )(marks, q0, q1, k, v, o, l, g)


def heads_back_kernel(s_ref, dq_ref, own_ref, got_ref, raw_ref, f_ref, g_ref, c_ref, sin_ref, bd_ref,
                      out_ref, scaled_ref, gain_ref):
    @pl.when(pl.program_id(0) == 0)
    def _():
        gain_ref[...] = jnp.zeros_like(gain_ref)

    lane1 = lax.broadcasted_iota(jnp.int32, (128, 128), 1)
    dq = dq_ref[0] * HEAD**-0.5
    dq = jnp.where(lane1 < 64, dq[:128], pltpu.roll(dq[128:], 64, 1))
    d = jnp.concatenate([dq, own_ref[0] + got_ref[0].astype(F32)], 1)
    raw = raw_ref[...]
    lane = lax.broadcasted_iota(jnp.int32, (128, 256), 1)
    bd = bd_ref[...]
    fac = jnp.where(lane < 192, lax.rsqrt(exact_sums(raw * raw, bd) + EPS_HEAD), 1.0)
    hat = raw * fac
    c, s = wide_tables(c_ref[...], sin_ref[...], lane)
    dh = d * c - half_turn(d * s, lane)
    gain_ref[...] += jnp.sum(dh * hat, axis=0, keepdims=True)
    dn = dh * g_ref[...]
    back = fac * (dn - hat * exact_sums(dn * hat, bd))
    res = jnp.where(lane < 192, back, d)
    out_ref[0] = res.astype(BF)
    scaled_ref[...] = (res * f_ref[...]).astype(BF)


def heads_back(marks, dq, own, got, raw, f, gains, cos, sin):
    mine = lambda m: pl.BlockSpec((128, m), lambda j, s: (2 * j + s[0], 0))
    return pl.pallas_call(
        heads_back_kernel,
        grid_spec=pltpu.PrefetchScalarGridSpec(
            num_scalar_prefetch=1,
            grid=(8,),
            in_specs=[block3(256, 128), block3(128, 128), block3(128, 128), mine(256), mine(1), whole(1, 256),
                      mine(128), mine(128), whole(256, 256)],
            out_specs=[block3(128, 256), pl.BlockSpec((128, 256), lambda j, s: (j, 0)), whole(1, 256)],
        ),
        out_shape=[sds((8, 128, 256), BF), sds((PLANE, 256), BF), sds((1, 256), F32)],
        compiler_params=params(),
        name="heads_back",
    )(marks, dq, own, got, raw, f, gains, cos, sin, head_sums())


def norm_factor(v):
    return lax.rsqrt(jnp.mean(v * v, axis=1, keepdims=True) + EPS_WIDE)


def after_attention_kernel(s_ref, j_ref, *refs):
    own, sib = refs[0:4], refs[4]
    x_ref, g_ref, hidden_ref, middle_ref, w_ref = refs[5:]
    core, a, b = s_ref[0], s_ref[1], s_ref[2]
    for i, d in enumerate((1, 3, 2, 0)):
        for r in range(2):
            chip = ((a - d) & 3) * 2 + (b ^ (1 - r))
            at = chip * 128 + core * 64
            w_ref[pl.ds(pl.multiple_of(at, 64), 64), :] = own[i][r]
            at = chip * 128 + (1 - core) * 64
            w_ref[pl.ds(pl.multiple_of(at, 64), 64), :] = sib[i, r]
    hidden = x_ref[...].astype(F32)
    for j in range(8):
        hidden = hidden + dot(j_ref[j], w_ref[j * 128 : j * 128 + 128, :])
    hidden_ref[...] = hidden
    middle_ref[...] = (hidden * norm_factor(hidden) * g_ref[...]).astype(BF)


def after_attention(marks, joined, own, sib, x, gain):
    return pl.pallas_call(
        after_attention_kernel,
        grid_spec=pltpu.PrefetchScalarGridSpec(
            num_scalar_prefetch=1,
            grid=(1,),
            in_specs=[whole(8, 128, 128)] + [whole(2, 64, D)] * 4 + [whole(4, 2, 64, D), whole(128, D), whole(1, D)],
            out_specs=[whole(128, D), whole(128, D), whole(D, D)],
        ),
        out_shape=[sds((128, D), F32), sds((128, D), BF), sds((D, D), BF)],
        compiler_params=params(),
        name="after_attention",
    )(marks, joined, *own, sib, x, gain)


def second_back_kernel(a0, a1, a2, a3, b0, b1, hidden_ref, cot_ref, g_ref, w_ref,
                       grad_ref, low_ref, joined_ref, gain_ref):
    fa = a0[...].astype(F32) + a1[...].astype(F32) + a2[...].astype(F32) + a3[...].astype(F32)
    fb = b0[...].astype(F32) + b1[...].astype(F32)
    mg = jnp.concatenate([fa, fb], 0)
    hidden = hidden_ref[...]
    f = norm_factor(hidden)
    hat = hidden * f
    gain_ref[...] = jnp.sum(mg * hat, axis=0, keepdims=True)
    dn = mg * g_ref[...]
    grad = cot_ref[...].astype(F32) + f * (dn - hat * jnp.mean(dn * hat, axis=1, keepdims=True))
    grad_ref[...] = grad
    low = grad.astype(BF)
    low_ref[...] = low
    joined = dot(low, w_ref[...], NT).astype(BF)
    for j in range(8):
        joined_ref[j] = joined[:, j * 128 : j * 128 + 128]


def second_back(terms_a, terms_b, hidden, cot, gain, w):
    return pl.pallas_call(
        second_back_kernel,
        out_shape=[sds((128, D), F32), sds((128, D), BF), sds((8, 128, 128), BF), sds((1, D), F32)],
        compiler_params=params(),
        name="second_back",
    )(*terms_a, *terms_b, hidden, cot, gain, w)


def first_back_kernel(raw_ref, w_ref, x_ref, g_ref, grad_ref, out_ref):
    ng = dot(raw_ref[0], w_ref[0:256, :])
    for j in range(1, 8):
        ng = ng + dot(raw_ref[j], w_ref[j * 256 : j * 256 + 256, :])
    x = x_ref[...].astype(F32)
    f = norm_factor(x)
    hat = x * f
    dn = ng * g_ref[...]
    out_ref[...] = (grad_ref[...] + f * (dn - hat * jnp.mean(dn * hat, axis=1, keepdims=True))).astype(BF)


def first_back(raw, w, x, gain, grad):
    return pl.pallas_call(
        first_back_kernel,
        out_shape=sds((128, D), BF),
        compiler_params=params(),
        name="first_back",
    )(raw, w, x, gain, grad)


def place_experts_kernel(s_ref, *refs):
    ya, xb, out = refs[0:4], refs[4:6], refs[6]
    a, b = s_ref[3], s_ref[4]
    for i, d in enumerate((1, 3, 2, 0)):
        for r in range(2):
            block = ((a - d) & 3) * 2 + (b ^ (1 - r))
            at = block * 128
            out[pl.ds(pl.multiple_of(at, 64), 64), :] = ya[i][r]
            at = block * 128 + 64
            out[pl.ds(pl.multiple_of(at, 64), 64), :] = xb[r][i]


def place_experts(marks, ya, xb):
    m = ya[0].shape[2]
    return pl.pallas_call(
        place_experts_kernel,
        grid_spec=pltpu.PrefetchScalarGridSpec(
            num_scalar_prefetch=1,
            grid=(1,),
            in_specs=[whole(2, 64, m)] * 4 + [whole(4, 64, m)] * 2,
            out_specs=whole(D, m),
        ),
        out_shape=sds((D, m), BF),
        compiler_params=params(),
        name="place_experts",
    )(marks, *ya, *xb)


def experts_kernel(s_ref, mid_ref, up_ref, g_ref, w_ref, entry_ref, gg_ref, ug_ref, in_ref):
    mid = mid_ref[...].reshape(256, D)
    up = up_ref[...].reshape(256, D)
    gates = g_ref[...].reshape(256, 2)
    entry = None
    for e in range(2):
        cg = slice(e * FF, e * FF + FF)
        cu = slice(1024 + e * FF, 1024 + e * FF + FF)
        cd = slice(2048 + e * FF, 2048 + e * FF + FF)
        gp = dot(mid, w_ref[:, cg])
        u = dot(mid, w_ref[:, cu])
        g = gates[:, e : e + 1]
        ig = dot(up, w_ref[:, cd]) * g
        sig = 0.5 * jnp.tanh(0.5 * gp) + 0.5
        act = gp * sig
        inner = (g * act * u).astype(BF)
        gg = (ig * u * (sig + act * (1.0 - sig))).astype(BF)
        ug = (ig * act).astype(BF)
        part = dot(gg, w_ref[:, cg], NT) + dot(ug, w_ref[:, cu], NT)
        entry = part if entry is None else entry + part
        for ref, v in ((in_ref, inner), (gg_ref, gg), (ug_ref, ug)):
            ref[0, :, :, e * FF : e * FF + FF] = v.reshape(2, 128, FF)
    entry = entry.astype(BF)
    own = s_ref[2]
    entry_ref[0, own ^ 1 ^ 0 ^ 0] = entry[:128]
    entry_ref[0, own] = entry[128:]


def run_experts(marks, which, mid, up, gates, w):
    def group(m):
        return pl.BlockSpec((1, 2, 1, 128, m), lambda i, s: (s[8 + i], 0, s[which], 0, 0))

    hid = pl.BlockSpec((1, 2, 128, 2 * FF), lambda i, s: (s[8 + i], 0, 0, 0))
    entry = pl.BlockSpec((1, 2, 128, D), lambda i, s: (i, 0, 0, 0))
    return pl.pallas_call(
        experts_kernel,
        grid_spec=pltpu.PrefetchScalarGridSpec(
            num_scalar_prefetch=1,
            grid=(4,),
            in_specs=[group(D), group(D), group(2), whole(D, 6 * FF)],
            out_specs=[entry, hid, hid, hid],
        ),
        out_shape=[sds((4, 2, 128, D), BF)] * 4,
        compiler_params=params(),
        name="run_experts",
    )(marks, mid, up, gates, w)


def results_kernel(s_ref, own_ref, other_ref, w_ref, out_ref):
    core = s_ref[0]
    w = w_ref[...]
    out_ref[0, :, core] = dot(own_ref[...].reshape(256, 2 * FF), w, NT).astype(BF).reshape(2, 128, D)
    out_ref[0, :, 1 - core] = dot(other_ref[...].reshape(256, 2 * FF), w, NT).astype(BF).reshape(2, 128, D)


def results(marks, own, other, w):
    hid = pl.BlockSpec((1, 2, 128, 2 * FF), lambda i, s: (i, 0, 0, 0))
    return pl.pallas_call(
        results_kernel,
        grid_spec=pltpu.PrefetchScalarGridSpec(
            num_scalar_prefetch=1,
            grid=(4,),
            in_specs=[hid, hid, pl.BlockSpec((D, 2 * FF), lambda i, s: (0, 2))],
            out_specs=pl.BlockSpec((1, 2, 2, 128, D), lambda i, s: (i, 0, 0, 0, 0)),
        ),
        out_shape=sds((4, 2, 2, 128, D), BF),
        compiler_params=params(),
        name="results",
    )(marks, own, other, w)


def weights_kernel(s_ref, m0, m1, u0, u1, gg0, gg1, ug0, ug1, in0, in1,
                   send_ref, keep_ref, b1_ref, b3_ref, b2_ref, b0_ref):
    i = pl.program_id(0)
    b = s_ref[4]
    sides = [m0[...].reshape(PLANE, 256), m1[...].reshape(PLANE, 256),
             u0[...].reshape(PLANE, 256), u1[...].reshape(PLANE, 256)]
    sides = [v.T for v in sides]
    for n, (l0, l1, r0, r1) in enumerate((
        (sides[0], sides[1], gg0, gg1),
        (sides[0], sides[1], ug0, ug1),
        (sides[2], sides[3], in0, in1),
    )):
        cols = slice(n * 1024, n * 1024 + 1024)
        o = dot(l0, r0[...].reshape(PLANE, 1024)) + dot(l1, r1[...].reshape(PLANE, 1024))
        o = o.astype(BF)
        other = jnp.where(b == 0, o[128:], o[:128])
        own = jnp.where(b == 0, o[:128], o[128:])
        send_ref[0, :, cols] = other[:64]
        keep_ref[0, :, cols] = own[:64]
        for k, ref in enumerate((b1_ref, b3_ref, b2_ref, b0_ref)):
            @pl.when(i == k)
            def _():
                ref[0, :, cols] = other[64:]
                ref[1, :, cols] = own[64:]


def weight_grads(marks, mid, up, gg, ug, inner):
    def side(which):
        return pl.BlockSpec((4, 2, 1, 128, 256), lambda i, s: (0, 0, s[which], 0, s[12 + i]))

    hid = whole(4, 2, 128, 2 * FF)
    part = pl.BlockSpec((1, 64, 6 * FF), lambda i, s: (i, 0, 0))
    return pl.pallas_call(
        weights_kernel,
        grid_spec=pltpu.PrefetchScalarGridSpec(
            num_scalar_prefetch=1,
            grid=(4,),
            in_specs=[side(0), side(5), side(0), side(5)] + [hid] * 6,
            out_specs=[part, part] + [whole(2, 64, 6 * FF)] * 4,
        ),
        out_shape=[sds((4, 64, 6 * FF), BF)] * 2 + [sds((2, 64, 6 * FF), BF)] * 4,
        compiler_params=params(58),
        name="weight_grads",
    )(marks, mid, mid, up, up, *gg, *ug, *inner)


def qkv_grads_kernel(s_ref, x_ref, r_ref, w_ref, g_ref, own_ref, other_ref, first_ref):
    core = s_ref[0]
    o = dot(x_ref[...].reshape(PLANE, 256), r_ref[...], TN)
    first_ref[...] = jnp.sum(o * w_ref[...].astype(F32), axis=1, keepdims=True)
    o = o * g_ref[...]
    own_ref[...] = jnp.where(core == 0, o[:, :128], o[:, 128:])
    other_ref[...] = jnp.where(core == 0, o[:, 128:], o[:, :128]).astype(BF)


def qkv_grads(marks, x, r, w, gain):
    rows = lambda m: pl.BlockSpec((256, m), lambda i, s: (i, 0))
    return pl.pallas_call(
        qkv_grads_kernel,
        grid_spec=pltpu.PrefetchScalarGridSpec(
            num_scalar_prefetch=1,
            grid=(4,),
            in_specs=[pl.BlockSpec((4, 2, 1, 128, 256), lambda i, s: (0, 0, s[0], 0, i)), whole(PLANE, 256),
                      rows(256), rows(1)],
            out_specs=[rows(128), rows(128), rows(1)],
        ),
        out_shape=[sds((D, 128), F32), sds((D, 128), BF), sds((D, 1), F32)],
        compiler_params=params(),
        name="qkv_grads",
    )(marks, x, r, w, gain)


def out_grads_kernel(s_ref, h0, h1, h2, h3, j_ref, own_ref, other_ref):
    core, a, b = s_ref[0], s_ref[1], s_ref[2]
    acc = jnp.zeros((D, 128), F32)
    for ref, d in zip((h0, h1, h2, h3), (1, 3, 2, 0)):
        at = ((a - d) & 3) * 2
        both = jnp.concatenate([j_ref[at + (b ^ 1)], j_ref[at + b]], 0)
        acc = acc + dot(ref[...].reshape(256, D), both, TN)
    other = pltpu.roll(acc, 64, 1)
    own_ref[...] = jnp.where(core == 0, acc, other)[:, :64]
    other_ref[...] = jnp.where(core == 0, other, acc)[:, :64].astype(BF)


def out_grads(marks, pieces, joined):
    return pl.pallas_call(
        out_grads_kernel,
        grid_spec=pltpu.PrefetchScalarGridSpec(
            num_scalar_prefetch=1,
            grid=(1,),
            in_specs=[whole(2, 128, D)] * 4 + [whole(8, 128, 128)],
            out_specs=[whole(D, 64), whole(D, 64)],
        ),
        out_shape=[sds((D, 64), F32), sds((D, 64), BF)],
        compiler_params=params(),
        name="out_grads",
    )(marks, *pieces, joined)


def body(tokens, cotangent, deal_order, lengths, routes, route_gates, gain_first, gain_second, gain_query, gain_key,
         weight_qkv, weight_out, weight_gate, weight_up, weight_down):
    col = lax.axis_index("col")
    core = col % 2
    a, b = place("col")
    ra, rb = place("row")
    order = [(a + d) % 4 for d in (1, 3, 2, 0)]
    row_order = [(ra + d) % 4 for d in (1, 3, 2, 0)]
    marks = jnp.stack([core, a, b, ra, rb, 1 - core, core, core] + order + row_order).astype(jnp.int32)
    planes = [[i for i in range(16) if i % 2 == k] for k in range(2)]
    swap_all = partial(lax.all_to_all, axis_name="col", split_axis=0, concat_axis=0, tiled=True,
                       axis_index_groups=planes)

    x_all = lax.all_gather(tokens, "col", axis=0, tiled=True)

    small = jnp.concatenate([weight_qkv, weight_out], 1).astype(BF)
    wide = jnp.concatenate([w.reshape(128, 2 * FF) for w in (weight_gate, weight_up, weight_down)], 1).astype(BF)
    pieces = gather_plain(small, "row")
    wide_a, wide_b = gather_first(wide, "row")
    small = jnp.zeros((4, 2, 128, 192), BF)
    for d, piece in zip((1, 3, 2, 0), pieces):
        small = lax.dynamic_update_slice(small, jnp.where(rb == 0, piece[::-1], piece)[None], ((ra - d) % 4, 0, 0, 0))
    small = small.reshape(D, 192)
    w_own = small[:, :128]
    w_pair = step_core(w_own)
    w_chip = jnp.where(core == 0, jnp.concatenate([w_own, w_pair], 1), jnp.concatenate([w_pair, w_own], 1))
    own_t = small.T
    out_own = gather_plain(own_t[128:], "col")
    out_sib = step_core(jnp.stack(out_own))
    x_all, cotangent_late, wide_a, wide_b, out_sib_late = together(x_all, cotangent, wide_a, wide_b, out_sib)
    wide_ya, wide_xb = gather_second(wide_a, wide_b, "row")

    deal_row = deal_order[0]
    slots = jnp.arange(GROUP, dtype=jnp.int32)
    inverse = jnp.zeros((GROUP,), jnp.int32).at[deal_row].set(slots)
    finish = jnp.cumsum(lengths[0])
    starts = finish - lengths[0]
    segment = jnp.sum((inverse[:, None] >= finish[None, :]).astype(jnp.int32), axis=1)
    labels = jnp.arange(4, dtype=jnp.int32)
    anchor = jnp.sum(jnp.where(segment[:, None] == labels[None, :], starts[None, :], 0), axis=1)
    offset = (inverse - anchor).astype(F32)
    frequency = THETA ** (-(jnp.arange(128) % 32).astype(F32) * 2.0 / HEAD)
    angles = offset[:, None] * frequency[None, :]
    cos, sin = jnp.cos(angles), jnp.sin(angles)

    r16 = routes.astype(BF)
    g_hi, g_mid, g_lo = three(route_gates)
    extra = jnp.concatenate([r16, g_hi.astype(BF), g_mid.astype(BF), g_lo.astype(BF)], 1).reshape(4, 1024)
    extra = jnp.concatenate([extra, jnp.zeros((12, 1024), BF)], 0)
    cot_all = lax.all_gather(jnp.concatenate([cotangent_late, extra], 0), "col", axis=0, tiled=False)
    cot_all = cot_all.reshape(4, 2, 2, 144, D)
    info = cot_all[:, :, :, 128:132].reshape(GROUP, 32).astype(F32)
    names = info[:, :8]
    values = info[:, 8:16] + info[:, 16:24] + info[:, 24:32]
    mine = (col * 2 + jnp.arange(2)).astype(F32)
    gates = jnp.sum(jnp.where(names[:, None, :] == mine[None, :, None], values[:, None, :], 0.0), axis=2)
    gates = gates[inverse].reshape(4, 2, 2, 128, 2)

    gains = jnp.concatenate([gain_query, gain_query, gain_key, jnp.ones((HEAD,), F32)])[None, :]
    w_scaled = (gain_first[:, None] * w_chip.astype(F32)).astype(BF)
    q0, q1, k, v, raw, f1_all = project_heads(x_all, w_scaled, gains, cos, sin, segment[:, None])
    joined, logs = attend(marks, q0, q1, k, v)
    hidden, middle, wout_t = after_attention(marks, swap_all(joined), out_own, out_sib, tokens, gain_second[None])
    mid_all = lax.all_gather(middle, "col", axis=0, tiled=True).reshape(4, 2, 2, 128, D)
    own_t, middle_late = together(own_t, mid_all)
    wqkv_t = lax.all_gather(own_t[:128], "col", axis=0, tiled=True)

    w_all = place_experts(marks, wide_ya, wide_xb)
    e_other, gg1, ug1, in1 = run_experts(marks, 5, mid_all, cot_all, gates, w_all)
    e_got = step_core(e_other)
    e_own, gg0, ug0, in0 = run_experts(marks, 0, mid_all, cot_all, gates, w_all)

    def entry(i, r, h):
        rows = slice(h * 64, h * 64 + 64)
        return (e_own[i, r, rows].astype(F32) + e_got[i, r, rows].astype(F32)).astype(BF)

    def entries(h, r, items):
        rows = slice(h * 64, h * 64 + 64)
        return (e_own[items, r, rows].astype(F32) + e_got[items, r, rows].astype(F32)).astype(BF)

    terms_a, terms_b = scatter_pieces(
        entries(0, 0, slice(0, 4)), entries(0, 1, slice(0, 4)),
        [entries(1, slice(0, 2), i) for i in range(4)], "col")
    out_parts = results(marks, in0, in1, w_all).reshape(GROUP, D)
    out_sum = lax.psum_scatter(out_parts, "col", scatter_dimension=0, tiled=True).astype(F32)
    block_out = (hidden + out_sum).astype(BF)
    send_a, keep_a, *send_b = weight_grads(marks, mid_all, cot_all, (gg0, gg1), (ug0, ug1), (in0, in1))
    wide_a, wide_b = scatter_pieces(send_a, keep_a, send_b, "row")
    grads_w = jnp.concatenate([added(wide_a), added(wide_b)], 0)

    hidden_grad, hidden_low, joined_grad, second = second_back(
        terms_a, terms_b, hidden, cotangent, gain_second[None], wout_t)
    joined_grad = swap_all(joined_grad)
    hidden_pieces = gather_plain(hidden_low, "col")
    dq, dkv_own, dkv_other = attend_back(marks, q0, q1, k, v, joined, logs, joined_grad)
    dkv_got = step_core(dkv_other)
    raw_grad, raw_scaled, gain_heads = heads_back(marks, dq, dkv_own, dkv_got, raw, f1_all, gains, cos, sin)
    raw_got = swap_all(raw_grad)
    own_q, other_q, first = qkv_grads(marks, x_all.reshape(4, 2, 2, 128, D), raw_scaled, w_chip, gain_first[:, None])
    own_o, other_o = out_grads(marks, hidden_pieces, joined)
    got = step_core(jnp.concatenate([other_q, other_o], 1))
    own = jnp.concatenate([own_q, own_o], 1) + got.astype(F32)
    own = own.astype(BF).reshape(4, 2, 128, 192)
    other_b = lax.dynamic_index_in_dim(own, 1 - rb, 1, keepdims=False)
    own_b = lax.dynamic_index_in_dim(own, rb, 1, keepdims=False)
    own = (own_b.astype(F32) + step_pair(other_b, "row").astype(F32)).astype(BF)
    terms = [step_ring(lax.dynamic_index_in_dim(own, (ra + d) % 4, 0, keepdims=False), "row", d) for d in AHEAD]
    own = added(terms + [lax.dynamic_index_in_dim(own, ra, 0, keepdims=False)])

    input_grad = first_back(raw_got, wqkv_t, tokens, gain_first[None], hidden_grad)

    heads = gain_heads[0]
    packed = jnp.concatenate([first[:, 0], second[0], heads[:64] + heads[64:128], heads[128:192]]).reshape(17, 128)
    packed = sum_all(packed).reshape(-1)
    shape = (128, 2, FF)
    return (
        block_out,
        input_grad,
        packed[:1024],
        packed[1024:2048],
        packed[2048:2112],
        packed[2112:],
        own[:, :128],
        own[:, 128:],
        grads_w[:, :1024].reshape(shape),
        grads_w[:, 1024:2048].reshape(shape),
        grads_w[:, 2048:].reshape(shape),
    )


def solution(mesh):
    both = P(("row", "col"), None)
    return jax.shard_map(
        body,
        mesh=mesh,
        in_specs=(both, both, P("row", None), P("row", None), both, both, P(), P(), P(), P(),
                  P("row", "col"), P("row", "col"), P("row", "col", None), P("row", "col", None),
                  P("row", "col", None)),
        out_specs=(both, both, P(), P(), P(), P(), P("row", "col"), P("row", "col"), P("row", "col", None),
                   P("row", "col", None), P("row", "col", None)),
        check_vma=False,
    )
```

```python
from functools import partial

import jax
import jax.numpy as jnp
import numpy as np
from jax import lax
from jax.experimental import pallas as pl
from jax.experimental.pallas import tpu as pltpu
from jax.sharding import PartitionSpec as P

D = 1024
HEAD = 64
EXPERTS = 32
FF = 512
TOP = 8
TOK = 128
GROUP = 2048
PLANE = 1024
EPS_WIDE = 1e-05
EPS_HEAD = 1e-06
THETA = 10000.0
LOG2E = 1.4426950408889634
LN2 = 0.6931471805599453
QSCALE = LOG2E * HEAD**-0.5
APART = -256.0
BF = jnp.bfloat16
F32 = jnp.float32
NT = (((1,), (1,)), ((), ()))
TN = (((0,), (0,)), ((), ()))
HIGH = lax.Precision.HIGHEST


def params(mib=56):
    return pltpu.CompilerParams(vmem_limit_bytes=mib * 2**20)


def cost(us, scale=0.02):
    us = us * scale
    return pl.CostEstimate(flops=int(us * 1e9), bytes_accessed=int(us * 1e6), transcendentals=0)


def dot(a, b, dims=None):
    if dims is None:
        dims = (((1,), (0,)), ((), ()))
    return lax.dot_general(a, b, dims, preferred_element_type=F32)


def sds(shape, kind):
    return jax.ShapeDtypeStruct(shape, kind)


def whole(*shape):
    return pl.BlockSpec(shape, lambda *_: (0,) * len(shape))


def together(*values):
    return lax.optimization_barrier(values)


AHEAD = (1, 3, 2)


def step_pair(v, axis):
    if axis == "row":
        route = [(i, i ^ 1) for i in range(8)]
    else:
        route = [(i, i ^ 2) for i in range(16)]
    return lax.ppermute(v, axis, route)


def step_ring(v, axis, d):
    if axis == "row":
        route = [(i, (i + 2 * d) % 8) for i in range(8)]
    else:
        route = [(i, (i + 4 * d) % 16) for i in range(16)]
    return lax.ppermute(v, axis, route)


def step_core(v):
    return lax.ppermute(v, "col", [(i, i ^ 1) for i in range(16)])


def place(axis):
    i = lax.axis_index(axis)
    if axis == "col":
        i = i // 2
    return i // 2, i % 2


def gather_rest(pair, v, axis):
    pair = jnp.stack([pair, v])
    return [step_ring(pair, axis, d) for d in AHEAD] + [pair]


def gather_plain(v, axis):
    return gather_rest(step_pair(v, axis), v, axis)


def added(terms):
    t = terms[0].astype(F32)
    for r in terms[1:]:
        t = t + r.astype(F32)
    return t


def head_sums():
    i = np.arange(256) // HEAD
    return jnp.asarray((i[:, None] == i[None, :]) / HEAD, BF)


def spread():
    s = np.zeros((256, 512), np.float32)
    for h in range(4):
        for i in range(64):
            s[h * 64 + i, h * 128 + i] = 1.0
    return jnp.asarray(s, BF)


def exact_sums(v, sums):
    hi = v.astype(BF)
    lo = (v - hi.astype(F32)).astype(BF)
    return dot(hi, sums) + dot(lo, sums)


def half_turn(v, lane):
    back = jnp.concatenate([pltpu.roll(v[:, :128], 96, 1), pltpu.roll(v[:, 128:], 96, 1)], 1)
    ahead = jnp.concatenate([pltpu.roll(v[:, :128], 32, 1), pltpu.roll(v[:, 128:], 32, 1)], 1)
    return jnp.where(lane % 64 < 32, -back, ahead)


def wide_tables(c, s, lane):
    c = jnp.where(lane < 192, jnp.concatenate([c, c], 1), 1.0)
    s = jnp.where(lane < 192, jnp.concatenate([s, s], 1), 0.0)
    return c, s


def heads_kernel(s_ref, x0, x1, x2, x3, w_ref, g_ref, c_ref, s_tab_ref, seg_ref, bd_ref, sp_ref,
                 q0_ref, q1_ref, kv_ref, raw_ref, f_ref):
    a, b = s_ref[1], s_ref[2]
    lane = lax.broadcasted_iota(jnp.int32, (256, 256), 1)
    l1 = lax.broadcasted_iota(jnp.int32, (256, 128), 1)
    inseg = (l1 >= 64) & (l1 < 68)
    aug_v = jnp.where((l1 >= 64) & (l1 < 67), 1.0, 0.0)
    for ref, d in zip((x0, x1, x2, x3), (1, 3, 2, 0)):
        at = ((a - d) & 3) * 2
        blocks = (at + (b ^ 1), at + b)

        def both(r):
            return jnp.concatenate([r[blocks[0]], r[blocks[1]]], 0)

        def put(r, v):
            r[blocks[0]] = v[:128]
            r[blocks[1]] = v[128:]

        x = ref[...].reshape(256, D)
        xf = x.astype(F32)
        f = lax.rsqrt(jnp.mean(xf * xf, axis=1, keepdims=True) + EPS_WIDE)
        raw = dot(x, w_ref[...]) * f
        put(raw_ref, raw)
        put(f_ref, f)
        fac = jnp.where(lane < 192, lax.rsqrt(exact_sums(raw * raw, bd_ref[...]) + EPS_HEAD), 1.0)
        h = raw * fac * g_ref[...]
        c, s = wide_tables(both(c_ref), both(s_tab_ref), lane)
        t = h * c + half_turn(h, lane) * s
        t = jnp.where(lane < 128, t * QSCALE, t).astype(BF)
        wide = dot(t, sp_ref[...])
        same = (l1 - 64) == both(seg_ref)
        aug_q = jnp.where(inseg & jnp.logical_not(same), APART, 0.0)
        aug_k = jnp.where((inseg & same) | ((l1 >= 68) & (l1 < 71)), 1.0, 0.0)
        put(q0_ref, (wide[:, 0:128] + aug_q).astype(BF))
        put(q1_ref, (wide[:, 128:256] + aug_q).astype(BF))
        put(kv_ref.at[0], (wide[:, 256:384] + aug_k).astype(BF))
        put(kv_ref.at[1], (wide[:, 384:512] + aug_v).astype(BF))


def project_heads(marks, pieces, w, gains, cos, sin, seg):
    return pl.pallas_call(
        heads_kernel,
        grid_spec=pltpu.PrefetchScalarGridSpec(
            num_scalar_prefetch=1,
            grid=(1,),
            in_specs=[whole(2, 128, D)] * 4 + [whole(D, 256), whole(1, 256), whole(8, 128, 128), whole(8, 128, 128),
                                               whole(8, 128, 1), whole(256, 256), whole(256, 512)],
            out_specs=[whole(8, 128, 128)] * 2 + [whole(2, 8, 128, 128), whole(8, 128, 256), whole(8, 128, 1)],
        ),
        out_shape=[sds((8, 128, 128), BF)] * 2 + [sds((2, 8, 128, 128), BF), sds((8, 128, 256), F32),
                                                  sds((8, 128, 1), F32)],
        compiler_params=params(56),
        cost_estimate=cost(7),
        name="project_heads",
    )(marks, *pieces, w, gains, cos, sin, seg, head_sums(), spread())


CHUNK = 512


def attend_kernel(q0_ref, q1_ref, own_ref, sib_ref, o_ref, l_ref):
    q = jnp.concatenate([q0_ref[0], q1_ref[0]], 0)
    acc = jnp.zeros((256, 128), F32)
    for ref in (own_ref, sib_ref):
        for j in range(PLANE // CHUNK):
            rows = pl.ds(j * CHUNK, CHUNK)
            s = dot(q, ref[0, rows, :], NT)
            p = jnp.exp2(s).astype(BF)
            acc = acc + dot(p, ref[1, rows, :])
    total = acc[:, 64:65]
    o = acc / total
    l_ref[0] = jnp.log2(total)
    lane = lax.broadcasted_iota(jnp.int32, (128, 128), 1)
    o_ref[0] = jnp.where(lane < 64, o[:128], pltpu.roll(o[128:], 64, 1)).astype(BF)


def block3(n, m):
    return pl.BlockSpec((1, n, m), lambda j, *_: (j, 0, 0))


def attend(q0, q1, own, sib):
    return pl.pallas_call(
        attend_kernel,
        grid=(8,),
        in_specs=[block3(128, 128), block3(128, 128), whole(2, PLANE, 128), whole(2, PLANE, 128)],
        out_specs=[block3(128, 128), block3(256, 1)],
        out_shape=[sds((8, 128, 128), BF), sds((8, 256, 1), F32)],
        compiler_params=params(56),
        cost_estimate=cost(10),
        name="attend",
    )(q0, q1, own.reshape(2, PLANE, 128), sib.reshape(2, PLANE, 128))


def three(v):
    hi = v.astype(BF).astype(F32)
    mid = (v - hi).astype(BF).astype(F32)
    return hi, mid, v - hi - mid


def attend_back_kernel(q0_ref, q1_ref, kvo_ref, kvs_ref, o_ref, l_ref, g_ref,
                       dq_ref, own_ref, other_ref, dk_ref, dv_ref):
    @pl.when(pl.program_id(0) == 0)
    def _():
        dk_ref[...] = jnp.zeros_like(dk_ref)
        dv_ref[...] = jnp.zeros_like(dv_ref)

    lane = lax.broadcasted_iota(jnp.int32, (256, 128), 1)
    q = jnp.concatenate([q0_ref[0], q1_ref[0]], 0)
    h0, h1, h2 = three(l_ref[0])
    ql = jnp.where(lane == 68, -h0, jnp.where(lane == 69, -h1, jnp.where(lane == 70, -h2, q.astype(F32))))
    ql = ql.astype(BF)
    g = g_ref[0].astype(F32)
    o = o_ref[0].astype(F32)
    g = jnp.concatenate([g, pltpu.roll(g, 64, 1)], 0)
    o = jnp.concatenate([o, pltpu.roll(o, 64, 1)], 0)
    g = jnp.where(lane < 64, g, 0.0)
    centre = jnp.sum(g * o, axis=1, keepdims=True)
    c0, c1, c2 = three(centre)
    gl = jnp.where(lane == 64, -c0, jnp.where(lane == 65, -c1, jnp.where(lane == 66, -c2, g)))
    gl = gl.astype(BF)
    gb = g.astype(BF)
    dq = jnp.zeros((256, 128), F32)
    for j in range(GROUP // CHUNK):
        rows = pl.ds(j * CHUNK, CHUNK)
        ref = kvo_ref if j * CHUNK < PLANE else kvs_ref
        part = pl.ds(j * CHUNK % PLANE, CHUNK)
        k = ref[0, part, :]
        st = dot(k, ql, NT)
        pt = jnp.exp2(st)
        gt = dot(ref[1, part, :], gl, NT)
        ds = (pt * gt).astype(BF)
        dv_ref[rows, :] += dot(pt.astype(BF), gb)
        dk_ref[rows, :] += dot(ds, q)
        dq = dq + dot(ds, k, TN)
    dq_ref[0] = dq

    @pl.when(pl.program_id(0) == 7)
    def _():
        low = lax.broadcasted_iota(jnp.int32, (128, 128), 1) < 64

        def block(j):
            rows = pl.ds(j * 128, 128)
            return jnp.where(low, dk_ref[rows, :] * LN2, pltpu.roll(dv_ref[rows, :], 64, 1))

        for j in range(8):
            own_ref[j] = block(j)
            other_ref[j] = block(8 + j).astype(BF)


def attend_back(q0, q1, own, sib, o, l, g):
    kv = whole(2, PLANE, 128)
    return pl.pallas_call(
        attend_back_kernel,
        grid=(8,),
        in_specs=[block3(128, 128), block3(128, 128), kv, kv, block3(128, 128), block3(256, 1), block3(128, 128)],
        out_specs=[block3(256, 128), whole(8, 128, 128), whole(8, 128, 128)],
        out_shape=[sds((8, 256, 128), F32), sds((8, 128, 128), F32), sds((8, 128, 128), BF)],
        scratch_shapes=[pltpu.VMEM((GROUP, 128), F32)] * 2,
        compiler_params=params(56),
        cost_estimate=cost(17),
        name="attend_back",
    )(q0, q1, own.reshape(2, PLANE, 128), sib.reshape(2, PLANE, 128), o, l, g)


def heads_back_kernel(dq_ref, own_ref, got_ref, raw_ref, f_ref, g_ref, c_ref, sin_ref, bd_ref,
                      out_ref, scaled_ref, gain_ref):
    @pl.when(pl.program_id(0) == 0)
    def _():
        gain_ref[...] = jnp.zeros_like(gain_ref)

    lane1 = lax.broadcasted_iota(jnp.int32, (128, 128), 1)
    dq = dq_ref[0] * HEAD**-0.5
    dq = jnp.where(lane1 < 64, dq[:128], pltpu.roll(dq[128:], 64, 1))
    d = jnp.concatenate([dq, own_ref[0] + got_ref[0].astype(F32)], 1)
    raw = raw_ref[0]
    lane = lax.broadcasted_iota(jnp.int32, (128, 256), 1)
    bd = bd_ref[...]
    fac = jnp.where(lane < 192, lax.rsqrt(exact_sums(raw * raw, bd) + EPS_HEAD), 1.0)
    hat = raw * fac
    c, s = wide_tables(c_ref[0], sin_ref[0], lane)
    dh = d * c - half_turn(d * s, lane)
    gain_ref[...] += jnp.sum(dh * hat, axis=0, keepdims=True)
    dn = dh * g_ref[...]
    back = fac * (dn - hat * exact_sums(dn * hat, bd))
    res = jnp.where(lane < 192, back, d)
    out_ref[0] = res.astype(BF)
    scaled_ref[0] = (res * f_ref[0]).astype(BF)


def heads_back(dq, own, got, raw, f, gains, cos, sin):
    return pl.pallas_call(
        heads_back_kernel,
        grid=(8,),
        in_specs=[block3(256, 128), block3(128, 128), block3(128, 128), block3(128, 256), block3(128, 1),
                  whole(1, 256), block3(128, 128), block3(128, 128), whole(256, 256)],
        out_specs=[block3(128, 256), block3(128, 256), whole(1, 256)],
        out_shape=[sds((8, 128, 256), BF), sds((8, 128, 256), BF), sds((1, 256), F32)],
        compiler_params=params(56),
        cost_estimate=cost(6),
        name="heads_back",
    )(dq, own, got, raw, f, gains, cos, sin, head_sums())


def norm_factor(v):
    return lax.rsqrt(jnp.mean(v * v, axis=1, keepdims=True) + EPS_WIDE)


def after_attention_kernel(s_ref, j_ref, *refs):
    own, sib = refs[0:4], refs[4]
    x_ref, g_ref, hidden_ref, middle_ref, w_ref = refs[5:]
    core, a, b = s_ref[0], s_ref[1], s_ref[2]
    for i, d in enumerate((1, 3, 2, 0)):
        for r in range(2):
            chip = ((a - d) & 3) * 2 + (b ^ (1 - r))
            at = chip * 128 + core * 64
            w_ref[pl.ds(pl.multiple_of(at, 64), 64), :] = own[i][r]
            at = chip * 128 + (1 - core) * 64
            w_ref[pl.ds(pl.multiple_of(at, 64), 64), :] = sib[i, r]
    hidden = x_ref[...].astype(F32)
    for j in range(8):
        hidden = hidden + dot(j_ref[j], w_ref[j * 128 : j * 128 + 128, :])
    hidden_ref[...] = hidden
    middle_ref[...] = (hidden * norm_factor(hidden) * g_ref[...]).astype(BF)


def after_attention(marks, joined, own, sib, x, gain):
    return pl.pallas_call(
        after_attention_kernel,
        grid_spec=pltpu.PrefetchScalarGridSpec(
            num_scalar_prefetch=1,
            grid=(1,),
            in_specs=[whole(8, 128, 128)] + [whole(2, 64, D)] * 4 + [whole(4, 2, 64, D), whole(128, D), whole(1, D)],
            out_specs=[whole(128, D), whole(128, D), whole(D, D)],
        ),
        out_shape=[sds((128, D), F32), sds((128, D), BF), sds((D, D), BF)],
        compiler_params=params(56),
        cost_estimate=cost(3),
        name="after_attention",
    )(marks, joined, *own, sib, x, gain)


def second_back_kernel(m_ref, hidden_ref, cot_ref, g_ref, w_ref, grad_ref, low_ref, joined_ref, gain_ref):
    mg = m_ref[0].astype(F32)
    for j in range(1, 8):
        mg = mg + m_ref[j].astype(F32)
    hidden = hidden_ref[...]
    f = norm_factor(hidden)
    hat = hidden * f
    gain_ref[...] = jnp.sum(mg * hat, axis=0, keepdims=True)
    dn = mg * g_ref[...]
    grad = cot_ref[...].astype(F32) + f * (dn - hat * jnp.mean(dn * hat, axis=1, keepdims=True))
    grad_ref[...] = grad
    low = grad.astype(BF)
    low_ref[...] = low
    joined = dot(low, w_ref[...], NT).astype(BF)
    for j in range(8):
        joined_ref[j] = joined[:, j * 128 : j * 128 + 128]


def second_back(chunks, hidden, cot, gain, w):
    return pl.pallas_call(
        second_back_kernel,
        out_shape=[sds((128, D), F32), sds((128, D), BF), sds((8, 128, 128), BF), sds((1, D), F32)],
        compiler_params=params(56),
        cost_estimate=cost(2),
        name="second_back",
    )(chunks, hidden, cot, gain, w)


def first_back_kernel(raw_ref, w_ref, x_ref, g_ref, grad_ref, out_ref):
    ng = dot(raw_ref[0], w_ref[0:256, :])
    for j in range(1, 8):
        ng = ng + dot(raw_ref[j], w_ref[j * 256 : j * 256 + 256, :])
    x = x_ref[...].astype(F32)
    f = norm_factor(x)
    hat = x * f
    dn = ng * g_ref[...]
    out_ref[...] = (grad_ref[...] + f * (dn - hat * jnp.mean(dn * hat, axis=1, keepdims=True))).astype(BF)


def first_back(raw, w, x, gain, grad):
    return pl.pallas_call(
        first_back_kernel,
        out_shape=sds((128, D), BF),
        compiler_params=params(56),
        cost_estimate=cost(2),
        name="first_back",
    )(raw, w, x, gain, grad)


def place_small_kernel(s_ref, p0, p1, p2, p3, own_ref, qkv_ref, out_ref):
    a, b = s_ref[3], s_ref[4]
    for ref, d in zip((p0, p1, p2, p3), (1, 3, 2, 0)):
        for r in range(2):
            at = pl.multiple_of((((a - d) & 3) * 2 + (b ^ (1 - r))) * 128, 128)
            v = ref[r].astype(F32)
            own_ref[pl.ds(at, 128), :] = v[:, :128].astype(BF)
            qkv_ref[:, pl.ds(at, 128)] = v[:, :128].T.astype(BF)
            out_ref[:, pl.ds(at, 128)] = v[:, 128:].T[:64].astype(BF)


def place_small(marks, pieces):
    return pl.pallas_call(
        place_small_kernel,
        grid_spec=pltpu.PrefetchScalarGridSpec(
            num_scalar_prefetch=1,
            grid=(1,),
            in_specs=[whole(2, 128, 256)] * 4,
            out_specs=[whole(D, 128), whole(128, D), whole(64, D)],
        ),
        out_shape=[sds((D, 128), BF), sds((128, D), BF), sds((64, D), BF)],
        compiler_params=params(56),
        cost_estimate=cost(2),
        name="place_small",
    )(marks, *pieces)


def given_gates_kernel(s_ref, own_ref, sib_ref, inv_ref, out_ref, dealt):
    core, a, b = s_ref[0], s_ref[1], s_ref[2]
    row = lax.broadcasted_iota(jnp.int32, (8, 128), 0)
    for ref, side in ((own_ref, core), (sib_ref, 1 - core)):
        for i, d in enumerate((1, 3, 2, 0)):
            for r in range(2):
                ex = ref[i, r].astype(F32)
                names = ex[:8, 0:128]
                values = ex[:8, 128:256] + ex[:8, 256:384] + ex[:8, 384:512]
                both = jnp.zeros((8, 128), F32)
                for e in range(2):
                    mine = (s_ref[6] * 2 + e).astype(F32)
                    g = jnp.sum(jnp.where(names == mine, values, 0.0), axis=0, keepdims=True)
                    both = jnp.where(row == e, g, both)
                dealt[((a - d) & 3) * 4 + (b ^ (1 - r)) * 2 + side] = both
    for n in range(16):
        slot = jnp.broadcast_to(inv_ref[n : n + 1, :], (8, 128))
        at, of = slot & 127, slot >> 7
        got = jnp.zeros((8, 128), F32)
        for k in range(16):
            got = jnp.where(of == k, jnp.take_along_axis(dealt[k], at, axis=1), got)
        out_ref[n] = got


def given_gates(marks, own, sib, inverse):
    extra = pl.BlockSpec((4, 2, 16, D), lambda i, s: (0, 0, 8, 0))
    return pl.pallas_call(
        given_gates_kernel,
        grid_spec=pltpu.PrefetchScalarGridSpec(
            num_scalar_prefetch=1,
            grid=(1,),
            in_specs=[extra, extra, whole(16, 128)],
            out_specs=whole(16, 8, 128),
            scratch_shapes=[pltpu.VMEM((16, 8, 128), F32)],
        ),
        out_shape=sds((16, 8, 128), F32),
        compiler_params=params(56),
        cost_estimate=cost(2),
        name="given_gates",
    )(marks, own, sib, inverse)


def inner_kernel(s_ref, own_ref, sib_ref, w_ref, out_ref, cot_ref):
    core, b = s_ref[0], s_ref[2]
    w = w_ref[...]
    for ref, side in ((own_ref, core), (sib_ref, 1 - core)):
        up = ref[0, :, :128]
        o = dot(up.reshape(256, D), w).astype(BF)
        for r in range(2):
            cot_ref[0, b ^ (1 - r), side] = up[r]
            out_ref[0, b ^ (1 - r), side] = o[r * 128 : r * 128 + 128]


def inner_products(marks, own, sib, w):
    side = pl.BlockSpec((1, 2, 144, D), lambda i, s: (i, 0, 0, 0))
    spec = pl.BlockSpec((1, 2, 2, 128, D), lambda i, s: (s[16 + i], 0, 0, 0, 0))
    return pl.pallas_call(
        inner_kernel,
        grid_spec=pltpu.PrefetchScalarGridSpec(
            num_scalar_prefetch=1,
            grid=(4,),
            in_specs=[side, side, pl.BlockSpec((D, 2 * FF), lambda i, s: (0, 2))],
            out_specs=[spec, spec],
        ),
        out_shape=[sds((4, 2, 2, 128, D), BF)] * 2,
        compiler_params=params(56),
        cost_estimate=cost(8),
        name="inner_products",
    )(marks, own, sib, w)


def experts_kernel(s_ref, mid_ref, pre_ref, g_ref, w_ref, entry_ref, gg_ref, ug_ref, in_ref):
    mid = mid_ref[...].reshape(256, D)
    gates = jnp.concatenate([g_ref[0, 0, 0].T, g_ref[0, 1, 0].T], 0)
    entry = None
    for e in range(2):
        cg = slice(e * FF, e * FF + FF)
        cu = slice(1024 + e * FF, 1024 + e * FF + FF)
        gp = dot(mid, w_ref[:, cg])
        u = dot(mid, w_ref[:, cu])
        g = gates[:, e : e + 1]
        ig = pre_ref[0, :, 0, :, cg].reshape(256, FF).astype(F32) * g
        sig = 0.5 * jnp.tanh(0.5 * gp) + 0.5
        act = gp * sig
        inner = (g * act * u).astype(BF)
        gg = (ig * u * (sig + act * (1.0 - sig))).astype(BF)
        ug = (ig * act).astype(BF)
        part = dot(gg, w_ref[:, cg], NT) + dot(ug, w_ref[:, cu], NT)
        entry = part if entry is None else entry + part
        for ref, v in ((in_ref, inner), (gg_ref, gg), (ug_ref, ug)):
            ref[0, :, :, cg] = v.reshape(2, 128, FF)
    entry_ref[...] = entry.astype(BF).reshape(1, 2, 128, D)


def run_experts(marks, which, mid, pre, gates, w):
    def group(n, m):
        return pl.BlockSpec((1, 2, 1, n, m), lambda i, s: (i, 0, s[which], 0, 0))

    hid = pl.BlockSpec((1, 2, 128, 2 * FF), lambda i, s: (i, 0, 0, 0))
    return pl.pallas_call(
        experts_kernel,
        grid_spec=pltpu.PrefetchScalarGridSpec(
            num_scalar_prefetch=1,
            grid=(4,),
            in_specs=[group(128, D), group(128, D), group(8, 128), whole(D, 4 * FF)],
            out_specs=[hid] * 4,
        ),
        out_shape=[sds((4, 2, 128, D), BF)] * 4,
        compiler_params=params(56),
        cost_estimate=cost(14),
        name="run_experts",
    )(marks, mid, pre, gates, w)


def add_pair_kernel(a_ref, b_ref, out_ref):
    out_ref[...] = (a_ref[...].astype(F32) + b_ref[...].astype(F32)).astype(BF)


def add_pair(a, b):
    spec = pl.BlockSpec((2, 128, D), lambda i: (i, 0, 0))
    return pl.pallas_call(
        add_pair_kernel,
        grid=(4,),
        in_specs=[spec, spec],
        out_specs=spec,
        out_shape=sds((8, 128, D), BF),
        compiler_params=params(8),
        cost_estimate=cost(2),
        name="add_pair",
    )(a.reshape(8, 128, D), b.reshape(8, 128, D))


def results_kernel(a_ref, b_ref, w_ref, x_ref, y_ref):
    w = w_ref[...]
    for i_ref, o_ref in ((a_ref, x_ref), (b_ref, y_ref)):
        o_ref[...] = dot(i_ref[...].reshape(512, 2 * FF), w, NT).astype(BF).reshape(2, 2, 128, D)


def results(one, two, w):
    hid = pl.BlockSpec((2, 2, 128, 2 * FF), lambda i: (i, 0, 0, 0))
    return pl.pallas_call(
        results_kernel,
        grid=(2,),
        in_specs=[hid, hid, pl.BlockSpec((D, 2 * FF), lambda i: (0, 2))],
        out_specs=[hid, hid],
        out_shape=[sds((4, 2, 128, D), BF)] * 2,
        compiler_params=params(56),
        cost_estimate=cost(8),
        name="results",
    )(one, two, w)


def add_up_kernel(h_ref, m_ref, out_ref):
    t = h_ref[...]
    for j in range(8):
        t = t + m_ref[j].astype(F32)
    out_ref[...] = t.astype(BF)


def add_up(hidden, chunks):
    return pl.pallas_call(
        add_up_kernel,
        out_shape=sds((128, D), BF),
        compiler_params=params(8),
        cost_estimate=cost(2),
        name="add_up",
    )(hidden, chunks)


def weights_kernel(s_ref, *refs):
    out_ref = refs[-1]
    for n in range(len(refs) // 4):
        l0, l1, r0, r1 = refs[4 * n : 4 * n + 4]
        o = dot(l0[...].reshape(PLANE, 256), r0[...].reshape(PLANE, 1024), TN)
        o = o + dot(l1[...].reshape(PLANE, 256), r1[...].reshape(PLANE, 1024), TN)
        out_ref[:, n * 1024 : n * 1024 + 1024] = o.astype(BF)


def weight_grads(marks, *sides):
    def side(which):
        return pl.BlockSpec((4, 2, 1, 128, 256), lambda i, s: (0, 0, s[which], 0, i))

    hid = whole(4, 2, 128, 2 * FF)
    n = len(sides)
    args = []
    for left, right in sides:
        args += [left, left, *right]
    return pl.pallas_call(
        weights_kernel,
        grid_spec=pltpu.PrefetchScalarGridSpec(
            num_scalar_prefetch=1,
            grid=(4,),
            in_specs=[side(0), side(5), hid, hid] * n,
            out_specs=pl.BlockSpec((256, n * 2 * FF), lambda i, s: (i, 0)),
        ),
        out_shape=sds((D, n * 2 * FF), BF),
        compiler_params=params(56),
        cost_estimate=cost(8 * n),
        name="weight_grads",
    )(marks, *args)


def unpack_kernel(a_ref, g_ref, u_ref, d_ref):
    t = a_ref[...].astype(F32)
    for e in range(2):
        at = e * FF
        g_ref[:, e, :] = t[:, at : at + FF]
        u_ref[:, e, :] = t[:, 1024 + at : 1024 + at + FF]
        d_ref[:, e, :] = t[:, 2048 + at : 2048 + at + FF]


def unpack(*parts):
    return pl.pallas_call(
        unpack_kernel,
        out_shape=[sds((128, 2, FF), F32)] * 3,
        compiler_params=params(12),
        cost_estimate=cost(2),
        name="unpack",
    )(*parts)


def qkv_grads_kernel(s_ref, x0, x1, x2, x3, r_ref, w_ref, g_ref, second_ref, heads_ref, ho_ref, hx_ref,
                     own_ref, other_ref, gains_ref):
    core = s_ref[0]
    i = pl.program_id(0)

    @pl.when(i == 0)
    def _():
        gains_ref[...] = jnp.zeros_like(gains_ref)
        gains_ref[8:9, :] = heads_ref[...]

    gains_ref[pl.ds(4 + i, 1), :] = second_ref[...]
    a, b = s_ref[1], s_ref[2]
    o = jnp.zeros((256, 256), F32)
    for ref, d in zip((x0, x1, x2, x3), (1, 3, 2, 0)):
        at = ((a - d) & 3) * 2
        both = jnp.concatenate([r_ref[at + (b ^ 1)], r_ref[at + b]], 0)
        o = o + dot(ref[...].reshape(256, 256), both, TN)
    first = jnp.sum(o * w_ref[...].astype(F32), axis=1, keepdims=True)
    gains_ref[pl.ds(i, 1), :] = jnp.broadcast_to(first, (256, 128)).T[:1]
    o = o * g_ref[...]
    own_ref[:, :128] = jnp.where(core == 0, o[:, :128], o[:, 128:])
    own_ref[:, 128:] = ho_ref[...]
    other_ref[:, :128] = jnp.where(core == 0, o[:, 128:], o[:, :128]).astype(BF)
    other_ref[:, 128:] = hx_ref[...]


def qkv_grads(marks, x, r, w, gain, second, heads, own, other):
    rows = lambda m: pl.BlockSpec((256, m), lambda i, s: (i, 0))
    return pl.pallas_call(
        qkv_grads_kernel,
        grid_spec=pltpu.PrefetchScalarGridSpec(
            num_scalar_prefetch=1,
            grid=(4,),
            in_specs=[pl.BlockSpec((2, 128, 256), lambda i, s: (0, 0, i))] * 4 + [whole(8, 128, 256),
                      rows(256), rows(1), pl.BlockSpec((1, 256), lambda i, s: (0, i)), whole(1, 256),
                      rows(128), rows(128)],
            out_specs=[rows(256), rows(256), whole(16, 256)],
        ),
        out_shape=[sds((D, 256), F32), sds((D, 256), BF), sds((16, 256), F32)],
        compiler_params=params(56),
        cost_estimate=cost(4),
        name="qkv_grads",
    )(marks, *x, r, w, gain, second, heads, own, other)


def write_gains(ref, at, gains):
    for k, part in enumerate(three(gains)):
        ref[at + 16 * k : at + 16 * k + 16, :] = part.astype(BF)


def read_gains(ref, at):
    g = ref[at : at + 16, :].astype(F32) + ref[at + 16 : at + 32, :].astype(F32)
    return g + ref[at + 32 : at + 48, :].astype(F32)


def out_grads_kernel(s_ref, h0, h1, h2, h3, j_ref, own_ref, other_ref):
    core, a, b = s_ref[0], s_ref[1], s_ref[2]
    acc = jnp.zeros((D, 128), F32)
    for ref, d in zip((h0, h1, h2, h3), (1, 3, 2, 0)):
        at = ((a - d) & 3) * 2
        both = jnp.concatenate([j_ref[at + (b ^ 1)], j_ref[at + b]], 0)
        acc = acc + dot(ref[...].reshape(256, D), both, TN)
    swapped = pltpu.roll(acc, 64, 1)
    low = lax.broadcasted_iota(jnp.int32, (D, 128), 1) < 64
    own_ref[...] = jnp.where(low, jnp.where(core == 0, acc, swapped), 0.0)
    other_ref[...] = jnp.where(low, jnp.where(core == 0, swapped, acc), 0.0).astype(BF)


def out_grads(marks, pieces, joined):
    return pl.pallas_call(
        out_grads_kernel,
        grid_spec=pltpu.PrefetchScalarGridSpec(
            num_scalar_prefetch=1,
            grid=(1,),
            in_specs=[whole(2, 128, D)] * 4 + [whole(8, 128, 128)],
            out_specs=[whole(D, 128), whole(D, 128)],
        ),
        out_shape=[sds((D, 128), F32), sds((D, 128), BF)],
        compiler_params=params(56),
        cost_estimate=cost(3),
        name="out_grads",
    )(marks, *pieces, joined)


def ring_parts_kernel(s_ref, own_ref, gains_ref, got_ref, keep_ref, m1, m3, m2):
    a, b = s_ref[3], s_ref[4]

    def rows(chunk):
        at = pl.ds(pl.multiple_of(chunk * 128, 128), 128)
        return own_ref[at, :] + got_ref[at, :].astype(F32)

    gains = gains_ref[...]
    for d, ref in ((1, m1), (3, m3), (2, m2)):
        at = ((a + d) & 3) * 2
        ref[:128, :] = rows(at + (b ^ 1)).astype(BF)
        ref[128:256, :] = rows(at + b).astype(BF)
        write_gains(ref, 256, gains)
    at = a * 2
    keep_ref[0] = rows(at + (b ^ 1))
    keep_ref[1] = rows(at + b)


def ring_parts(marks, own, gains, got):
    return pl.pallas_call(
        ring_parts_kernel,
        grid_spec=pltpu.PrefetchScalarGridSpec(
            num_scalar_prefetch=1,
            grid=(1,),
            in_specs=[whole(D, 256), whole(16, 256), whole(D, 256)],
            out_specs=[whole(2, 128, 256)] + [whole(304, 256)] * 3,
        ),
        out_shape=[sds((2, 128, 256), F32)] + [sds((304, 256), BF)] * 3,
        compiler_params=params(56),
        cost_estimate=cost(2),
        name="ring_parts",
    )(marks, own, gains, got)


def pair_parts_kernel(keep_ref, gains_ref, m1, m3, m2, own_ref, out_ref, msg_ref):
    other, own = keep_ref[0], keep_ref[1]
    gains = gains_ref[...]
    for ref in (m1, m3, m2):
        other = other + ref[:128, :].astype(F32)
        own = own + ref[128:256, :].astype(F32)
        gains = gains + read_gains(ref, 256)
    own_ref[...] = own
    out_ref[...] = gains
    msg_ref[:128, :] = other.astype(BF)
    write_gains(msg_ref, 128, gains)


def pair_parts(keep, gains, got):
    return pl.pallas_call(
        pair_parts_kernel,
        out_shape=[sds((128, 256), F32), sds((16, 256), F32), sds((176, 256), BF)],
        compiler_params=params(56),
        cost_estimate=cost(2),
        name="pair_parts",
    )(keep, gains, *got)


def last_parts_kernel(own_ref, gains_ref, got_ref, qkv_ref, out_ref, sum_ref):
    t = own_ref[...] + got_ref[:128, :].astype(F32)
    sum_ref[...] = gains_ref[...] + read_gains(got_ref, 128)
    qkv_ref[...] = t[:, :128]
    out_ref[...] = t[:, 128:192]


def last_parts(own, gains, got):
    return pl.pallas_call(
        last_parts_kernel,
        out_shape=[sds((128, 128), F32), sds((128, 64), F32), sds((16, 256), F32)],
        compiler_params=params(56),
        cost_estimate=cost(2),
        name="last_parts",
    )(own, gains, got)


def body(tokens, cotangent, deal_order, lengths, routes, route_gates, gain_first, gain_second, gain_query, gain_key,
         weight_qkv, weight_out, weight_gate, weight_up, weight_down):
    col = lax.axis_index("col")
    core = col % 2
    a, b = place("col")
    ra, rb = place("row")
    order = [(a + d) % 4 for d in (1, 3, 2, 0)]
    row_order = [(ra + d) % 4 for d in (1, 3, 2, 0)]
    back = [(a - d) % 4 for d in (1, 3, 2, 0)]
    marks = jnp.stack([core, a, b, ra, rb, 1 - core, col, core] + order + row_order + back).astype(jnp.int32)
    planes = [[i for i in range(16) if i % 2 == k] for k in range(2)]
    swap_all = partial(lax.all_to_all, axis_name="col", split_axis=0, concat_axis=0, tiled=True,
                       axis_index_groups=planes)

    extra = jnp.concatenate([routes.T.astype(BF)] + [p.T.astype(BF) for p in three(route_gates)], 1)
    cot = jnp.concatenate([cotangent, jnp.pad(extra, ((0, 8), (0, 512)))], 0)
    wide = jnp.concatenate([w.reshape(128, 2 * FF) for w in (weight_gate, weight_up, weight_down)], 1).astype(BF)
    w_all = lax.all_gather(wide, "row", axis=0, tiled=True)

    small = jnp.pad(jnp.concatenate([weight_qkv, weight_out], 1), ((0, 0), (0, 64))).astype(BF)
    near, small_pair = together(step_pair(tokens, "col"), step_pair(small, "row"))
    x_pieces = gather_rest(near, tokens, "col")
    w_own, qkv_t, out_t = place_small(marks, gather_rest(small_pair, small, "row"))
    w_pair = step_core(w_own)
    w_pair, *x_pieces = together(w_pair, *x_pieces)
    out_pair = jnp.stack([step_pair(out_t, "col"), out_t])
    w_chip = jnp.where(core == 0, jnp.concatenate([w_own, w_pair], 1), jnp.concatenate([w_pair, w_own], 1))
    w_scaled = (gain_first[:, None] * w_chip.astype(F32)).astype(BF)

    deal_row = deal_order[0]
    slots = jnp.arange(GROUP, dtype=jnp.int32)
    inverse = jnp.zeros((GROUP,), jnp.int32).at[deal_row].set(slots).reshape(8, 2, 128)
    mine = lax.dynamic_index_in_dim(inverse, core, 1, keepdims=False).reshape(PLANE)
    finish = jnp.cumsum(lengths[0])
    starts = finish - lengths[0]
    segment = jnp.sum((mine[:, None] >= finish[None, :]).astype(jnp.int32), axis=1)
    labels = jnp.arange(4, dtype=jnp.int32)
    anchor = jnp.sum(jnp.where(segment[:, None] == labels[None, :], starts[None, :], 0), axis=1)
    offset = (mine - anchor).astype(F32)
    frequency = THETA ** (-(jnp.arange(128) % 32).astype(F32) * 2.0 / HEAD)
    angles = offset[:, None] * frequency[None, :]
    cos, sin = jnp.cos(angles).reshape(8, 128, 128), jnp.sin(angles).reshape(8, 128, 128)
    gains = jnp.concatenate([gain_query, gain_query, gain_key, jnp.ones((HEAD,), F32)])[None, :]

    out_pair, w_scaled, cos, sin, segment, cot, *x_pieces = together(
        out_pair, w_scaled, cos, sin, segment, cot, *x_pieces)
    cot_near = step_pair(cot, "col")
    out_own = [step_ring(out_pair, "col", d) for d in AHEAD] + [out_pair]
    q0, q1, kv, raw, f1_all = project_heads(
        marks, x_pieces, w_scaled, gains, cos, sin, segment.reshape(8, 128, 1))
    kv_sib = step_core(kv)
    joined, logs = attend(q0, q1, kv, kv_sib)
    joined, cot_near, *out_own = together(joined, cot_near, *out_own)
    cot_ring = gather_rest(cot_near, cot, "col")
    out_sib = step_core(jnp.stack(out_own))
    joined_got = swap_all(joined)
    cot_own = jnp.stack(cot_ring)
    hidden, middle, wout_t = after_attention(marks, joined_got, out_own, out_sib, tokens, gain_second[None])
    mid_all = lax.all_gather(middle, "col", axis=0, tiled=True).reshape(4, 2, 2, 128, D)
    cot_own, hidden = together(cot_own, hidden)
    cot_sib = step_core(cot_own)
    gates = given_gates(marks, cot_own, cot_sib, inverse.reshape(16, 128)).reshape(4, 2, 2, 8, 128)
    pre, cot_all = inner_products(marks, cot_own, cot_sib, w_all)

    e_other, gg1, ug1, in1 = run_experts(marks, 5, mid_all, pre, gates, w_all)
    qkv_t, e_other = together(qkv_t, e_other)
    wqkv_t = lax.all_gather(qkv_t, "col", axis=0, tiled=True)
    e_got = step_core(e_other)
    e_own, gg0, ug0, in0 = run_experts(marks, 0, mid_all, pre, gates, w_all)
    entry = add_pair(e_own, e_got)
    entry, gg0 = together(entry, gg0)
    entry_got = swap_all(entry)
    grads = weight_grads(marks, (mid_all, (gg0, gg1)), (mid_all, (ug0, ug1)), (cot_all, (in0, in1)))
    in1, grads = together(in1, grads)
    r_other, r_own = results(in1, in0, w_all)

    entry_got, grads, r_own, r_other = together(entry_got, grads, r_own, r_other)
    grads = lax.psum_scatter(grads, "row", scatter_dimension=0, tiled=True)
    hidden_grad, hidden_low, joined_grad, second = second_back(entry_got, hidden, cotangent, gain_second[None], wout_t)
    joined_grad, r_other = together(joined_grad, r_other)
    joined_grad = swap_all(joined_grad)
    r_sum = add_pair(r_own, step_core(r_other))
    hidden_pair = jnp.stack([step_pair(hidden_low, "col"), hidden_low])
    joined_grad, r_sum, hidden_pair = together(joined_grad, r_sum, hidden_pair)
    hidden_pieces = [step_ring(hidden_pair, "col", d) for d in AHEAD] + [hidden_pair]
    dq, dkv_own, dkv_other = attend_back(q0, q1, kv, kv_sib, joined, logs, joined_grad)
    dkv_got = step_core(dkv_other)
    dq, *hidden_pieces = together(dq, *hidden_pieces)
    own_o, other_o = out_grads(marks, hidden_pieces, joined)
    dq, own_o = together(dq, own_o)
    raw_grad, raw_scaled, gain_heads = heads_back(dq, dkv_own, dkv_got, raw, f1_all, gains, cos, sin)
    raw_got = swap_all(raw_grad)
    own, msg, sums = qkv_grads(
        marks, x_pieces, raw_scaled, w_chip, gain_first[:, None], second, gain_heads, own_o, other_o)
    for n in (0, 1, 2, 3):
        sums = sums + lax.ppermute(sums, "col", [(i, i ^ (1 << n)) for i in range(16)])
    raw_got, sums, r_sum = together(raw_got, sums, r_sum)
    out_got = swap_all(r_sum)
    keep, *msgs = ring_parts(marks, own, sums, step_core(msg))
    own, sums, msg = pair_parts(keep, sums, [step_ring(m, "row", d) for m, d in zip(msgs, AHEAD)])
    grad_qkv, grad_out, sums = last_parts(own, sums, step_pair(msg, "row"))

    input_grad = first_back(raw_got, wqkv_t, tokens, gain_first[None], hidden_grad)
    block_out = add_up(hidden, out_got)
    grads_w = unpack(grads)
    heads = sums[8]
    return (
        block_out,
        input_grad,
        sums[:4].reshape(-1),
        sums[4:8].reshape(-1),
        heads[:64] + heads[64:128],
        heads[128:192],
        grad_qkv,
        grad_out,
        *grads_w,
    )


def solution(mesh):
    both = P(("row", "col"), None)
    return jax.shard_map(
        body,
        mesh=mesh,
        in_specs=(both, both, P("row", None), P("row", None), both, both, P(), P(), P(), P(),
                  P("row", "col"), P("row", "col"), P("row", "col", None), P("row", "col", None),
                  P("row", "col", None)),
        out_specs=(both, both, P(), P(), P(), P(), P("row", "col"), P("row", "col"), P("row", "col", None),
                   P("row", "col", None), P("row", "col", None)),
        check_vma=False,
    )
```

```python
from functools import partial

import jax
import jax.numpy as jnp
import numpy as np
from jax import lax
from jax.experimental import pallas as pl
from jax.experimental.pallas import tpu as pltpu
from jax.sharding import PartitionSpec as P

D = 1024
HEAD = 64
EXPERTS = 32
FF = 512
TOP = 8
TOK = 128
GROUP = 2048
PLANE = 1024
EPS_WIDE = 1e-05
EPS_HEAD = 1e-06
THETA = 10000.0
LOG2E = 1.4426950408889634
LN2 = 0.6931471805599453
QSCALE = LOG2E * HEAD**-0.5
APART = -256.0
BF = jnp.bfloat16
F32 = jnp.float32
NT = (((1,), (1,)), ((), ()))
TN = (((0,), (0,)), ((), ()))
HIGH = lax.Precision.HIGHEST


def params(mib=56):
    return pltpu.CompilerParams(vmem_limit_bytes=mib * 2**20)


def cost(us, scale=0.02):
    us = us * scale
    return pl.CostEstimate(flops=int(us * 1e9), bytes_accessed=int(us * 1e6), transcendentals=0)


def dot(a, b, dims=None):
    if dims is None:
        dims = (((1,), (0,)), ((), ()))
    return lax.dot_general(a, b, dims, preferred_element_type=F32)


def sds(shape, kind):
    return jax.ShapeDtypeStruct(shape, kind)


def whole(*shape):
    return pl.BlockSpec(shape, lambda *_: (0,) * len(shape))


def together(*values):
    return lax.optimization_barrier(values)


AHEAD = (1, 3, 2)


def step_pair(v, axis):
    if axis == "row":
        route = [(i, i ^ 1) for i in range(8)]
    else:
        route = [(i, i ^ 2) for i in range(16)]
    return lax.ppermute(v, axis, route)


def step_ring(v, axis, d):
    if axis == "row":
        route = [(i, (i + 2 * d) % 8) for i in range(8)]
    else:
        route = [(i, (i + 4 * d) % 16) for i in range(16)]
    return lax.ppermute(v, axis, route)


def step_core(v):
    return lax.ppermute(v, "col", [(i, i ^ 1) for i in range(16)])


def place(axis):
    i = lax.axis_index(axis)
    if axis == "col":
        i = i // 2
    return i // 2, i % 2


def gather_rest(pair, v, axis):
    pair = jnp.stack([pair, v])
    return [step_ring(pair, axis, d) for d in AHEAD] + [pair]


def gather_plain(v, axis):
    return gather_rest(step_pair(v, axis), v, axis)


def added(terms):
    t = terms[0].astype(F32)
    for r in terms[1:]:
        t = t + r.astype(F32)
    return t


def places_kernel(s_ref, l_ref, deal_ref, inv_ref, seg_ref, off_ref):
    core = s_ref[0]
    row = lax.broadcasted_iota(jnp.int32, (128, 128), 0)
    lane = lax.broadcasted_iota(jnp.int32, (128, 128), 1)
    ends = [l_ref[0, 0]]
    for n in range(1, 4):
        ends.append(ends[-1] + l_ref[0, n])
    for k in range(16):
        found = jnp.zeros((128, 128), jnp.int32)
        for n in range(16):
            deal = jnp.broadcast_to(deal_ref[n : n + 1, :], (128, 128))
            found = jnp.where(deal == row + k * 128, lane + n * 128, found)
        slot = jnp.sum(found.astype(F32), axis=1, keepdims=True)
        inv_ref[k : k + 1, :] = jnp.broadcast_to(slot, (128, 128)).T[:1].astype(jnp.int32)
        slot = slot.astype(jnp.int32)
        seg = jnp.zeros((128, 1), jnp.int32)
        start = jnp.zeros((128, 1), jnp.int32)
        for end in ends:
            seg = seg + jnp.where(slot >= end, 1, 0)
            start = jnp.where(slot >= end, end, start)

        @pl.when(core == k % 2)
        def _():
            seg_ref[k // 2] = seg
            off_ref[k // 2] = (slot - start).astype(F32)


def places(marks, lengths, deal):
    return pl.pallas_call(
        places_kernel,
        grid_spec=pltpu.PrefetchScalarGridSpec(
            num_scalar_prefetch=2,
            grid=(1,),
            in_specs=[whole(16, 128)],
            out_specs=[whole(16, 128), whole(8, 128, 1), whole(8, 128, 1)],
        ),
        out_shape=[sds((16, 128), jnp.int32), sds((8, 128, 1), jnp.int32), sds((8, 128, 1), F32)],
        compiler_params=params(56),
        cost_estimate=cost(3),
        name="places",
    )(marks, lengths, deal)


def head_sums():
    i = np.arange(256) // HEAD
    return jnp.asarray((i[:, None] == i[None, :]) / HEAD, BF)


def spread():
    s = np.zeros((256, 512), np.float32)
    for h in range(4):
        for i in range(64):
            s[h * 64 + i, h * 128 + i] = 1.0
    return jnp.asarray(s, BF)


def exact_sums(v, sums):
    hi = v.astype(BF)
    lo = (v - hi.astype(F32)).astype(BF)
    return dot(hi, sums) + dot(lo, sums)


def half_turn(v, lane):
    back = jnp.concatenate([pltpu.roll(v[:, :128], 96, 1), pltpu.roll(v[:, 128:], 96, 1)], 1)
    ahead = jnp.concatenate([pltpu.roll(v[:, :128], 32, 1), pltpu.roll(v[:, 128:], 32, 1)], 1)
    return jnp.where(lane % 64 < 32, -back, ahead)


def wide_tables(c, s, lane):
    c = jnp.where(lane < 192, jnp.concatenate([c, c], 1), 1.0)
    s = jnp.where(lane < 192, jnp.concatenate([s, s], 1), 0.0)
    return c, s


def heads_kernel(s_ref, x0, x1, x2, x3, w_ref, g_ref, c_ref, s_tab_ref, seg_ref, bd_ref, sp_ref,
                 q0_ref, q1_ref, kv_ref, raw_ref, f_ref):
    a, b = s_ref[1], s_ref[2]
    lane = lax.broadcasted_iota(jnp.int32, (256, 256), 1)
    l1 = lax.broadcasted_iota(jnp.int32, (256, 128), 1)
    inseg = (l1 >= 64) & (l1 < 68)
    aug_v = jnp.where((l1 >= 64) & (l1 < 67), 1.0, 0.0)
    for ref, d in zip((x0, x1, x2, x3), (1, 3, 2, 0)):
        at = ((a - d) & 3) * 2
        blocks = (at + (b ^ 1), at + b)

        def both(r):
            return jnp.concatenate([r[blocks[0]], r[blocks[1]]], 0)

        def put(r, v):
            r[blocks[0]] = v[:128]
            r[blocks[1]] = v[128:]

        x = ref[...].reshape(256, D)
        xf = x.astype(F32)
        f = lax.rsqrt(jnp.mean(xf * xf, axis=1, keepdims=True) + EPS_WIDE)
        raw = dot(x, w_ref[...]) * f
        put(raw_ref, raw)
        put(f_ref, f)
        fac = jnp.where(lane < 192, lax.rsqrt(exact_sums(raw * raw, bd_ref[...]) + EPS_HEAD), 1.0)
        h = raw * fac * g_ref[...]
        c, s = wide_tables(both(c_ref), both(s_tab_ref), lane)
        t = h * c + half_turn(h, lane) * s
        t = jnp.where(lane < 128, t * QSCALE, t).astype(BF)
        wide = dot(t, sp_ref[...])
        same = (l1 - 64) == both(seg_ref)
        aug_q = jnp.where(inseg & jnp.logical_not(same), APART, 0.0)
        aug_k = jnp.where((inseg & same) | ((l1 >= 68) & (l1 < 71)), 1.0, 0.0)
        put(q0_ref, (wide[:, 0:128] + aug_q).astype(BF))
        put(q1_ref, (wide[:, 128:256] + aug_q).astype(BF))
        put(kv_ref.at[0], (wide[:, 256:384] + aug_k).astype(BF))
        put(kv_ref.at[1], (wide[:, 384:512] + aug_v).astype(BF))


def project_heads(marks, pieces, w, gains, cos, sin, seg):
    return pl.pallas_call(
        heads_kernel,
        grid_spec=pltpu.PrefetchScalarGridSpec(
            num_scalar_prefetch=1,
            grid=(1,),
            in_specs=[whole(2, 128, D)] * 4 + [whole(D, 256), whole(1, 256), whole(8, 128, 128), whole(8, 128, 128),
                                               whole(8, 128, 1), whole(256, 256), whole(256, 512)],
            out_specs=[whole(8, 128, 128)] * 2 + [whole(2, 8, 128, 128), whole(8, 128, 256), whole(8, 128, 1)],
        ),
        out_shape=[sds((8, 128, 128), BF)] * 2 + [sds((2, 8, 128, 128), BF), sds((8, 128, 256), F32),
                                                  sds((8, 128, 1), F32)],
        compiler_params=params(56),
        cost_estimate=cost(7),
        name="project_heads",
    )(marks, *pieces, w, gains, cos, sin, seg, head_sums(), spread())


WIDE = 512


def attend_kernel(q0_ref, q1_ref, own_ref, sib_ref, o_ref, l_ref):
    q = jnp.concatenate([q0_ref[...].reshape(WIDE, 128), q1_ref[...].reshape(WIDE, 128)], 0)
    acc = jnp.zeros((128, 2 * WIDE), F32)
    for ref in (own_ref, sib_ref):
        p = jnp.exp2(dot(ref[0], q, NT)).astype(BF)
        acc = acc + dot(ref[1], p, TN)
    acc = acc.T
    total = acc[:, 64:65]
    o = acc / total
    l_ref[...] = jnp.log2(total).reshape(2, 4, 128, 1)
    lane = lax.broadcasted_iota(jnp.int32, (WIDE, 128), 1)
    o = jnp.where(lane < 64, o[:WIDE], pltpu.roll(o[WIDE:], 64, 1))
    o_ref[...] = o.astype(BF).reshape(4, 128, 128)


def four(n, m):
    return pl.BlockSpec((4, n, m), lambda j: (j, 0, 0))


def two_four(n, m):
    return pl.BlockSpec((2, 4, n, m), lambda j: (0, j, 0, 0))


def attend(q0, q1, own, sib):
    return pl.pallas_call(
        attend_kernel,
        grid=(2,),
        in_specs=[four(128, 128), four(128, 128), whole(2, PLANE, 128), whole(2, PLANE, 128)],
        out_specs=[four(128, 128), two_four(128, 1)],
        out_shape=[sds((8, 128, 128), BF), sds((2, 8, 128, 1), F32)],
        compiler_params=params(56),
        cost_estimate=cost(7),
        name="attend",
    )(q0, q1, own.reshape(2, PLANE, 128), sib.reshape(2, PLANE, 128))


def three(v):
    hi = v.astype(BF).astype(F32)
    mid = (v - hi).astype(BF).astype(F32)
    return hi, mid, v - hi - mid


def attend_back_kernel(q0_ref, q1_ref, kvo_ref, kvs_ref, o_ref, l_ref, g_ref,
                       dq_ref, own_ref, other_ref, dk_ref, dv_ref):
    @pl.when(pl.program_id(0) == 0)
    def _():
        dk_ref[...] = jnp.zeros_like(dk_ref)
        dv_ref[...] = jnp.zeros_like(dv_ref)

    lane = lax.broadcasted_iota(jnp.int32, (2 * WIDE, 128), 1)
    q = jnp.concatenate([q0_ref[...].reshape(WIDE, 128), q1_ref[...].reshape(WIDE, 128)], 0)
    h0, h1, h2 = three(l_ref[...].reshape(2 * WIDE, 1))
    ql = jnp.where(lane == 68, -h0, jnp.where(lane == 69, -h1, jnp.where(lane == 70, -h2, q.astype(F32))))
    ql = ql.astype(BF)
    g = g_ref[...].reshape(WIDE, 128).astype(F32)
    o = o_ref[...].reshape(WIDE, 128).astype(F32)
    g = jnp.concatenate([g, pltpu.roll(g, 64, 1)], 0)
    o = jnp.concatenate([o, pltpu.roll(o, 64, 1)], 0)
    g = jnp.where(lane < 64, g, 0.0)
    centre = jnp.sum(g * o, axis=1, keepdims=True)
    c0, c1, c2 = three(centre)
    gl = jnp.where(lane == 64, -c0, jnp.where(lane == 65, -c1, jnp.where(lane == 66, -c2, g)))
    gl = gl.astype(BF)
    gb = g.astype(BF)
    dq = jnp.zeros((128, 2 * WIDE), F32)
    for j in range(GROUP // WIDE):
        rows = pl.ds(j * WIDE, WIDE)
        ref = kvo_ref if j * WIDE < PLANE else kvs_ref
        part = pl.ds(j * WIDE % PLANE, WIDE)
        k = ref[0, part, :]
        pt = jnp.exp2(dot(k, ql, NT))
        ds = (pt * dot(ref[1, part, :], gl, NT)).astype(BF)
        dv_ref[rows, :] += dot(pt.astype(BF), gb)
        dk_ref[rows, :] += dot(ds, q)
        dq = dq + dot(k, ds, TN)
    dq_ref[...] = dq.T.reshape(2, 4, 128, 128)

    @pl.when(pl.program_id(0) == 1)
    def _():
        low = lax.broadcasted_iota(jnp.int32, (128, 128), 1) < 64

        def block(j):
            rows = pl.ds(j * 128, 128)
            return jnp.where(low, dk_ref[rows, :] * LN2, pltpu.roll(dv_ref[rows, :], 64, 1))

        for j in range(8):
            own_ref[j] = block(j)
            other_ref[j] = block(8 + j).astype(BF)


def attend_back(q0, q1, own, sib, o, l, g):
    kv = whole(2, PLANE, 128)
    return pl.pallas_call(
        attend_back_kernel,
        grid=(2,),
        in_specs=[four(128, 128), four(128, 128), kv, kv, four(128, 128), two_four(128, 1), four(128, 128)],
        out_specs=[two_four(128, 128), whole(8, 128, 128), whole(8, 128, 128)],
        out_shape=[sds((2, 8, 128, 128), F32), sds((8, 128, 128), F32), sds((8, 128, 128), BF)],
        scratch_shapes=[pltpu.VMEM((GROUP, 128), F32)] * 2,
        compiler_params=params(56),
        cost_estimate=cost(17),
        name="attend_back",
    )(q0, q1, own.reshape(2, PLANE, 128), sib.reshape(2, PLANE, 128), o, l, g)


def heads_back_kernel(dq_ref, own_ref, got_ref, raw_ref, f_ref, g_ref, c_ref, sin_ref, bd_ref,
                      out_ref, scaled_ref, gain_ref):
    @pl.when(pl.program_id(0) == 0)
    def _():
        gain_ref[...] = jnp.zeros_like(gain_ref)

    rows = WIDE
    lane1 = lax.broadcasted_iota(jnp.int32, (rows, 128), 1)
    dq = dq_ref[...].reshape(2 * rows, 128) * HEAD**-0.5
    dq = jnp.where(lane1 < 64, dq[:rows], pltpu.roll(dq[rows:], 64, 1))
    dkv = own_ref[...] + got_ref[...].astype(F32)
    d = jnp.concatenate([dq, dkv.reshape(rows, 128)], 1)
    raw = raw_ref[...].reshape(rows, 256)
    lane = lax.broadcasted_iota(jnp.int32, (rows, 256), 1)
    bd = bd_ref[...]
    fac = jnp.where(lane < 192, lax.rsqrt(exact_sums(raw * raw, bd) + EPS_HEAD), 1.0)
    hat = raw * fac
    c, s = wide_tables(c_ref[...].reshape(rows, 128), sin_ref[...].reshape(rows, 128), lane)
    dh = d * c - half_turn(d * s, lane)
    gain_ref[...] += jnp.sum(dh * hat, axis=0, keepdims=True)
    dn = dh * g_ref[...]
    back = fac * (dn - hat * exact_sums(dn * hat, bd))
    res = jnp.where(lane < 192, back, d)
    out_ref[...] = res.astype(BF).reshape(4, 128, 256)
    scaled_ref[...] = (res * f_ref[...].reshape(rows, 1)).astype(BF).reshape(4, 128, 256)


def heads_back(dq, own, got, raw, f, gains, cos, sin):
    return pl.pallas_call(
        heads_back_kernel,
        grid=(2,),
        in_specs=[two_four(128, 128), four(128, 128), four(128, 128), four(128, 256), four(128, 1),
                  whole(1, 256), four(128, 128), four(128, 128), whole(256, 256)],
        out_specs=[four(128, 256), four(128, 256), whole(1, 256)],
        out_shape=[sds((8, 128, 256), BF), sds((8, 128, 256), BF), sds((1, 256), F32)],
        compiler_params=params(56),
        cost_estimate=cost(6),
        name="heads_back",
    )(dq, own, got, raw, f, gains, cos, sin, head_sums())


def norm_factor(v):
    return lax.rsqrt(jnp.mean(v * v, axis=1, keepdims=True) + EPS_WIDE)


def after_attention_kernel(s_ref, j_ref, *refs):
    own, sib = refs[0:4], refs[4]
    x_ref, g_ref, hidden_ref, middle_ref, w_ref = refs[5:]
    core, a, b = s_ref[0], s_ref[1], s_ref[2]
    for i, d in enumerate((1, 3, 2, 0)):
        for r in range(2):
            chip = ((a - d) & 3) * 2 + (b ^ (1 - r))
            at = chip * 128 + core * 64
            w_ref[pl.ds(pl.multiple_of(at, 64), 64), :] = own[i][r]
            at = chip * 128 + (1 - core) * 64
            w_ref[pl.ds(pl.multiple_of(at, 64), 64), :] = sib[i, r]
    hidden = x_ref[...].astype(F32)
    for j in range(8):
        hidden = hidden + dot(j_ref[j], w_ref[j * 128 : j * 128 + 128, :])
    hidden_ref[...] = hidden
    middle_ref[...] = (hidden * norm_factor(hidden) * g_ref[...]).astype(BF)


def after_attention(marks, joined, own, sib, x, gain):
    return pl.pallas_call(
        after_attention_kernel,
        grid_spec=pltpu.PrefetchScalarGridSpec(
            num_scalar_prefetch=1,
            grid=(1,),
            in_specs=[whole(8, 128, 128)] + [whole(2, 64, D)] * 4 + [whole(4, 2, 64, D), whole(128, D), whole(1, D)],
            out_specs=[whole(128, D), whole(128, D), whole(D, D)],
        ),
        out_shape=[sds((128, D), F32), sds((128, D), BF), sds((D, D), BF)],
        compiler_params=params(56),
        cost_estimate=cost(3),
        name="after_attention",
    )(marks, joined, *own, sib, x, gain)


def second_back_kernel(m_ref, hidden_ref, cot_ref, g_ref, w_ref, grad_ref, low_ref, joined_ref, gain_ref):
    mg = m_ref[0].astype(F32)
    for j in range(1, 8):
        mg = mg + m_ref[j].astype(F32)
    hidden = hidden_ref[...]
    f = norm_factor(hidden)
    hat = hidden * f
    gain_ref[...] = jnp.sum(mg * hat, axis=0, keepdims=True)
    dn = mg * g_ref[...]
    grad = cot_ref[...].astype(F32) + f * (dn - hat * jnp.mean(dn * hat, axis=1, keepdims=True))
    grad_ref[...] = grad
    low = grad.astype(BF)
    low_ref[...] = low
    joined = dot(low, w_ref[...], NT).astype(BF)
    for j in range(8):
        joined_ref[j] = joined[:, j * 128 : j * 128 + 128]


def second_back(chunks, hidden, cot, gain, w):
    return pl.pallas_call(
        second_back_kernel,
        out_shape=[sds((128, D), F32), sds((128, D), BF), sds((8, 128, 128), BF), sds((1, D), F32)],
        compiler_params=params(56),
        cost_estimate=cost(2),
        name="second_back",
    )(chunks, hidden, cot, gain, w)


def first_back_kernel(raw_ref, w_ref, x_ref, g_ref, grad_ref, out_ref):
    ng = dot(raw_ref[0], w_ref[0:256, :])
    for j in range(1, 8):
        ng = ng + dot(raw_ref[j], w_ref[j * 256 : j * 256 + 256, :])
    x = x_ref[...].astype(F32)
    f = norm_factor(x)
    hat = x * f
    dn = ng * g_ref[...]
    out_ref[...] = (grad_ref[...] + f * (dn - hat * jnp.mean(dn * hat, axis=1, keepdims=True))).astype(BF)


def first_back(raw, w, x, gain, grad):
    return pl.pallas_call(
        first_back_kernel,
        out_shape=sds((128, D), BF),
        compiler_params=params(56),
        cost_estimate=cost(2),
        name="first_back",
    )(raw, w, x, gain, grad)


def place_small_kernel(s_ref, p0, p1, p2, p3, g_ref, chip_ref, scaled_ref, qkv_ref, out_ref):
    core, a, b = s_ref[0], s_ref[3], s_ref[4]
    for ref, d in zip((p0, p1, p2, p3), (1, 3, 2, 0)):
        for r in range(2):
            at = pl.multiple_of((((a - d) & 3) * 2 + (b ^ (1 - r))) * 128, 128)
            v = ref[r]
            own, other = v[:, :128], v[:, 128:256]
            chip = jnp.where(core == 0, jnp.concatenate([own, other], 1), jnp.concatenate([other, own], 1))
            chip_ref[pl.ds(at, 128), :] = chip
            gain = jnp.broadcast_to(g_ref[:, pl.ds(at, 128)], (128, 128)).T
            gain = jnp.concatenate([gain, gain], 1)
            scaled_ref[pl.ds(at, 128), :] = (chip.astype(F32) * gain).astype(BF)
            qkv_ref[:, pl.ds(at, 128)] = own.astype(F32).T.astype(BF)
            out_ref[:, pl.ds(at, 128)] = v[:, 256:].astype(F32).T[:64].astype(BF)


def place_small(marks, pieces, gain):
    return pl.pallas_call(
        place_small_kernel,
        grid_spec=pltpu.PrefetchScalarGridSpec(
            num_scalar_prefetch=1,
            grid=(1,),
            in_specs=[whole(2, 128, 384)] * 4 + [whole(1, D)],
            out_specs=[whole(D, 256), whole(D, 256), whole(128, D), whole(64, D)],
        ),
        out_shape=[sds((D, 256), BF), sds((D, 256), BF), sds((128, D), BF), sds((64, D), BF)],
        compiler_params=params(56),
        cost_estimate=cost(2),
        name="place_small",
    )(marks, *pieces, gain)


def given_gates_kernel(s_ref, own_ref, sib_ref, inv_ref, out_ref, dealt):
    core, a, b = s_ref[0], s_ref[1], s_ref[2]
    row = lax.broadcasted_iota(jnp.int32, (8, 128), 0)
    for ref, side in ((own_ref, core), (sib_ref, 1 - core)):
        for i, d in enumerate((1, 3, 2, 0)):
            for r in range(2):
                ex = ref[i, r].astype(F32)
                names = ex[:8, 0:128]
                values = ex[:8, 128:256] + ex[:8, 256:384] + ex[:8, 384:512]
                both = jnp.zeros((8, 128), F32)
                for e in range(2):
                    mine = (s_ref[6] * 2 + e).astype(F32)
                    g = jnp.sum(jnp.where(names == mine, values, 0.0), axis=0, keepdims=True)
                    both = jnp.where(row == e, g, both)
                dealt[((a - d) & 3) * 4 + (b ^ (1 - r)) * 2 + side] = both
    for n in range(16):
        slot = jnp.broadcast_to(inv_ref[n : n + 1, :], (8, 128))
        at, of = slot & 127, slot >> 7
        got = jnp.zeros((8, 128), F32)
        for k in range(16):
            got = jnp.where(of == k, jnp.take_along_axis(dealt[k], at, axis=1), got)
        out_ref[n] = got


def given_gates(marks, own, sib, inverse):
    extra = pl.BlockSpec((4, 2, 16, D), lambda i, s: (0, 0, 8, 0))
    return pl.pallas_call(
        given_gates_kernel,
        grid_spec=pltpu.PrefetchScalarGridSpec(
            num_scalar_prefetch=1,
            grid=(1,),
            in_specs=[extra, extra, whole(16, 128)],
            out_specs=whole(16, 8, 128),
            scratch_shapes=[pltpu.VMEM((16, 8, 128), F32)],
        ),
        out_shape=sds((16, 8, 128), F32),
        compiler_params=params(56),
        cost_estimate=cost(2),
        name="given_gates",
    )(marks, own, sib, inverse)


def inner_kernel(own_ref, sib_ref, w_ref, po_ref, ps_ref, co_ref, cs_ref):
    w = w_ref[...]
    for ref, p_ref, c_ref in ((own_ref, po_ref, co_ref), (sib_ref, ps_ref, cs_ref)):
        up = ref[0, :, :128]
        c_ref[0] = up
        p_ref[0] = dot(up.reshape(256, D), w).astype(BF).reshape(2, 128, D)


def inner_products(own, sib, w):
    side = pl.BlockSpec((1, 2, 144, D), lambda i: (i, 0, 0, 0))
    spec = pl.BlockSpec((1, 2, 128, D), lambda i: (i, 0, 0, 0))
    return pl.pallas_call(
        inner_kernel,
        grid=(4,),
        in_specs=[side, side, pl.BlockSpec((D, 2 * FF), lambda i: (0, 2))],
        out_specs=[spec] * 4,
        out_shape=[sds((4, 2, 128, D), BF)] * 4,
        compiler_params=params(56),
        cost_estimate=cost(8),
        name="inner_products",
    )(own, sib, w)


def experts_kernel(s_ref, mid_ref, pre_ref, g_ref, w_ref, entry_ref, gg_ref, ug_ref, in_ref):
    mid = mid_ref[...].reshape(256, D)
    b = s_ref[2]
    gates = jnp.concatenate([g_ref[0, b ^ 1, 0].T, g_ref[0, b, 0].T], 0)
    entry = None
    for e in range(2):
        cg = slice(e * FF, e * FF + FF)
        cu = slice(1024 + e * FF, 1024 + e * FF + FF)
        gp = dot(mid, w_ref[:, cg])
        u = dot(mid, w_ref[:, cu])
        g = gates[:, e : e + 1]
        ig = pre_ref[0, :, :, cg].reshape(256, FF).astype(F32) * g
        sig = 0.5 * jnp.tanh(0.5 * gp) + 0.5
        act = gp * sig
        inner = (g * act * u).astype(BF)
        gg = (ig * u * (sig + act * (1.0 - sig))).astype(BF)
        ug = (ig * act).astype(BF)
        part = dot(gg, w_ref[:, cg], NT) + dot(ug, w_ref[:, cu], NT)
        entry = part if entry is None else entry + part
        for ref, v in ((in_ref, inner), (gg_ref, gg), (ug_ref, ug)):
            ref[0, :, :, cg] = v.reshape(2, 128, FF)
    entry = entry.astype(BF)
    entry_ref[0, b ^ 1] = entry[:128]
    entry_ref[0, b] = entry[128:]


def run_experts(marks, which, mid, pre, gates, w):
    hid = pl.BlockSpec((1, 2, 128, D), lambda i, s: (i, 0, 0, 0))
    return pl.pallas_call(
        experts_kernel,
        grid_spec=pltpu.PrefetchScalarGridSpec(
            num_scalar_prefetch=1,
            grid=(4,),
            in_specs=[hid, hid, pl.BlockSpec((1, 2, 1, 8, 128), lambda i, s: (s[16 + i], 0, s[which], 0, 0)),
                      whole(D, 4 * FF)],
            out_specs=[pl.BlockSpec((1, 2, 128, D), lambda i, s: (s[16 + i], 0, 0, 0))] + [hid] * 3,
        ),
        out_shape=[sds((4, 2, 128, D), BF)] * 4,
        compiler_params=params(56),
        cost_estimate=cost(14),
        name="run_experts",
    )(marks, mid, pre, gates, w)


def add_pair_kernel(a_ref, b_ref, out_ref):
    out_ref[...] = (a_ref[...].astype(F32) + b_ref[...].astype(F32)).astype(BF)


def add_pair(a, b):
    spec = pl.BlockSpec((2, 128, D), lambda i: (i, 0, 0))
    return pl.pallas_call(
        add_pair_kernel,
        grid=(4,),
        in_specs=[spec, spec],
        out_specs=spec,
        out_shape=sds((8, 128, D), BF),
        compiler_params=params(8),
        cost_estimate=cost(2),
        name="add_pair",
    )(a.reshape(8, 128, D), b.reshape(8, 128, D))


def results_kernel(s_ref, in_ref, w_ref, *refs):
    b = s_ref[2]
    o = dot(in_ref[...].reshape(256, 2 * FF), w_ref[...], NT)
    for r in range(2):
        at = b ^ (1 - r)
        v = o[r * 128 : r * 128 + 128]
        if len(refs) == 2:
            v = v + refs[0][0, at].astype(F32)
        refs[-1][0, at] = v.astype(BF)


def results(marks, inner, w, got=None):
    hid = pl.BlockSpec((1, 2, 128, 2 * FF), lambda i, s: (i, 0, 0, 0))
    there = pl.BlockSpec((1, 2, 128, D), lambda i, s: (s[16 + i], 0, 0, 0))
    more = [] if got is None else [got]
    return pl.pallas_call(
        results_kernel,
        grid_spec=pltpu.PrefetchScalarGridSpec(
            num_scalar_prefetch=1,
            grid=(4,),
            in_specs=[hid, pl.BlockSpec((D, 2 * FF), lambda i, s: (0, 2))] + [there] * len(more),
            out_specs=there,
        ),
        out_shape=sds((4, 2, 128, D), BF),
        compiler_params=params(56),
        cost_estimate=cost(4),
        name="results",
    )(marks, inner, w, *more)


def add_up_kernel(h_ref, m_ref, out_ref):
    t = h_ref[...]
    for j in range(8):
        t = t + m_ref[j].astype(F32)
    out_ref[...] = t.astype(BF)


def add_up(hidden, chunks):
    return pl.pallas_call(
        add_up_kernel,
        out_shape=sds((128, D), BF),
        compiler_params=params(8),
        cost_estimate=cost(2),
        name="add_up",
    )(hidden, chunks)


def weights_kernel(*refs):
    out_ref = refs[-1]
    for n in range(len(refs) // 4):
        l0, l1, r0, r1 = refs[4 * n : 4 * n + 4]
        o = dot(l0[...].reshape(PLANE, 256), r0[...].reshape(PLANE, 1024), TN)
        o = o + dot(l1[...].reshape(PLANE, 256), r1[...].reshape(PLANE, 1024), TN)
        out_ref[:, n * 1024 : n * 1024 + 1024] = o.astype(BF)


def weight_grads(*sides):
    side = pl.BlockSpec((4, 2, 128, 256), lambda i: (0, 0, 0, i))
    hid = whole(4, 2, 128, 2 * FF)
    n = len(sides)
    return pl.pallas_call(
        weights_kernel,
        grid=(4,),
        in_specs=[side, side, hid, hid] * n,
        out_specs=pl.BlockSpec((256, n * 2 * FF), lambda i: (i, 0)),
        out_shape=sds((D, n * 2 * FF), BF),
        compiler_params=params(56),
        cost_estimate=cost(8 * n),
        name="weight_grads",
    )(*[v for left, right in sides for v in (*left, *right)])


def unpack_kernel(a_ref, g_ref, u_ref, d_ref):
    t = a_ref[...].astype(F32)
    for e in range(2):
        at = e * FF
        g_ref[:, e, :] = t[:, at : at + FF]
        u_ref[:, e, :] = t[:, 1024 + at : 1024 + at + FF]
        d_ref[:, e, :] = t[:, 2048 + at : 2048 + at + FF]


def unpack(*parts):
    return pl.pallas_call(
        unpack_kernel,
        out_shape=[sds((128, 2, FF), F32)] * 3,
        compiler_params=params(12),
        cost_estimate=cost(2),
        name="unpack",
    )(*parts)


def qkv_grads_kernel(s_ref, x0, x1, x2, x3, r_ref, w_ref, g_ref, second_ref, heads_ref,
                     own_ref, other_ref, gains_ref):
    core = s_ref[0]
    i = pl.program_id(0)

    @pl.when(i == 0)
    def _():
        gains_ref[...] = jnp.zeros_like(gains_ref)
        gains_ref[8:9, :] = heads_ref[...]

    gains_ref[pl.ds(4 + i, 1), :] = second_ref[...]
    a, b = s_ref[1], s_ref[2]
    o = jnp.zeros((256, 256), F32)
    for ref, d in zip((x0, x1, x2, x3), (1, 3, 2, 0)):
        at = ((a - d) & 3) * 2
        both = jnp.concatenate([r_ref[at + (b ^ 1)], r_ref[at + b]], 0)
        o = o + dot(ref[...].reshape(256, 256), both, TN)
    first = jnp.sum(o * w_ref[...].astype(F32), axis=1, keepdims=True)
    gains_ref[pl.ds(i, 1), :] = jnp.broadcast_to(first, (256, 128)).T[:1]
    o = o * g_ref[...]
    own_ref[...] = jnp.where(core == 0, o[:, :128], o[:, 128:])
    other_ref[...] = jnp.where(core == 0, o[:, 128:], o[:, :128]).astype(BF)


def qkv_grads(marks, x, r, w, gain, second, heads):
    rows = lambda m: pl.BlockSpec((256, m), lambda i, s: (i, 0))
    return pl.pallas_call(
        qkv_grads_kernel,
        grid_spec=pltpu.PrefetchScalarGridSpec(
            num_scalar_prefetch=1,
            grid=(4,),
            in_specs=[pl.BlockSpec((2, 128, 256), lambda i, s: (0, 0, i))] * 4 + [whole(8, 128, 256),
                      rows(256), rows(1), pl.BlockSpec((1, 256), lambda i, s: (0, i)), whole(1, 256)],
            out_specs=[rows(128), rows(128), whole(16, 256)],
        ),
        out_shape=[sds((D, 128), F32), sds((D, 128), BF), sds((16, 256), F32)],
        compiler_params=params(56),
        cost_estimate=cost(4),
        name="qkv_grads",
    )(marks, *x, r, w, gain, second, heads)


def write_gains(ref, at, gains):
    for k, part in enumerate(three(gains)):
        ref[at + 16 * k : at + 16 * k + 16, :] = part.astype(BF)


def read_gains(ref, at):
    g = ref[at : at + 16, :].astype(F32) + ref[at + 16 : at + 32, :].astype(F32)
    return g + ref[at + 32 : at + 48, :].astype(F32)


def out_grads_kernel(s_ref, h0, h1, h2, h3, j_ref, own_ref, other_ref):
    core, a, b = s_ref[0], s_ref[1], s_ref[2]
    acc = jnp.zeros((D, 128), F32)
    for ref, d in zip((h0, h1, h2, h3), (1, 3, 2, 0)):
        at = ((a - d) & 3) * 2
        both = jnp.concatenate([j_ref[at + (b ^ 1)], j_ref[at + b]], 0)
        acc = acc + dot(ref[...].reshape(256, D), both, TN)
    swapped = pltpu.roll(acc, 64, 1)
    low = lax.broadcasted_iota(jnp.int32, (D, 128), 1) < 64
    own_ref[...] = jnp.where(low, jnp.where(core == 0, acc, swapped), 0.0)
    other_ref[...] = jnp.where(low, jnp.where(core == 0, swapped, acc), 0.0).astype(BF)


def out_grads(marks, pieces, joined):
    return pl.pallas_call(
        out_grads_kernel,
        grid_spec=pltpu.PrefetchScalarGridSpec(
            num_scalar_prefetch=1,
            grid=(1,),
            in_specs=[whole(2, 128, D)] * 4 + [whole(8, 128, 128)],
            out_specs=[whole(D, 128), whole(D, 128)],
        ),
        out_shape=[sds((D, 128), F32), sds((D, 128), BF)],
        compiler_params=params(56),
        cost_estimate=cost(3),
        name="out_grads",
    )(marks, *pieces, joined)


def ring_parts_kernel(s_ref, q_ref, o_ref, gains_ref, got_ref, keep_ref, m1, m3, m2):
    a, b = s_ref[3], s_ref[4]

    def rows(chunk):
        at = pl.ds(pl.multiple_of(chunk * 128, 128), 128)
        return jnp.concatenate([q_ref[at, :], o_ref[at, :]], 1) + got_ref[at, :].astype(F32)

    gains = gains_ref[...]
    for d, ref in ((1, m1), (3, m3), (2, m2)):
        at = ((a + d) & 3) * 2
        ref[:128, :] = rows(at + (b ^ 1)).astype(BF)
        ref[128:256, :] = rows(at + b).astype(BF)
        write_gains(ref, 256, gains)
    at = a * 2
    keep_ref[0] = rows(at + (b ^ 1))
    keep_ref[1] = rows(at + b)


def ring_parts(marks, own_q, own_o, gains, got):
    return pl.pallas_call(
        ring_parts_kernel,
        grid_spec=pltpu.PrefetchScalarGridSpec(
            num_scalar_prefetch=1,
            grid=(1,),
            in_specs=[whole(D, 128), whole(D, 128), whole(16, 256), whole(D, 256)],
            out_specs=[whole(2, 128, 256)] + [whole(304, 256)] * 3,
        ),
        out_shape=[sds((2, 128, 256), F32)] + [sds((304, 256), BF)] * 3,
        compiler_params=params(56),
        cost_estimate=cost(2),
        name="ring_parts",
    )(marks, own_q, own_o, gains, got)


def pair_parts_kernel(keep_ref, gains_ref, m1, m3, m2, own_ref, out_ref, msg_ref):
    other, own = keep_ref[0], keep_ref[1]
    gains = gains_ref[...]
    for ref in (m1, m3, m2):
        other = other + ref[:128, :].astype(F32)
        own = own + ref[128:256, :].astype(F32)
        gains = gains + read_gains(ref, 256)
    own_ref[...] = own
    out_ref[...] = gains
    msg_ref[:128, :] = other.astype(BF)
    write_gains(msg_ref, 128, gains)


def pair_parts(keep, gains, got):
    return pl.pallas_call(
        pair_parts_kernel,
        out_shape=[sds((128, 256), F32), sds((16, 256), F32), sds((176, 256), BF)],
        compiler_params=params(56),
        cost_estimate=cost(2),
        name="pair_parts",
    )(keep, gains, *got)


def last_parts_kernel(own_ref, gains_ref, got_ref, qkv_ref, out_ref, sum_ref):
    t = own_ref[...] + got_ref[:128, :].astype(F32)
    sum_ref[...] = gains_ref[...] + read_gains(got_ref, 128)
    qkv_ref[...] = t[:, :128]
    out_ref[...] = t[:, 128:192]


def last_parts(own, gains, got):
    return pl.pallas_call(
        last_parts_kernel,
        out_shape=[sds((128, 128), F32), sds((128, 64), F32), sds((16, 256), F32)],
        compiler_params=params(56),
        cost_estimate=cost(2),
        name="last_parts",
    )(own, gains, got)


def body(tokens, cotangent, deal_order, lengths, routes, route_gates, gain_first, gain_second, gain_query, gain_key,
         weight_qkv, weight_out, weight_gate, weight_up, weight_down):
    col = lax.axis_index("col")
    core = col % 2
    a, b = place("col")
    ra, rb = place("row")
    order = [(a + d) % 4 for d in (1, 3, 2, 0)]
    row_order = [(ra + d) % 4 for d in (1, 3, 2, 0)]
    back = [(a - d) % 4 for d in (1, 3, 2, 0)]
    marks = jnp.stack([core, a, b, ra, rb, 1 - core, col, core] + order + row_order + back).astype(jnp.int32)
    planes = [[i for i in range(16) if i % 2 == k] for k in range(2)]
    swap_all = partial(lax.all_to_all, axis_name="col", split_axis=0, concat_axis=0, tiled=True,
                       axis_index_groups=planes)

    extra = jnp.concatenate([routes.T.astype(BF)] + [p.T.astype(BF) for p in three(route_gates)], 1)
    cot = jnp.concatenate([cotangent, jnp.pad(extra, ((0, 8), (0, 512)))], 0)
    wide = jnp.concatenate([w.reshape(128, 2 * FF) for w in (weight_gate, weight_up, weight_down)], 1).astype(BF)

    qkv_low = weight_qkv.astype(BF)
    near, qkv_pair, wide, cot = together(step_pair(tokens, "col"), step_core(qkv_low), wide, cot)
    small = jnp.concatenate([qkv_low, qkv_pair, weight_out.astype(BF), jnp.zeros((128, 64), BF)], 1)
    small_pair = step_pair(small, "row")
    cot_near = step_pair(cot, "col")
    x_pieces = gather_rest(near, tokens, "col")
    w_all = lax.all_gather(wide, "row", axis=0, tiled=True)
    w_chip, w_scaled, qkv_t, out_t = place_small(marks, gather_rest(small_pair, small, "row"), gain_first[None])
    out_near = step_pair(out_t, "col")

    inverse, segment, offset = places(marks, lengths, deal_order.reshape(16, 128))
    frequency = THETA ** (-(jnp.arange(128) % 32).astype(F32) * 2.0 / HEAD)
    angles = offset * frequency[None, None, :]
    cos, sin = jnp.cos(angles), jnp.sin(angles)
    gains = jnp.concatenate([gain_query, gain_query, gain_key, jnp.ones((HEAD,), F32)])[None, :]

    out_near, w_scaled, cos, sin, segment, *x_pieces = together(out_near, w_scaled, cos, sin, segment, *x_pieces)
    both = gather_rest(jnp.concatenate([cot_near, out_near], 0), jnp.concatenate([cot, out_t], 0), "col")
    q0, q1, kv, raw, f1_all = project_heads(
        marks, x_pieces, w_scaled, gains, cos, sin, segment)
    kv_sib = step_core(kv)
    joined, logs = attend(q0, q1, kv, kv_sib)
    joined_got = swap_all(joined)
    joined_got, *both = together(joined_got, *both)
    out_own = [v[:, 144:] for v in both]
    out_sib = step_core(jnp.stack(out_own))
    hidden, middle, wout_t = after_attention(marks, joined_got, out_own, out_sib, tokens, gain_second[None])
    mid_pair = step_pair(middle, "col")
    hidden, *both = together(hidden, *both)
    cot_own = jnp.stack([v[:, :144] for v in both])
    cot_sib = step_core(cot_own)
    gates = given_gates(marks, cot_own, cot_sib, inverse).reshape(4, 2, 2, 8, 128)
    pre0, pre1, cot0, cot1 = inner_products(cot_own, cot_sib, w_all)
    mid_pieces = gather_rest(mid_pair, middle, "col")
    gates, pre0, *mid_pieces = together(gates, pre0, *mid_pieces)
    mid0 = jnp.stack(mid_pieces)
    mid1 = step_core(mid0)
    qkv_t, mid0 = together(qkv_t, mid0)
    wqkv_t = lax.all_gather(qkv_t, "col", axis=0, tiled=True)

    e_own, gg0, ug0, in0 = run_experts(marks, 0, mid0, pre0, gates, w_all)
    e_own, mid1 = together(e_own, mid1)
    e_other, gg1, ug1, in1 = run_experts(marks, 5, mid1, pre1, gates, w_all)
    r_other = results(marks, in1, w_all)
    entry = add_pair(e_own, step_core(e_other))
    entry, gg0 = together(entry, gg0)
    entry_got = swap_all(entry)
    grads = weight_grads(((mid0, mid1), (gg0, gg1)), ((mid0, mid1), (ug0, ug1)), ((cot0, cot1), (in0, in1)))
    in0, grads = together(in0, grads)
    r_sum = results(marks, in0, w_all, step_core(r_other)).reshape(8, 128, D)

    entry_got, grads, r_sum = together(entry_got, grads, r_sum)
    grads = lax.psum_scatter(grads, "row", scatter_dimension=0, tiled=True)
    hidden_grad, hidden_low, joined_grad, second = second_back(entry_got, hidden, cotangent, gain_second[None], wout_t)
    joined_grad = swap_all(joined_grad)
    hidden_pair = jnp.stack([step_pair(hidden_low, "col"), hidden_low])
    joined_grad, r_sum, hidden_pair = together(joined_grad, r_sum, hidden_pair)
    hidden_pieces = [step_ring(hidden_pair, "col", d) for d in AHEAD] + [hidden_pair]
    dq, dkv_own, dkv_other = attend_back(q0, q1, kv, kv_sib, joined, logs, joined_grad)
    dkv_got = step_core(dkv_other)
    dq, *hidden_pieces = together(dq, *hidden_pieces)
    raw_grad, raw_scaled, gain_heads = heads_back(dq, dkv_own, dkv_got, raw, f1_all, gains, cos, sin)
    raw_got = swap_all(raw_grad)
    own_o, other_o = out_grads(marks, hidden_pieces, joined)
    own_q, other_q, sums = qkv_grads(
        marks, x_pieces, raw_scaled, w_chip, gain_first[:, None], second, gain_heads)
    for n in (0, 1, 2, 3):
        sums = sums + lax.ppermute(sums, "col", [(i, i ^ (1 << n)) for i in range(16)])
    raw_got, sums, r_sum = together(raw_got, sums, r_sum)
    out_got = swap_all(r_sum)
    msg = jnp.concatenate([other_q, other_o], 1)
    keep, *msgs = ring_parts(marks, own_q, own_o, sums, step_core(msg))
    input_grad = first_back(raw_got, wqkv_t, tokens, gain_first[None], hidden_grad)
    block_out = add_up(hidden, out_got)
    keep, input_grad, *msgs = together(
        keep, input_grad, *[step_ring(m, "row", d) for m, d in zip(msgs, AHEAD)])
    own, sums, msg = pair_parts(keep, sums, msgs)
    grad_qkv, grad_out, sums = last_parts(own, sums, step_pair(msg, "row"))

    grads_w = unpack(grads)
    heads = sums[8]
    return (
        block_out,
        input_grad,
        sums[:4].reshape(-1),
        sums[4:8].reshape(-1),
        heads[:64] + heads[64:128],
        heads[128:192],
        grad_qkv,
        grad_out,
        *grads_w,
    )


def solution(mesh):
    both = P(("row", "col"), None)
    return jax.shard_map(
        body,
        mesh=mesh,
        in_specs=(both, both, P("row", None), P("row", None), both, both, P(), P(), P(), P(),
                  P("row", "col"), P("row", "col"), P("row", "col", None), P("row", "col", None),
                  P("row", "col", None)),
        out_specs=(both, both, P(), P(), P(), P(), P("row", "col"), P("row", "col"), P("row", "col", None),
                   P("row", "col", None), P("row", "col", None)),
        check_vma=False,
    )
```

```python
from functools import partial

import jax
import jax.numpy as jnp
import numpy as np
from jax import lax
from jax.experimental import pallas as pl
from jax.experimental.pallas import tpu as pltpu
from jax.sharding import PartitionSpec as P

D = 1024
HEAD = 64
EXPERTS = 32
FF = 512
TOP = 8
TOK = 128
GROUP = 2048
PLANE = 1024
EPS_WIDE = 1e-05
EPS_HEAD = 1e-06
THETA = 10000.0
LOG2E = 1.4426950408889634
LN2 = 0.6931471805599453
QSCALE = LOG2E * HEAD**-0.5
APART = -256.0
BF = jnp.bfloat16
F32 = jnp.float32
NT = (((1,), (1,)), ((), ()))
TN = (((0,), (0,)), ((), ()))
HIGH = lax.Precision.HIGHEST


def params(mib=56):
    return pltpu.CompilerParams(vmem_limit_bytes=mib * 2**20)


def cost(us, scale=0.02):
    us = us * scale
    return pl.CostEstimate(flops=int(us * 1e9), bytes_accessed=int(us * 1e6), transcendentals=0)


def dot(a, b, dims=None):
    if dims is None:
        dims = (((1,), (0,)), ((), ()))
    return lax.dot_general(a, b, dims, preferred_element_type=F32)


def sds(shape, kind):
    return jax.ShapeDtypeStruct(shape, kind)


def whole(*shape):
    return pl.BlockSpec(shape, lambda *_: (0,) * len(shape))


def together(*values):
    return lax.optimization_barrier(values)


AHEAD = (1, 3, 2)


def step_pair(v, axis):
    if axis == "row":
        route = [(i, i ^ 1) for i in range(8)]
    else:
        route = [(i, i ^ 2) for i in range(16)]
    return lax.ppermute(v, axis, route)


def step_ring(v, axis, d):
    if axis == "row":
        route = [(i, (i + 2 * d) % 8) for i in range(8)]
    else:
        route = [(i, (i + 4 * d) % 16) for i in range(16)]
    return lax.ppermute(v, axis, route)


def step_core(v):
    return lax.ppermute(v, "col", [(i, i ^ 1) for i in range(16)])


def place(axis):
    i = lax.axis_index(axis)
    if axis == "col":
        i = i // 2
    return i // 2, i % 2


def gather_rest(pair, v, axis):
    pair = jnp.stack([pair, v])
    return [step_ring(pair, axis, d) for d in AHEAD] + [pair]


def gather_plain(v, axis):
    return gather_rest(step_pair(v, axis), v, axis)


def added(terms):
    t = terms[0].astype(F32)
    for r in terms[1:]:
        t = t + r.astype(F32)
    return t


def places_kernel(s_ref, l_ref, deal_ref, inv_ref, seg_ref, off_ref):
    core = s_ref[0]
    row = lax.broadcasted_iota(jnp.int32, (128, 128), 0)
    lane = lax.broadcasted_iota(jnp.int32, (128, 128), 1)
    ends = [l_ref[0, 0]]
    for n in range(1, 4):
        ends.append(ends[-1] + l_ref[0, n])
    for k in range(16):
        found = jnp.zeros((128, 128), jnp.int32)
        for n in range(16):
            deal = jnp.broadcast_to(deal_ref[n : n + 1, :], (128, 128))
            found = jnp.where(deal == row + k * 128, lane + n * 128, found)
        slot = jnp.sum(found.astype(F32), axis=1, keepdims=True)
        inv_ref[k : k + 1, :] = jnp.broadcast_to(slot, (128, 128)).T[:1].astype(jnp.int32)
        slot = slot.astype(jnp.int32)
        seg = jnp.zeros((128, 1), jnp.int32)
        start = jnp.zeros((128, 1), jnp.int32)
        for end in ends:
            seg = seg + jnp.where(slot >= end, 1, 0)
            start = jnp.where(slot >= end, end, start)

        @pl.when(core == k % 2)
        def _():
            seg_ref[k // 2] = seg
            off_ref[k // 2] = (slot - start).astype(F32)


def places(marks, lengths, deal):
    return pl.pallas_call(
        places_kernel,
        grid_spec=pltpu.PrefetchScalarGridSpec(
            num_scalar_prefetch=2,
            grid=(1,),
            in_specs=[whole(16, 128)],
            out_specs=[whole(16, 128), whole(8, 128, 1), whole(8, 128, 1)],
        ),
        out_shape=[sds((16, 128), jnp.int32), sds((8, 128, 1), jnp.int32), sds((8, 128, 1), F32)],
        compiler_params=params(56),
        cost_estimate=cost(3),
        name="places",
    )(marks, lengths, deal)


def head_sums():
    i = np.arange(256) // HEAD
    return jnp.asarray((i[:, None] == i[None, :]) / HEAD, BF)


def spread():
    s = np.zeros((256, 512), np.float32)
    for h in range(4):
        for i in range(64):
            s[h * 64 + i, h * 128 + i] = 1.0
    return jnp.asarray(s, BF)


def exact_sums(v, sums):
    hi = v.astype(BF)
    lo = (v - hi.astype(F32)).astype(BF)
    return dot(hi, sums) + dot(lo, sums)


def half_turn(v, lane):
    back = jnp.concatenate([pltpu.roll(v[:, :128], 96, 1), pltpu.roll(v[:, 128:], 96, 1)], 1)
    ahead = jnp.concatenate([pltpu.roll(v[:, :128], 32, 1), pltpu.roll(v[:, 128:], 32, 1)], 1)
    return jnp.where(lane % 64 < 32, -back, ahead)


def wide_tables(c, s, lane):
    c = jnp.where(lane < 192, jnp.concatenate([c, c], 1), 1.0)
    s = jnp.where(lane < 192, jnp.concatenate([s, s], 1), 0.0)
    return c, s


def heads_kernel(s_ref, x0, x1, x2, x3, w_ref, g_ref, c_ref, s_tab_ref, seg_ref, bd_ref, sp_ref,
                 q0_ref, q1_ref, kv_ref, raw_ref, f_ref):
    a, b = s_ref[1], s_ref[2]
    lane = lax.broadcasted_iota(jnp.int32, (256, 256), 1)
    l1 = lax.broadcasted_iota(jnp.int32, (256, 128), 1)
    inseg = (l1 >= 64) & (l1 < 68)
    aug_v = jnp.where((l1 >= 64) & (l1 < 67), 1.0, 0.0)
    for ref, d in zip((x0, x1, x2, x3), (1, 3, 2, 0)):
        at = ((a - d) & 3) * 2
        blocks = (at + (b ^ 1), at + b)

        def both(r):
            return jnp.concatenate([r[blocks[0]], r[blocks[1]]], 0)

        def put(r, v):
            r[blocks[0]] = v[:128]
            r[blocks[1]] = v[128:]

        x = ref[...].reshape(256, D)
        xf = x.astype(F32)
        f = lax.rsqrt(jnp.mean(xf * xf, axis=1, keepdims=True) + EPS_WIDE)
        raw = dot(x, w_ref[...]) * f
        put(raw_ref, raw)
        put(f_ref, f)
        fac = jnp.where(lane < 192, lax.rsqrt(exact_sums(raw * raw, bd_ref[...]) + EPS_HEAD), 1.0)
        h = raw * fac * g_ref[...]
        c, s = wide_tables(both(c_ref), both(s_tab_ref), lane)
        t = h * c + half_turn(h, lane) * s
        t = jnp.where(lane < 128, t * QSCALE, t).astype(BF)
        wide = dot(t, sp_ref[...])
        same = (l1 - 64) == both(seg_ref)
        aug_q = jnp.where(inseg & jnp.logical_not(same), APART, 0.0)
        aug_k = jnp.where((inseg & same) | ((l1 >= 68) & (l1 < 71)), 1.0, 0.0)
        put(q0_ref, (wide[:, 0:128] + aug_q).astype(BF))
        put(q1_ref, (wide[:, 128:256] + aug_q).astype(BF))
        put(kv_ref.at[0], (wide[:, 256:384] + aug_k).astype(BF))
        put(kv_ref.at[1], (wide[:, 384:512] + aug_v).astype(BF))


def project_heads(marks, pieces, w, gains, cos, sin, seg):
    return pl.pallas_call(
        heads_kernel,
        grid_spec=pltpu.PrefetchScalarGridSpec(
            num_scalar_prefetch=1,
            grid=(1,),
            in_specs=[whole(2, 128, D)] * 4 + [whole(D, 256), whole(1, 256), whole(8, 128, 128), whole(8, 128, 128),
                                               whole(8, 128, 1), whole(256, 256), whole(256, 512)],
            out_specs=[whole(8, 128, 128)] * 2 + [whole(2, 8, 128, 128), whole(8, 128, 256), whole(8, 128, 1)],
        ),
        out_shape=[sds((8, 128, 128), BF)] * 2 + [sds((2, 8, 128, 128), BF), sds((8, 128, 256), F32),
                                                  sds((8, 128, 1), F32)],
        compiler_params=params(56),
        cost_estimate=cost(7),
        name="project_heads",
    )(marks, *pieces, w, gains, cos, sin, seg, head_sums(), spread())


WIDE = 512


def attend_kernel(q0_ref, q1_ref, own_ref, sib_ref, o_ref, l_ref):
    q = jnp.concatenate([q0_ref[...].reshape(WIDE, 128), q1_ref[...].reshape(WIDE, 128)], 0)
    acc = jnp.zeros((128, 2 * WIDE), F32)
    for ref in (own_ref, sib_ref):
        p = jnp.exp2(dot(ref[0], q, NT)).astype(BF)
        acc = acc + dot(ref[1], p, TN)
    acc = acc.T
    total = acc[:, 64:65]
    o = acc / total
    l_ref[...] = jnp.log2(total).reshape(2, 4, 128, 1)
    lane = lax.broadcasted_iota(jnp.int32, (WIDE, 128), 1)
    o = jnp.where(lane < 64, o[:WIDE], pltpu.roll(o[WIDE:], 64, 1))
    o_ref[...] = o.astype(BF).reshape(4, 128, 128)


def four(n, m):
    return pl.BlockSpec((4, n, m), lambda j: (j, 0, 0))


def two_four(n, m):
    return pl.BlockSpec((2, 4, n, m), lambda j: (0, j, 0, 0))


def attend(q0, q1, own, sib):
    return pl.pallas_call(
        attend_kernel,
        grid=(2,),
        in_specs=[four(128, 128), four(128, 128), whole(2, PLANE, 128), whole(2, PLANE, 128)],
        out_specs=[four(128, 128), two_four(128, 1)],
        out_shape=[sds((8, 128, 128), BF), sds((2, 8, 128, 1), F32)],
        compiler_params=params(56),
        cost_estimate=cost(7),
        name="attend",
    )(q0, q1, own.reshape(2, PLANE, 128), sib.reshape(2, PLANE, 128))


def three(v):
    hi = v.astype(BF).astype(F32)
    mid = (v - hi).astype(BF).astype(F32)
    return hi, mid, v - hi - mid


def attend_back_kernel(q0_ref, q1_ref, kvo_ref, kvs_ref, o_ref, l_ref, g_ref,
                       dq_ref, own_ref, other_ref, dk_ref, dv_ref):
    @pl.when(pl.program_id(0) == 0)
    def _():
        dk_ref[...] = jnp.zeros_like(dk_ref)
        dv_ref[...] = jnp.zeros_like(dv_ref)

    lane = lax.broadcasted_iota(jnp.int32, (2 * WIDE, 128), 1)
    q = jnp.concatenate([q0_ref[...].reshape(WIDE, 128), q1_ref[...].reshape(WIDE, 128)], 0)
    h0, h1, h2 = three(l_ref[...].reshape(2 * WIDE, 1))
    ql = jnp.where(lane == 68, -h0, jnp.where(lane == 69, -h1, jnp.where(lane == 70, -h2, q.astype(F32))))
    ql = ql.astype(BF)
    g = g_ref[...].reshape(WIDE, 128).astype(F32)
    o = o_ref[...].reshape(WIDE, 128).astype(F32)
    g = jnp.concatenate([g, pltpu.roll(g, 64, 1)], 0)
    o = jnp.concatenate([o, pltpu.roll(o, 64, 1)], 0)
    g = jnp.where(lane < 64, g, 0.0)
    centre = jnp.sum(g * o, axis=1, keepdims=True)
    c0, c1, c2 = three(centre)
    gl = jnp.where(lane == 64, -c0, jnp.where(lane == 65, -c1, jnp.where(lane == 66, -c2, g)))
    gl = gl.astype(BF)
    gb = g.astype(BF)
    dq = jnp.zeros((128, 2 * WIDE), F32)
    for j in range(GROUP // WIDE):
        rows = pl.ds(j * WIDE, WIDE)
        ref = kvo_ref if j * WIDE < PLANE else kvs_ref
        part = pl.ds(j * WIDE % PLANE, WIDE)
        k = ref[0, part, :]
        pt = jnp.exp2(dot(k, ql, NT))
        ds = (pt * dot(ref[1, part, :], gl, NT)).astype(BF)
        dv_ref[rows, :] += dot(pt.astype(BF), gb)
        dk_ref[rows, :] += dot(ds, q)
        dq = dq + dot(k, ds, TN)
    dq_ref[...] = dq.T.reshape(2, 4, 128, 128)

    @pl.when(pl.program_id(0) == 1)
    def _():
        low = lax.broadcasted_iota(jnp.int32, (128, 128), 1) < 64

        def block(j):
            rows = pl.ds(j * 128, 128)
            return jnp.where(low, dk_ref[rows, :] * LN2, pltpu.roll(dv_ref[rows, :], 64, 1))

        for j in range(8):
            own_ref[j] = block(j)
            other_ref[j] = block(8 + j).astype(BF)


def attend_back(q0, q1, own, sib, o, l, g):
    kv = whole(2, PLANE, 128)
    return pl.pallas_call(
        attend_back_kernel,
        grid=(2,),
        in_specs=[four(128, 128), four(128, 128), kv, kv, four(128, 128), two_four(128, 1), four(128, 128)],
        out_specs=[two_four(128, 128), whole(8, 128, 128), whole(8, 128, 128)],
        out_shape=[sds((2, 8, 128, 128), F32), sds((8, 128, 128), F32), sds((8, 128, 128), BF)],
        scratch_shapes=[pltpu.VMEM((GROUP, 128), F32)] * 2,
        compiler_params=params(56),
        cost_estimate=cost(17),
        name="attend_back",
    )(q0, q1, own.reshape(2, PLANE, 128), sib.reshape(2, PLANE, 128), o, l, g)


def heads_back_kernel(dq_ref, own_ref, got_ref, raw_ref, f_ref, g_ref, c_ref, sin_ref, bd_ref,
                      out_ref, scaled_ref, gain_ref):
    @pl.when(pl.program_id(0) == 0)
    def _():
        gain_ref[...] = jnp.zeros_like(gain_ref)

    rows = WIDE
    lane1 = lax.broadcasted_iota(jnp.int32, (rows, 128), 1)
    dq = dq_ref[...].reshape(2 * rows, 128) * HEAD**-0.5
    dq = jnp.where(lane1 < 64, dq[:rows], pltpu.roll(dq[rows:], 64, 1))
    dkv = own_ref[...] + got_ref[...].astype(F32)
    d = jnp.concatenate([dq, dkv.reshape(rows, 128)], 1)
    raw = raw_ref[...].reshape(rows, 256)
    lane = lax.broadcasted_iota(jnp.int32, (rows, 256), 1)
    bd = bd_ref[...]
    fac = jnp.where(lane < 192, lax.rsqrt(exact_sums(raw * raw, bd) + EPS_HEAD), 1.0)
    hat = raw * fac
    c, s = wide_tables(c_ref[...].reshape(rows, 128), sin_ref[...].reshape(rows, 128), lane)
    dh = d * c - half_turn(d * s, lane)
    gain_ref[...] += jnp.sum(dh * hat, axis=0, keepdims=True)
    dn = dh * g_ref[...]
    back = fac * (dn - hat * exact_sums(dn * hat, bd))
    res = jnp.where(lane < 192, back, d)
    out_ref[:, :128] = res.astype(BF).reshape(4, 128, 256)
    scaled_ref[...] = (res * f_ref[...].reshape(rows, 1)).astype(BF).reshape(4, 128, 256)


def heads_back(dq, own, got, raw, f, gains, cos, sin):
    return pl.pallas_call(
        heads_back_kernel,
        grid=(2,),
        in_specs=[two_four(128, 128), four(128, 128), four(128, 128), four(128, 256), four(128, 1),
                  whole(1, 256), four(128, 128), four(128, 128), whole(256, 256)],
        out_specs=[four(128, 256), four(128, 256), whole(1, 256)],
        out_shape=[sds((8, 176, 256), BF), sds((8, 128, 256), BF), sds((1, 256), F32)],
        compiler_params=params(56),
        cost_estimate=cost(6),
        name="heads_back",
    )(dq, own, got, raw, f, gains, cos, sin, head_sums())


def norm_factor(v):
    return lax.rsqrt(jnp.mean(v * v, axis=1, keepdims=True) + EPS_WIDE)


def after_attention_kernel(s_ref, j_ref, *refs):
    own, sib = refs[0:4], refs[4]
    x_ref, g_ref, hidden_ref, middle_ref, w_ref = refs[5:]
    core, a, b = s_ref[0], s_ref[1], s_ref[2]
    for i, d in enumerate((1, 3, 2, 0)):
        for r in range(2):
            chip = ((a - d) & 3) * 2 + (b ^ (1 - r))
            at = chip * 128 + core * 64
            w_ref[pl.ds(pl.multiple_of(at, 64), 64), :] = own[i][r]
            at = chip * 128 + (1 - core) * 64
            w_ref[pl.ds(pl.multiple_of(at, 64), 64), :] = sib[i, r]
    hidden = x_ref[...].astype(F32)
    for j in range(8):
        hidden = hidden + dot(j_ref[j], w_ref[j * 128 : j * 128 + 128, :])
    hidden_ref[...] = hidden
    middle_ref[...] = (hidden * norm_factor(hidden) * g_ref[...]).astype(BF)


def after_attention(marks, joined, own, sib, x, gain):
    return pl.pallas_call(
        after_attention_kernel,
        grid_spec=pltpu.PrefetchScalarGridSpec(
            num_scalar_prefetch=1,
            grid=(1,),
            in_specs=[whole(8, 128, 128)] + [whole(2, 64, D)] * 4 + [whole(4, 2, 64, D), whole(128, D), whole(1, D)],
            out_specs=[whole(128, D), whole(128, D), whole(D, D)],
        ),
        out_shape=[sds((128, D), F32), sds((128, D), BF), sds((D, D), BF)],
        compiler_params=params(24),
        cost_estimate=cost(3),
        name="after_attention",
    )(marks, joined, *own, sib, x, gain)


def second_back_kernel(m_ref, hidden_ref, cot_ref, g_ref, w_ref, grad_ref, low_ref, joined_ref, gain_ref):
    mg = m_ref[0].astype(F32)
    for j in range(1, 8):
        mg = mg + m_ref[j].astype(F32)
    hidden = hidden_ref[...]
    f = norm_factor(hidden)
    hat = hidden * f
    gain_ref[...] = jnp.sum(mg * hat, axis=0, keepdims=True)
    dn = mg * g_ref[...]
    grad = cot_ref[...].astype(F32) + f * (dn - hat * jnp.mean(dn * hat, axis=1, keepdims=True))
    grad_ref[...] = grad
    low = grad.astype(BF)
    low_ref[...] = low
    joined = dot(low, w_ref[...], NT).astype(BF)
    for j in range(8):
        joined_ref[j] = joined[:, j * 128 : j * 128 + 128]


def second_back(chunks, hidden, cot, gain, w):
    return pl.pallas_call(
        second_back_kernel,
        out_shape=[sds((128, D), F32), sds((128, D), BF), sds((8, 128, 128), BF), sds((1, D), F32)],
        compiler_params=params(20),
        cost_estimate=cost(2),
        name="second_back",
    )(chunks, hidden, cot, gain, w)


def first_back_kernel(raw_ref, w_ref, x_ref, g_ref, grad_ref, out_ref):
    ng = dot(raw_ref[0, :128], w_ref[0:256, :])
    for j in range(1, 8):
        ng = ng + dot(raw_ref[j, :128], w_ref[j * 256 : j * 256 + 256, :])
    x = x_ref[...].astype(F32)
    f = norm_factor(x)
    hat = x * f
    dn = ng * g_ref[...]
    out_ref[...] = (grad_ref[...] + f * (dn - hat * jnp.mean(dn * hat, axis=1, keepdims=True))).astype(BF)


def first_back(raw, w, x, gain, grad):
    return pl.pallas_call(
        first_back_kernel,
        out_shape=sds((128, D), BF),
        compiler_params=params(24),
        cost_estimate=cost(2),
        name="first_back",
    )(raw, w, x, gain, grad)


def place_small_kernel(s_ref, p0, p1, p2, p3, g_ref, chip_ref, scaled_ref, qkv_ref, out_ref):
    core, a, b = s_ref[0], s_ref[3], s_ref[4]
    for ref, d in zip((p0, p1, p2, p3), (1, 3, 2, 0)):
        for r in range(2):
            at = pl.multiple_of((((a - d) & 3) * 2 + (b ^ (1 - r))) * 128, 128)
            v = ref[r]
            own, other = v[:, :128], v[:, 128:256]
            chip = jnp.where(core == 0, jnp.concatenate([own, other], 1), jnp.concatenate([other, own], 1))
            chip_ref[pl.ds(at, 128), :] = chip
            gain = jnp.broadcast_to(g_ref[:, pl.ds(at, 128)], (128, 128)).T
            gain = jnp.concatenate([gain, gain], 1)
            scaled_ref[pl.ds(at, 128), :] = (chip.astype(F32) * gain).astype(BF)
            qkv_ref[:, pl.ds(at, 128)] = own.astype(F32).T.astype(BF)
            out_ref[:, pl.ds(at, 128)] = v[:, 256:].astype(F32).T[:64].astype(BF)


def place_small(marks, pieces, gain):
    return pl.pallas_call(
        place_small_kernel,
        grid_spec=pltpu.PrefetchScalarGridSpec(
            num_scalar_prefetch=1,
            grid=(1,),
            in_specs=[whole(2, 128, 384)] * 4 + [whole(1, D)],
            out_specs=[whole(D, 256), whole(D, 256), whole(128, D), whole(64, D)],
        ),
        out_shape=[sds((D, 256), BF), sds((D, 256), BF), sds((128, D), BF), sds((64, D), BF)],
        compiler_params=params(56),
        cost_estimate=cost(2),
        name="place_small",
    )(marks, *pieces, gain)


def given_gates_kernel(s_ref, own_ref, sib_ref, inv_ref, out_ref, dealt):
    core, a, b = s_ref[0], s_ref[1], s_ref[2]
    row = lax.broadcasted_iota(jnp.int32, (8, 128), 0)
    for ref, side in ((own_ref, core), (sib_ref, 1 - core)):
        for i, d in enumerate((1, 3, 2, 0)):
            for r in range(2):
                ex = ref[i, r].astype(F32)
                names = ex[:8, 0:128]
                values = ex[:8, 128:256] + ex[:8, 256:384] + ex[:8, 384:512]
                both = jnp.zeros((8, 128), F32)
                for e in range(2):
                    mine = (s_ref[6] * 2 + e).astype(F32)
                    g = jnp.sum(jnp.where(names == mine, values, 0.0), axis=0, keepdims=True)
                    both = jnp.where(row == e, g, both)
                dealt[((a - d) & 3) * 4 + (b ^ (1 - r)) * 2 + side] = both
    for n in range(16):
        slot = jnp.broadcast_to(inv_ref[n : n + 1, :], (8, 128))
        at, of = slot & 127, slot >> 7
        got = jnp.zeros((8, 128), F32)
        for k in range(16):
            got = jnp.where(of == k, jnp.take_along_axis(dealt[k], at, axis=1), got)
        out_ref[n] = got


def given_gates(marks, own, sib, inverse):
    extra = pl.BlockSpec((4, 2, 16, D), lambda i, s: (0, 0, 8, 0))
    return pl.pallas_call(
        given_gates_kernel,
        grid_spec=pltpu.PrefetchScalarGridSpec(
            num_scalar_prefetch=1,
            grid=(1,),
            in_specs=[extra, extra, whole(16, 128)],
            out_specs=whole(16, 8, 128),
            scratch_shapes=[pltpu.VMEM((16, 8, 128), F32)],
        ),
        out_shape=sds((16, 8, 128), F32),
        compiler_params=params(56),
        cost_estimate=cost(2),
        name="given_gates",
    )(marks, own, sib, inverse)


def inner_kernel(own_ref, sib_ref, w_ref, po_ref, ps_ref, co_ref, cs_ref):
    w = w_ref[...]
    for ref, p_ref, c_ref in ((own_ref, po_ref, co_ref), (sib_ref, ps_ref, cs_ref)):
        up = ref[0, :, :128]
        c_ref[0] = up
        p_ref[0] = dot(up.reshape(256, D), w).astype(BF).reshape(2, 128, D)


def inner_products(own, sib, w):
    side = pl.BlockSpec((1, 2, 144, D), lambda i: (i, 0, 0, 0))
    spec = pl.BlockSpec((1, 2, 128, D), lambda i: (i, 0, 0, 0))
    return pl.pallas_call(
        inner_kernel,
        grid=(4,),
        in_specs=[side, side, pl.BlockSpec((D, 2 * FF), lambda i: (0, 2))],
        out_specs=[spec] * 4,
        out_shape=[sds((4, 2, 128, D), BF)] * 4,
        compiler_params=params(56),
        cost_estimate=cost(8),
        name="inner_products",
    )(own, sib, w)


def experts_kernel(s_ref, mid_ref, pre_ref, g_ref, w_ref, *refs):
    entry_ref, gg_ref, ug_ref, in_ref = refs[-4:]
    mid = mid_ref[...].reshape(256, D)
    b = s_ref[2]
    gates = jnp.concatenate([g_ref[0, b ^ 1, 0].T, g_ref[0, b, 0].T], 0)
    entry = None
    for e in range(2):
        cg = slice(e * FF, e * FF + FF)
        cu = slice(1024 + e * FF, 1024 + e * FF + FF)
        gp = dot(mid, w_ref[:, cg])
        u = dot(mid, w_ref[:, cu])
        g = gates[:, e : e + 1]
        ig = pre_ref[0, :, :, cg].reshape(256, FF).astype(F32) * g
        sig = 0.5 * jnp.tanh(0.5 * gp) + 0.5
        act = gp * sig
        inner = (g * act * u).astype(BF)
        gg = (ig * u * (sig + act * (1.0 - sig))).astype(BF)
        ug = (ig * act).astype(BF)
        part = dot(gg, w_ref[:, cg], NT) + dot(ug, w_ref[:, cu], NT)
        entry = part if entry is None else entry + part
        for ref, v in ((in_ref, inner), (gg_ref, gg), (ug_ref, ug)):
            ref[0, :, :, cg] = v.reshape(2, 128, FF)
    entry = entry.astype(BF)
    entry_ref[0, b ^ 1] = entry[:128]
    entry_ref[0, b] = entry[128:]


def run_experts(marks, which, mid, pre, gates, w, pick=lambda i: i, before=()):
    hid = pl.BlockSpec((1, 2, 128, D), lambda i, s: (pick(i), 0, 0, 0))
    n = mid.shape[0]
    return pl.pallas_call(
        experts_kernel,
        grid_spec=pltpu.PrefetchScalarGridSpec(
            num_scalar_prefetch=1,
            grid=(n,),
            in_specs=[pl.BlockSpec((1, 2, 128, D), lambda i, s: (i, 0, 0, 0)), hid,
                      pl.BlockSpec((1, 2, 1, 8, 128), lambda i, s: (s[16 + pick(i)], 0, s[which], 0, 0)),
                      whole(D, 4 * FF)] + [pl.BlockSpec(memory_space=pl.ANY)] * len(before),
            out_specs=[pl.BlockSpec((1, 2, 128, D), lambda i, s: (s[16 + pick(i)], 0, 0, 0))] + [hid] * 3,
        ),
        out_shape=[sds((4, 2, 128, D), BF)] * 4,
        input_output_aliases={5 + k: k for k in range(len(before))},
        compiler_params=params(56),
        cost_estimate=cost(4 * n),
        name="run_experts",
    )(marks, mid, pre, gates, w, *before)


def add_pair_kernel(a_ref, b_ref, out_ref):
    out_ref[...] = (a_ref[...].astype(F32) + b_ref[...].astype(F32)).astype(BF)


def add_pair(a, b):
    spec = pl.BlockSpec((2, 128, D), lambda i: (i, 0, 0))
    return pl.pallas_call(
        add_pair_kernel,
        grid=(4,),
        in_specs=[spec, spec],
        out_specs=spec,
        out_shape=sds((8, 128, D), BF),
        compiler_params=params(8),
        cost_estimate=cost(2),
        name="add_pair",
    )(a.reshape(8, 128, D), b.reshape(8, 128, D))


def results_kernel(s_ref, in_ref, w_ref, *refs):
    b = s_ref[2]
    o = dot(in_ref[...].reshape(256, 2 * FF), w_ref[...], NT)
    for r in range(2):
        at = b ^ (1 - r)
        v = o[r * 128 : r * 128 + 128]
        if len(refs) == 2:
            v = v + refs[0][0, at].astype(F32)
        refs[-1][0, at] = v.astype(BF)


def results(marks, inner, w, got=None):
    hid = pl.BlockSpec((1, 2, 128, 2 * FF), lambda i, s: (i, 0, 0, 0))
    there = pl.BlockSpec((1, 2, 128, D), lambda i, s: (s[16 + i], 0, 0, 0))
    more = [] if got is None else [got]
    return pl.pallas_call(
        results_kernel,
        grid_spec=pltpu.PrefetchScalarGridSpec(
            num_scalar_prefetch=1,
            grid=(4,),
            in_specs=[hid, pl.BlockSpec((D, 2 * FF), lambda i, s: (0, 2))] + [there] * len(more),
            out_specs=there,
        ),
        out_shape=sds((4, 2, 128, D), BF),
        compiler_params=params(56),
        cost_estimate=cost(4),
        name="results",
    )(marks, inner, w, *more)


def add_up_kernel(h_ref, m_ref, out_ref):
    t = h_ref[...]
    for j in range(8):
        t = t + m_ref[j].astype(F32)
    out_ref[...] = t.astype(BF)


def add_up(hidden, chunks):
    return pl.pallas_call(
        add_up_kernel,
        out_shape=sds((128, D), BF),
        compiler_params=params(8),
        cost_estimate=cost(2),
        name="add_up",
    )(hidden, chunks)


def weights_kernel(*refs):
    out_ref = refs[-1]
    for n in range(len(refs) // 4):
        l0, l1, r0, r1 = refs[4 * n : 4 * n + 4]
        o = dot(l0[...].reshape(PLANE, 256), r0[...].reshape(PLANE, 1024), TN)
        o = o + dot(l1[...].reshape(PLANE, 256), r1[...].reshape(PLANE, 1024), TN)
        out_ref[:, n * 1024 : n * 1024 + 1024] = o.astype(BF)


def weight_grads(*sides):
    side = pl.BlockSpec((4, 2, 128, 256), lambda i: (0, 0, 0, i))
    hid = whole(4, 2, 128, 2 * FF)
    n = len(sides)
    return pl.pallas_call(
        weights_kernel,
        grid=(4,),
        in_specs=[side, side, hid, hid] * n,
        out_specs=pl.BlockSpec((256, n * 2 * FF), lambda i: (i, 0)),
        out_shape=sds((D, n * 2 * FF), BF),
        compiler_params=params(56),
        cost_estimate=cost(8 * n),
        name="weight_grads",
    )(*[v for left, right in sides for v in (*left, *right)])


def unpack_kernel(a_ref, g_ref, u_ref, d_ref):
    t = a_ref[...].astype(F32)
    for e in range(2):
        at = e * FF
        g_ref[:, e, :] = t[:, at : at + FF]
        u_ref[:, e, :] = t[:, 1024 + at : 1024 + at + FF]
        d_ref[:, e, :] = t[:, 2048 + at : 2048 + at + FF]


def unpack(*parts):
    return pl.pallas_call(
        unpack_kernel,
        out_shape=[sds((128, 2, FF), F32)] * 3,
        compiler_params=params(12),
        cost_estimate=cost(2),
        name="unpack",
    )(*parts)


def qkv_grads_kernel(s_ref, x0, x1, x2, x3, r_ref, w_ref, g_ref, second_ref, heads_ref,
                     own_ref, other_ref, gains_ref):
    core = s_ref[0]
    i = pl.program_id(0)

    @pl.when(i == 0)
    def _():
        gains_ref[...] = jnp.zeros_like(gains_ref)
        gains_ref[8:9, :] = heads_ref[...]

    gains_ref[pl.ds(4 + i, 1), :] = second_ref[...]
    a, b = s_ref[1], s_ref[2]
    o = jnp.zeros((256, 256), F32)
    for ref, d in zip((x0, x1, x2, x3), (1, 3, 2, 0)):
        at = ((a - d) & 3) * 2
        both = jnp.concatenate([r_ref[at + (b ^ 1)], r_ref[at + b]], 0)
        o = o + dot(ref[...].reshape(256, 256), both, TN)
    first = jnp.sum(o * w_ref[...].astype(F32), axis=1, keepdims=True)
    gains_ref[pl.ds(i, 1), :] = jnp.broadcast_to(first, (256, 128)).T[:1]
    o = o * g_ref[...]
    own_ref[...] = jnp.where(core == 0, o[:, :128], o[:, 128:])
    other_ref[...] = jnp.where(core == 0, o[:, 128:], o[:, :128]).astype(BF)


def qkv_grads(marks, x, r, w, gain, second, heads):
    rows = lambda m: pl.BlockSpec((256, m), lambda i, s: (i, 0))
    return pl.pallas_call(
        qkv_grads_kernel,
        grid_spec=pltpu.PrefetchScalarGridSpec(
            num_scalar_prefetch=1,
            grid=(4,),
            in_specs=[pl.BlockSpec((2, 128, 256), lambda i, s: (0, 0, i))] * 4 + [whole(8, 128, 256),
                      rows(256), rows(1), pl.BlockSpec((1, 256), lambda i, s: (0, i)), whole(1, 256)],
            out_specs=[rows(128), rows(128), whole(16, 256)],
        ),
        out_shape=[sds((D, 128), F32), sds((D, 128), BF), sds((16, 256), F32)],
        compiler_params=params(56),
        cost_estimate=cost(4),
        name="qkv_grads",
    )(marks, *x, r, w, gain, second, heads)


def add_gains_kernel(own_ref, got_ref, raw_ref, out_ref):
    parts = three(own_ref[...] + got_ref[...])
    k = pl.program_id(0)
    part = jnp.where(k == 0, parts[0], jnp.where(k == 1, parts[1], parts[2]))
    for j in range(8):
        out_ref[j] = part.astype(BF)


def add_gains(own, got, raw):
    return pl.pallas_call(
        add_gains_kernel,
        grid=(3,),
        in_specs=[whole(16, 256), whole(16, 256), pl.BlockSpec(memory_space=pl.ANY)],
        out_specs=pl.BlockSpec((8, 16, 256), lambda i: (0, 8 + i, 0)),
        out_shape=sds((8, 176, 256), BF),
        input_output_aliases={2: 0},
        compiler_params=params(56),
        cost_estimate=cost(1),
        name="add_gains",
    )(own, got, raw)


def write_gains(ref, at, gains):
    for k, part in enumerate(three(gains)):
        ref[at + 16 * k : at + 16 * k + 16, :] = part.astype(BF)


def read_gains(ref, at):
    g = ref[at : at + 16, :].astype(F32) + ref[at + 16 : at + 32, :].astype(F32)
    return g + ref[at + 32 : at + 48, :].astype(F32)


def out_grads_kernel(s_ref, h0, h1, h2, h3, j_ref, own_ref, other_ref):
    core, a, b = s_ref[0], s_ref[1], s_ref[2]
    acc = jnp.zeros((D, 128), F32)
    for ref, d in zip((h0, h1, h2, h3), (1, 3, 2, 0)):
        at = ((a - d) & 3) * 2
        both = jnp.concatenate([j_ref[at + (b ^ 1)], j_ref[at + b]], 0)
        acc = acc + dot(ref[...].reshape(256, D), both, TN)
    swapped = pltpu.roll(acc, 64, 1)
    low = lax.broadcasted_iota(jnp.int32, (D, 128), 1) < 64
    own_ref[...] = jnp.where(low, jnp.where(core == 0, acc, swapped), 0.0)
    other_ref[...] = jnp.where(low, jnp.where(core == 0, swapped, acc), 0.0).astype(BF)


def out_grads(marks, pieces, joined):
    return pl.pallas_call(
        out_grads_kernel,
        grid_spec=pltpu.PrefetchScalarGridSpec(
            num_scalar_prefetch=1,
            grid=(1,),
            in_specs=[whole(2, 128, D)] * 4 + [whole(8, 128, 128)],
            out_specs=[whole(D, 128), whole(D, 128)],
        ),
        out_shape=[sds((D, 128), F32), sds((D, 128), BF)],
        compiler_params=params(56),
        cost_estimate=cost(3),
        name="out_grads",
    )(marks, *pieces, joined)


def ring_parts_kernel(s_ref, q_ref, o_ref, raw_ref, got_ref, keep_ref, sum_ref, m1, m3, m2):
    a, b = s_ref[3], s_ref[4]

    def rows(chunk):
        at = pl.ds(pl.multiple_of(chunk * 128, 128), 128)
        return jnp.concatenate([q_ref[at, :], o_ref[at, :]], 1) + got_ref[at, :].astype(F32)

    gains = read_gains(raw_ref.at[0], 128)
    for j in range(1, 8):
        gains = gains + read_gains(raw_ref.at[j], 128)
    sum_ref[...] = gains
    for d, ref in ((1, m1), (3, m3), (2, m2)):
        at = ((a + d) & 3) * 2
        ref[:128, :] = rows(at + (b ^ 1)).astype(BF)
        ref[128:256, :] = rows(at + b).astype(BF)
        write_gains(ref, 256, gains)
    at = a * 2
    keep_ref[0] = rows(at + (b ^ 1))
    keep_ref[1] = rows(at + b)


def ring_parts(marks, own_q, own_o, raw, got):
    return pl.pallas_call(
        ring_parts_kernel,
        grid_spec=pltpu.PrefetchScalarGridSpec(
            num_scalar_prefetch=1,
            grid=(1,),
            in_specs=[whole(D, 128), whole(D, 128), whole(8, 176, 256), whole(D, 256)],
            out_specs=[whole(2, 128, 256), whole(16, 256)] + [whole(304, 256)] * 3,
        ),
        out_shape=[sds((2, 128, 256), F32), sds((16, 256), F32)] + [sds((304, 256), BF)] * 3,
        compiler_params=params(56),
        cost_estimate=cost(2),
        name="ring_parts",
    )(marks, own_q, own_o, raw, got)


def pair_parts_kernel(keep_ref, gains_ref, m1, m3, m2, own_ref, out_ref, msg_ref):
    other, own = keep_ref[0], keep_ref[1]
    gains = gains_ref[...]
    for ref in (m1, m3, m2):
        other = other + ref[:128, :].astype(F32)
        own = own + ref[128:256, :].astype(F32)
        gains = gains + read_gains(ref, 256)
    own_ref[...] = own
    out_ref[...] = gains
    msg_ref[:128, :] = other.astype(BF)
    write_gains(msg_ref, 128, gains)


def pair_parts(keep, gains, got):
    return pl.pallas_call(
        pair_parts_kernel,
        out_shape=[sds((128, 256), F32), sds((16, 256), F32), sds((176, 256), BF)],
        compiler_params=params(56),
        cost_estimate=cost(2),
        name="pair_parts",
    )(keep, gains, *got)


def last_parts_kernel(own_ref, gains_ref, got_ref, qkv_ref, out_ref, sum_ref):
    t = own_ref[...] + got_ref[:128, :].astype(F32)
    sum_ref[...] = gains_ref[...] + read_gains(got_ref, 128)
    qkv_ref[...] = t[:, :128]
    out_ref[...] = t[:, 128:].T[:64]


def last_parts(own, gains, got):
    return pl.pallas_call(
        last_parts_kernel,
        out_shape=[sds((128, 128), F32), sds((64, 128), F32), sds((16, 256), F32)],
        compiler_params=params(56),
        cost_estimate=cost(2),
        name="last_parts",
    )(own, gains, got)


def body(tokens, cotangent, deal_order, lengths, routes, route_gates, gain_first, gain_second, gain_query, gain_key,
         weight_qkv, weight_out, weight_gate, weight_up, weight_down):
    col = lax.axis_index("col")
    core = col % 2
    a, b = place("col")
    ra, rb = place("row")
    order = [(a + d) % 4 for d in (1, 3, 2, 0)]
    row_order = [(ra + d) % 4 for d in (1, 3, 2, 0)]
    back = [(a - d) % 4 for d in (1, 3, 2, 0)]
    marks = jnp.stack([core, a, b, ra, rb, 1 - core, col, core] + order + row_order + back).astype(jnp.int32)
    planes = [[i for i in range(16) if i % 2 == k] for k in range(2)]
    swap_all = partial(lax.all_to_all, axis_name="col", split_axis=0, concat_axis=0, tiled=True,
                       axis_index_groups=planes)

    extra = jnp.concatenate([routes.T.astype(BF)] + [p.T.astype(BF) for p in three(route_gates)], 1)
    cot = jnp.concatenate([cotangent, jnp.pad(extra, ((0, 8), (0, 512)))], 0)
    wide = jnp.concatenate([w.reshape(128, 2 * FF) for w in (weight_gate, weight_up, weight_down)], 1).astype(BF)

    qkv_low = weight_qkv.astype(BF)
    near, qkv_pair, wide, cot = together(step_pair(tokens, "col"), step_core(qkv_low), wide, cot)
    small = jnp.concatenate([qkv_low, qkv_pair, weight_out.astype(BF), jnp.zeros((128, 64), BF)], 1)
    small_pair = step_pair(small, "row")
    cot_near = step_pair(cot, "col")
    x_pieces = gather_rest(near, tokens, "col")
    w_all = lax.all_gather(wide, "row", axis=0, tiled=True)
    w_chip, w_scaled, qkv_t, out_t = place_small(marks, gather_rest(small_pair, small, "row"), gain_first[None])
    out_near = step_pair(out_t, "col")

    inverse, segment, offset = places(marks, lengths, deal_order.reshape(16, 128))
    frequency = THETA ** (-(jnp.arange(128) % 32).astype(F32) * 2.0 / HEAD)
    angles = offset * frequency[None, None, :]
    cos, sin = jnp.cos(angles), jnp.sin(angles)
    gains = jnp.concatenate([gain_query, gain_query, gain_key, jnp.ones((HEAD,), F32)])[None, :]

    out_near, w_scaled, cos, sin, segment, gain_column, *x_pieces = together(
        out_near, w_scaled, cos, sin, segment, gain_first[:, None], *x_pieces)
    both = gather_rest(jnp.concatenate([cot_near, out_near], 0), jnp.concatenate([cot, out_t], 0), "col")
    q0, q1, kv, raw, f1_all = project_heads(
        marks, x_pieces, w_scaled, gains, cos, sin, segment)
    kv_sib = step_core(kv)
    joined, logs = attend(q0, q1, kv, kv_sib)
    joined_got = swap_all(joined)
    joined_got, *both = together(joined_got, *both)
    out_own = [v[:, 144:] for v in both]
    out_sib = step_core(jnp.stack(out_own))
    hidden, middle, wout_t = after_attention(marks, joined_got, out_own, out_sib, tokens, gain_second[None])
    mid_pair = step_pair(middle, "col")
    hidden, *both = together(hidden, *both)
    cot_own = jnp.stack([v[:, :144] for v in both])
    cot_sib = step_core(cot_own)
    gates = given_gates(marks, cot_own, cot_sib, inverse).reshape(4, 2, 2, 8, 128)
    pre0, pre1, cot0, cot1 = inner_products(cot_own, cot_sib, w_all)
    own0 = jnp.stack([mid_pair, middle])
    near0, far0 = step_ring(own0, "col", 1), step_ring(own0, "col", 3)
    near0, far0, own0, gates, pre0 = together(near0, far0, own0, gates, pre0)
    last0 = step_ring(own0, "col", 2)
    part = run_experts(marks, 0, jnp.stack([near0, far0, own0]), pre0, gates, w_all, lambda i: i + i // 2)
    last0, *part = together(last0, *part)
    mid0 = jnp.stack([near0, far0, last0, own0])
    mid1 = step_core(mid0)
    qkv_t, mid0 = together(qkv_t, mid0)
    wqkv_t = lax.all_gather(qkv_t, "col", axis=0, tiled=True)

    mid1, *part = together(mid1, *part)
    e_other, gg1, ug1, in1 = run_experts(marks, 5, mid1, pre1, gates, w_all)
    last0, e_other = together(last0, e_other)
    e_own, gg0, ug0, in0 = run_experts(marks, 0, last0[None], pre0, gates, w_all, lambda i: i + 2, part)
    entry = add_pair(e_own, step_core(e_other))
    entry, gg0 = together(entry, gg0)
    entry_got = swap_all(entry)
    in1, entry = together(in1, entry)
    r_other = results(marks, in1, w_all)
    grads = weight_grads(((mid0, mid1), (gg0, gg1)), ((mid0, mid1), (ug0, ug1)), ((cot0, cot1), (in0, in1)))

    entry_got, grads, r_other = together(entry_got, grads, r_other)
    r_got = step_core(r_other)
    grads = lax.psum_scatter(grads, "row", scatter_dimension=0, tiled=True)
    hidden_grad, hidden_low, joined_grad, second = second_back(entry_got, hidden, cotangent, gain_second[None], wout_t)
    joined_grad, in0 = together(joined_grad, in0)
    joined_grad = swap_all(joined_grad)
    r_sum = results(marks, in0, w_all, r_got).reshape(8, 128, D)
    hidden_near, r_sum = together(step_pair(hidden_low, "col"), r_sum)
    hidden_pair = jnp.stack([hidden_near, hidden_low])
    joined_grad, r_sum, hidden_pair = together(joined_grad, r_sum, hidden_pair)
    hidden_pieces = [step_ring(hidden_pair, "col", d) for d in AHEAD] + [hidden_pair]
    dq, dkv_own, dkv_other = attend_back(q0, q1, kv, kv_sib, joined, logs, joined_grad)
    dkv_got = step_core(dkv_other)
    raw_grad, raw_scaled, gain_heads = heads_back(dq, dkv_own, dkv_got, raw, f1_all, gains, cos, sin)
    raw_scaled, *hidden_pieces = together(raw_scaled, *hidden_pieces)
    own_q, other_q, sums = qkv_grads(
        marks, x_pieces, raw_scaled, w_chip, gain_column, second, gain_heads)
    sums_got = step_core(sums)
    own_o, other_o = out_grads(marks, hidden_pieces, joined)
    raw_got = swap_all(add_gains(sums, sums_got, raw_grad))
    msg_got = step_core(jnp.concatenate([other_q, other_o], 1))
    raw_got, r_sum, msg_got = together(raw_got, r_sum, msg_got)
    out_got = swap_all(r_sum)
    keep, sums, *msgs = ring_parts(marks, own_q, own_o, raw_got, msg_got)
    input_grad = first_back(raw_got, wqkv_t, tokens, gain_first[None], hidden_grad)
    keep, input_grad, *msgs = together(
        keep, input_grad, *[step_ring(m, "row", d) for m, d in zip(msgs, AHEAD)])
    own, sums, msg = pair_parts(keep, sums, msgs)
    msg_got, grads = together(step_pair(msg, "row"), grads)
    grads_w = unpack(grads)
    grad_qkv, grad_out, sums = last_parts(own, sums, msg_got)
    out_got, grad_qkv = together(out_got, grad_qkv)
    block_out = add_up(hidden, out_got)
    heads = sums[8]
    return (
        block_out,
        input_grad,
        sums[:4].reshape(-1),
        sums[4:8].reshape(-1),
        heads[:64] + heads[64:128],
        heads[128:192],
        grad_qkv,
        grad_out.T,
        *grads_w,
    )


def solution(mesh):
    both = P(("row", "col"), None)
    return jax.shard_map(
        body,
        mesh=mesh,
        in_specs=(both, both, P("row", None), P("row", None), both, both, P(), P(), P(), P(),
                  P("row", "col"), P("row", "col"), P("row", "col", None), P("row", "col", None),
                  P("row", "col", None)),
        out_specs=(both, both, P(), P(), P(), P(), P("row", "col"), P("row", "col"), P("row", "col", None),
                   P("row", "col", None), P("row", "col", None)),
        check_vma=False,
    )
```

```python
from functools import partial

import jax
import jax.numpy as jnp
import numpy as np
from jax import lax
from jax.experimental import pallas as pl
from jax.experimental.pallas import tpu as pltpu
from jax.sharding import PartitionSpec as P

D = 1024
HEAD = 64
EXPERTS = 32
FF = 512
TOP = 8
TOK = 128
GROUP = 2048
PLANE = 1024
EPS_WIDE = 1e-05
EPS_HEAD = 1e-06
THETA = 10000.0
LOG2E = 1.4426950408889634
LN2 = 0.6931471805599453
QSCALE = LOG2E * HEAD**-0.5
APART = -256.0
BF = jnp.bfloat16
F32 = jnp.float32
NT = (((1,), (1,)), ((), ()))
TN = (((0,), (0,)), ((), ()))
HIGH = lax.Precision.HIGHEST


def params(mib=56):
    return pltpu.CompilerParams(vmem_limit_bytes=mib * 2**20)


def cost(us, scale=0.02):
    us = us * scale
    return pl.CostEstimate(flops=int(us * 1e9), bytes_accessed=int(us * 1e6), transcendentals=0)


def dot(a, b, dims=None):
    if dims is None:
        dims = (((1,), (0,)), ((), ()))
    return lax.dot_general(a, b, dims, preferred_element_type=F32)


def sds(shape, kind):
    return jax.ShapeDtypeStruct(shape, kind)


def whole(*shape):
    return pl.BlockSpec(shape, lambda *_: (0,) * len(shape))


def together(*values):
    return lax.optimization_barrier(values)


AHEAD = (1, 3, 2)


def step_pair(v, axis):
    if axis == "row":
        route = [(i, i ^ 1) for i in range(8)]
    else:
        route = [(i, i ^ 2) for i in range(16)]
    return lax.ppermute(v, axis, route)


def step_ring(v, axis, d):
    if axis == "row":
        route = [(i, (i + 2 * d) % 8) for i in range(8)]
    else:
        route = [(i, (i + 4 * d) % 16) for i in range(16)]
    return lax.ppermute(v, axis, route)


def step_core(v):
    return lax.ppermute(v, "col", [(i, i ^ 1) for i in range(16)])


def place(axis):
    i = lax.axis_index(axis)
    if axis == "col":
        i = i // 2
    return i // 2, i % 2


def gather_rest(pair, v, axis):
    pair = jnp.stack([pair, v])
    return [step_ring(pair, axis, d) for d in AHEAD] + [pair]


def gather_plain(v, axis):
    return gather_rest(step_pair(v, axis), v, axis)


def added(terms):
    t = terms[0].astype(F32)
    for r in terms[1:]:
        t = t + r.astype(F32)
    return t


def places_kernel(s_ref, l_ref, deal_ref, inv_ref, seg_ref, off_ref):
    core = s_ref[0]
    row = lax.broadcasted_iota(jnp.int32, (128, 128), 0)
    lane = lax.broadcasted_iota(jnp.int32, (128, 128), 1)
    ends = [l_ref[0, 0]]
    for n in range(1, 4):
        ends.append(ends[-1] + l_ref[0, n])
    for k in range(16):
        found = jnp.zeros((128, 128), jnp.int32)
        for n in range(16):
            deal = jnp.broadcast_to(deal_ref[n : n + 1, :], (128, 128))
            found = jnp.where(deal == row + k * 128, lane + n * 128, found)
        slot = jnp.sum(found.astype(F32), axis=1, keepdims=True)
        inv_ref[k : k + 1, :] = jnp.broadcast_to(slot, (128, 128)).T[:1].astype(jnp.int32)
        slot = slot.astype(jnp.int32)
        seg = jnp.zeros((128, 1), jnp.int32)
        start = jnp.zeros((128, 1), jnp.int32)
        for end in ends:
            seg = seg + jnp.where(slot >= end, 1, 0)
            start = jnp.where(slot >= end, end, start)

        @pl.when(core == k % 2)
        def _():
            seg_ref[k // 2] = seg
            off_ref[k // 2] = (slot - start).astype(F32)


def places(marks, lengths, deal):
    return pl.pallas_call(
        places_kernel,
        grid_spec=pltpu.PrefetchScalarGridSpec(
            num_scalar_prefetch=2,
            grid=(1,),
            in_specs=[whole(16, 128)],
            out_specs=[whole(16, 128), whole(8, 128, 1), whole(8, 128, 1)],
        ),
        out_shape=[sds((16, 128), jnp.int32), sds((8, 128, 1), jnp.int32), sds((8, 128, 1), F32)],
        compiler_params=params(56),
        cost_estimate=cost(3),
        name="places",
    )(marks, lengths, deal)


def head_sums():
    i = np.arange(256) // HEAD
    return jnp.asarray((i[:, None] == i[None, :]) / HEAD, BF)


def spread():
    s = np.zeros((256, 512), np.float32)
    for h in range(4):
        for i in range(64):
            s[h * 64 + i, h * 128 + i] = 1.0
    return jnp.asarray(s, BF)


def exact_sums(v, sums):
    hi = v.astype(BF)
    lo = (v - hi.astype(F32)).astype(BF)
    return dot(hi, sums) + dot(lo, sums)


def half_turn(v, lane):
    back = jnp.concatenate([pltpu.roll(v[:, :128], 96, 1), pltpu.roll(v[:, 128:], 96, 1)], 1)
    ahead = jnp.concatenate([pltpu.roll(v[:, :128], 32, 1), pltpu.roll(v[:, 128:], 32, 1)], 1)
    return jnp.where(lane % 64 < 32, -back, ahead)


def wide_tables(c, s, lane):
    c = jnp.where(lane < 192, jnp.concatenate([c, c], 1), 1.0)
    s = jnp.where(lane < 192, jnp.concatenate([s, s], 1), 0.0)
    return c, s


def heads_kernel(s_ref, x0, x1, x2, x3, w_ref, g_ref, c_ref, s_tab_ref, seg_ref, bd_ref, sp_ref,
                 q0_ref, q1_ref, kv_ref, raw_ref, f_ref):
    a, b = s_ref[1], s_ref[2]
    lane = lax.broadcasted_iota(jnp.int32, (256, 256), 1)
    l1 = lax.broadcasted_iota(jnp.int32, (256, 128), 1)
    inseg = (l1 >= 64) & (l1 < 68)
    aug_v = jnp.where((l1 >= 64) & (l1 < 67), 1.0, 0.0)
    for ref, d in zip((x0, x1, x2, x3), (1, 3, 2, 0)):
        at = ((a - d) & 3) * 2
        blocks = (at + (b ^ 1), at + b)

        def both(r):
            return jnp.concatenate([r[blocks[0]], r[blocks[1]]], 0)

        def put(r, v):
            r[blocks[0]] = v[:128]
            r[blocks[1]] = v[128:]

        x = ref[...].reshape(256, D)
        xf = x.astype(F32)
        f = lax.rsqrt(jnp.mean(xf * xf, axis=1, keepdims=True) + EPS_WIDE)
        raw = dot(x, w_ref[...]) * f
        put(raw_ref, raw)
        put(f_ref, f)
        fac = jnp.where(lane < 192, lax.rsqrt(exact_sums(raw * raw, bd_ref[...]) + EPS_HEAD), 1.0)
        h = raw * fac * g_ref[...]
        c, s = wide_tables(both(c_ref), both(s_tab_ref), lane)
        t = h * c + half_turn(h, lane) * s
        t = jnp.where(lane < 128, t * QSCALE, t).astype(BF)
        wide = dot(t, sp_ref[...])
        same = (l1 - 64) == both(seg_ref)
        aug_q = jnp.where(inseg & jnp.logical_not(same), APART, 0.0)
        aug_k = jnp.where((inseg & same) | ((l1 >= 68) & (l1 < 71)), 1.0, 0.0)
        put(q0_ref, (wide[:, 0:128] + aug_q).astype(BF))
        put(q1_ref, (wide[:, 128:256] + aug_q).astype(BF))
        put(kv_ref.at[0], (wide[:, 256:384] + aug_k).astype(BF))
        put(kv_ref.at[1], (wide[:, 384:512] + aug_v).astype(BF))


def project_heads(marks, pieces, w, gains, cos, sin, seg):
    return pl.pallas_call(
        heads_kernel,
        grid_spec=pltpu.PrefetchScalarGridSpec(
            num_scalar_prefetch=1,
            grid=(1,),
            in_specs=[whole(2, 128, D)] * 4 + [whole(D, 256), whole(1, 256), whole(8, 128, 128), whole(8, 128, 128),
                                               whole(8, 128, 1), whole(256, 256), whole(256, 512)],
            out_specs=[whole(8, 128, 128)] * 2 + [whole(2, 8, 128, 128), whole(8, 128, 256), whole(8, 128, 1)],
        ),
        out_shape=[sds((8, 128, 128), BF)] * 2 + [sds((2, 8, 128, 128), BF), sds((8, 128, 256), F32),
                                                  sds((8, 128, 1), F32)],
        compiler_params=params(56),
        cost_estimate=cost(7),
        name="project_heads",
    )(marks, *pieces, w, gains, cos, sin, seg, head_sums(), spread())


WIDE = 512


def attend_kernel(q0_ref, q1_ref, own_ref, sib_ref, o_ref, l_ref):
    q = jnp.concatenate([q0_ref[...].reshape(WIDE, 128), q1_ref[...].reshape(WIDE, 128)], 0)
    acc = jnp.zeros((128, 2 * WIDE), F32)
    for ref in (own_ref, sib_ref):
        p = jnp.exp2(dot(ref[0], q, NT)).astype(BF)
        acc = acc + dot(ref[1], p, TN)
    acc = acc.T
    total = acc[:, 64:65]
    o = acc / total
    l_ref[...] = jnp.log2(total).reshape(2, 4, 128, 1)
    lane = lax.broadcasted_iota(jnp.int32, (WIDE, 128), 1)
    o = jnp.where(lane < 64, o[:WIDE], pltpu.roll(o[WIDE:], 64, 1))
    o_ref[...] = o.astype(BF).reshape(4, 128, 128)


def four(n, m):
    return pl.BlockSpec((4, n, m), lambda j: (j, 0, 0))


def two_four(n, m):
    return pl.BlockSpec((2, 4, n, m), lambda j: (0, j, 0, 0))


def attend(q0, q1, own, sib):
    return pl.pallas_call(
        attend_kernel,
        grid=(2,),
        in_specs=[four(128, 128), four(128, 128), whole(2, PLANE, 128), whole(2, PLANE, 128)],
        out_specs=[four(128, 128), two_four(128, 1)],
        out_shape=[sds((8, 128, 128), BF), sds((2, 8, 128, 1), F32)],
        compiler_params=params(56),
        cost_estimate=cost(7),
        name="attend",
    )(q0, q1, own.reshape(2, PLANE, 128), sib.reshape(2, PLANE, 128))


def three(v):
    hi = v.astype(BF).astype(F32)
    mid = (v - hi).astype(BF).astype(F32)
    return hi, mid, v - hi - mid


def attend_back_kernel(q0_ref, q1_ref, kvo_ref, kvs_ref, o_ref, l_ref, g_ref,
                       dq_ref, own_ref, other_ref, dk_ref, dv_ref):
    @pl.when(pl.program_id(0) == 0)
    def _():
        dk_ref[...] = jnp.zeros_like(dk_ref)
        dv_ref[...] = jnp.zeros_like(dv_ref)

    lane = lax.broadcasted_iota(jnp.int32, (2 * WIDE, 128), 1)
    q = jnp.concatenate([q0_ref[...].reshape(WIDE, 128), q1_ref[...].reshape(WIDE, 128)], 0)
    h0, h1, h2 = three(l_ref[...].reshape(2 * WIDE, 1))
    ql = jnp.where(lane == 68, -h0, jnp.where(lane == 69, -h1, jnp.where(lane == 70, -h2, q.astype(F32))))
    ql = ql.astype(BF)
    g = g_ref[...].reshape(WIDE, 128).astype(F32)
    o = o_ref[...].reshape(WIDE, 128).astype(F32)
    g = jnp.concatenate([g, pltpu.roll(g, 64, 1)], 0)
    o = jnp.concatenate([o, pltpu.roll(o, 64, 1)], 0)
    g = jnp.where(lane < 64, g, 0.0)
    centre = jnp.sum(g * o, axis=1, keepdims=True)
    c0, c1, c2 = three(centre)
    gl = jnp.where(lane == 64, -c0, jnp.where(lane == 65, -c1, jnp.where(lane == 66, -c2, g)))
    gl = gl.astype(BF)
    gb = g.astype(BF)
    dq = jnp.zeros((128, 2 * WIDE), F32)
    for j in range(GROUP // WIDE):
        rows = pl.ds(j * WIDE, WIDE)
        ref = kvo_ref if j * WIDE < PLANE else kvs_ref
        part = pl.ds(j * WIDE % PLANE, WIDE)
        k = ref[0, part, :]
        pt = jnp.exp2(dot(k, ql, NT))
        ds = (pt * dot(ref[1, part, :], gl, NT)).astype(BF)
        dv_ref[rows, :] += dot(pt.astype(BF), gb)
        dk_ref[rows, :] += dot(ds, q)
        dq = dq + dot(k, ds, TN)
    dq_ref[...] = dq.T.reshape(2, 4, 128, 128)

    @pl.when(pl.program_id(0) == 1)
    def _():
        low = lax.broadcasted_iota(jnp.int32, (128, 128), 1) < 64

        def block(j):
            rows = pl.ds(j * 128, 128)
            return jnp.where(low, dk_ref[rows, :] * LN2, pltpu.roll(dv_ref[rows, :], 64, 1))

        for j in range(8):
            own_ref[j] = block(j)
            other_ref[j] = block(8 + j).astype(BF)


def attend_back(q0, q1, own, sib, o, l, g):
    kv = whole(2, PLANE, 128)
    return pl.pallas_call(
        attend_back_kernel,
        grid=(2,),
        in_specs=[four(128, 128), four(128, 128), kv, kv, four(128, 128), two_four(128, 1), four(128, 128)],
        out_specs=[two_four(128, 128), whole(8, 128, 128), whole(8, 128, 128)],
        out_shape=[sds((2, 8, 128, 128), F32), sds((8, 128, 128), F32), sds((8, 128, 128), BF)],
        scratch_shapes=[pltpu.VMEM((GROUP, 128), F32)] * 2,
        compiler_params=params(56),
        cost_estimate=cost(17),
        name="attend_back",
    )(q0, q1, own.reshape(2, PLANE, 128), sib.reshape(2, PLANE, 128), o, l, g)


def heads_back_kernel(dq_ref, own_ref, got_ref, raw_ref, f_ref, g_ref, c_ref, sin_ref, bd_ref,
                      out_ref, scaled_ref, gain_ref):
    @pl.when(pl.program_id(0) == 0)
    def _():
        gain_ref[...] = jnp.zeros_like(gain_ref)

    rows = WIDE
    lane1 = lax.broadcasted_iota(jnp.int32, (rows, 128), 1)
    dq = dq_ref[...].reshape(2 * rows, 128) * HEAD**-0.5
    dq = jnp.where(lane1 < 64, dq[:rows], pltpu.roll(dq[rows:], 64, 1))
    dkv = own_ref[...] + got_ref[...].astype(F32)
    d = jnp.concatenate([dq, dkv.reshape(rows, 128)], 1)
    raw = raw_ref[...].reshape(rows, 256)
    lane = lax.broadcasted_iota(jnp.int32, (rows, 256), 1)
    bd = bd_ref[...]
    fac = jnp.where(lane < 192, lax.rsqrt(exact_sums(raw * raw, bd) + EPS_HEAD), 1.0)
    hat = raw * fac
    c, s = wide_tables(c_ref[...].reshape(rows, 128), sin_ref[...].reshape(rows, 128), lane)
    dh = d * c - half_turn(d * s, lane)
    gain_ref[...] += jnp.sum(dh * hat, axis=0, keepdims=True)
    dn = dh * g_ref[...]
    back = fac * (dn - hat * exact_sums(dn * hat, bd))
    res = jnp.where(lane < 192, back, d)
    out_ref[:, :128] = res.astype(BF).reshape(4, 128, 256)
    scaled_ref[...] = (res * f_ref[...].reshape(rows, 1)).astype(BF).reshape(4, 128, 256)


def heads_back(dq, own, got, raw, f, gains, cos, sin):
    return pl.pallas_call(
        heads_back_kernel,
        grid=(2,),
        in_specs=[two_four(128, 128), four(128, 128), four(128, 128), four(128, 256), four(128, 1),
                  whole(1, 256), four(128, 128), four(128, 128), whole(256, 256)],
        out_specs=[four(128, 256), four(128, 256), whole(1, 256)],
        out_shape=[sds((8, 176, 256), BF), sds((8, 128, 256), BF), sds((1, 256), F32)],
        compiler_params=params(56),
        cost_estimate=cost(6),
        name="heads_back",
    )(dq, own, got, raw, f, gains, cos, sin, head_sums())


def norm_factor(v):
    return lax.rsqrt(jnp.mean(v * v, axis=1, keepdims=True) + EPS_WIDE)


def after_attention_kernel(s_ref, j_ref, *refs):
    own, sib = refs[0:4], refs[4]
    x_ref, g_ref, hidden_ref, middle_ref, w_ref = refs[5:]
    core, a, b = s_ref[0], s_ref[1], s_ref[2]
    for i, d in enumerate((1, 3, 2, 0)):
        for r in range(2):
            chip = ((a - d) & 3) * 2 + (b ^ (1 - r))
            at = chip * 128 + core * 64
            w_ref[pl.ds(pl.multiple_of(at, 64), 64), :] = own[i][r]
            at = chip * 128 + (1 - core) * 64
            w_ref[pl.ds(pl.multiple_of(at, 64), 64), :] = sib[i, r]
    hidden = x_ref[...].astype(F32)
    for j in range(8):
        hidden = hidden + dot(j_ref[j], w_ref[j * 128 : j * 128 + 128, :])
    hidden_ref[...] = hidden
    middle_ref[...] = (hidden * norm_factor(hidden) * g_ref[...]).astype(BF)


def after_attention(marks, joined, own, sib, x, gain):
    return pl.pallas_call(
        after_attention_kernel,
        grid_spec=pltpu.PrefetchScalarGridSpec(
            num_scalar_prefetch=1,
            grid=(1,),
            in_specs=[whole(8, 128, 128)] + [whole(2, 64, D)] * 4 + [whole(4, 2, 64, D), whole(128, D), whole(1, D)],
            out_specs=[whole(128, D), whole(128, D), whole(D, D)],
        ),
        out_shape=[sds((128, D), F32), sds((128, D), BF), sds((D, D), BF)],
        compiler_params=params(24),
        cost_estimate=cost(3),
        name="after_attention",
    )(marks, joined, *own, sib, x, gain)


def second_back_kernel(m_ref, hidden_ref, cot_ref, g_ref, w_ref, grad_ref, low_ref, joined_ref, gain_ref):
    mg = m_ref[0].astype(F32)
    for j in range(1, 8):
        mg = mg + m_ref[j].astype(F32)
    hidden = hidden_ref[...]
    f = norm_factor(hidden)
    hat = hidden * f
    gain_ref[...] = jnp.sum(mg * hat, axis=0, keepdims=True)
    dn = mg * g_ref[...]
    grad = cot_ref[...].astype(F32) + f * (dn - hat * jnp.mean(dn * hat, axis=1, keepdims=True))
    grad_ref[...] = grad
    low = grad.astype(BF)
    low_ref[...] = low
    joined = dot(low, w_ref[...], NT).astype(BF)
    for j in range(8):
        joined_ref[j] = joined[:, j * 128 : j * 128 + 128]


def second_back(chunks, hidden, cot, gain, w):
    return pl.pallas_call(
        second_back_kernel,
        out_shape=[sds((128, D), F32), sds((128, D), BF), sds((8, 128, 128), BF), sds((1, D), F32)],
        compiler_params=params(20),
        cost_estimate=cost(2),
        name="second_back",
    )(chunks, hidden, cot, gain, w)


def first_back_kernel(raw_ref, w_ref, x_ref, g_ref, grad_ref, out_ref):
    ng = dot(raw_ref[0, :128], w_ref[0:256, :])
    for j in range(1, 8):
        ng = ng + dot(raw_ref[j, :128], w_ref[j * 256 : j * 256 + 256, :])
    x = x_ref[...].astype(F32)
    f = norm_factor(x)
    hat = x * f
    dn = ng * g_ref[...]
    out_ref[...] = (grad_ref[...] + f * (dn - hat * jnp.mean(dn * hat, axis=1, keepdims=True))).astype(BF)


def first_back(raw, w, x, gain, grad):
    return pl.pallas_call(
        first_back_kernel,
        out_shape=sds((128, D), BF),
        compiler_params=params(24),
        cost_estimate=cost(2),
        name="first_back",
    )(raw, w, x, gain, grad)


def place_small_kernel(s_ref, p0, p1, p2, p3, g_ref, chip_ref, scaled_ref, qkv_ref, out_ref):
    core, a, b = s_ref[0], s_ref[3], s_ref[4]
    for ref, d in zip((p0, p1, p2, p3), (1, 3, 2, 0)):
        for r in range(2):
            at = pl.multiple_of((((a - d) & 3) * 2 + (b ^ (1 - r))) * 128, 128)
            v = ref[r]
            own, other = v[:, :128], v[:, 128:256]
            chip = jnp.where(core == 0, jnp.concatenate([own, other], 1), jnp.concatenate([other, own], 1))
            chip_ref[pl.ds(at, 128), :] = chip
            gain = jnp.broadcast_to(g_ref[:, pl.ds(at, 128)], (128, 128)).T
            gain = jnp.concatenate([gain, gain], 1)
            scaled_ref[pl.ds(at, 128), :] = (chip.astype(F32) * gain).astype(BF)
            qkv_ref[:, pl.ds(at, 128)] = own.astype(F32).T.astype(BF)
            out_ref[:, pl.ds(at, 128)] = v[:, 256:].astype(F32).T[:64].astype(BF)


def place_small(marks, pieces, gain):
    return pl.pallas_call(
        place_small_kernel,
        grid_spec=pltpu.PrefetchScalarGridSpec(
            num_scalar_prefetch=1,
            grid=(1,),
            in_specs=[whole(2, 128, 384)] * 4 + [whole(1, D)],
            out_specs=[whole(D, 256), whole(D, 256), whole(128, D), whole(64, D)],
        ),
        out_shape=[sds((D, 256), BF), sds((D, 256), BF), sds((128, D), BF), sds((64, D), BF)],
        compiler_params=params(56),
        cost_estimate=cost(2),
        name="place_small",
    )(marks, *pieces, gain)


def given_gates_kernel(s_ref, own_ref, sib_ref, inv_ref, out_ref, dealt):
    core, a, b = s_ref[0], s_ref[1], s_ref[2]
    row = lax.broadcasted_iota(jnp.int32, (8, 128), 0)
    for ref, side in ((own_ref, core), (sib_ref, 1 - core)):
        for i, d in enumerate((1, 3, 2, 0)):
            for r in range(2):
                ex = ref[i, r].astype(F32)
                names = ex[:8, 0:128]
                values = ex[:8, 128:256] + ex[:8, 256:384] + ex[:8, 384:512]
                both = jnp.zeros((8, 128), F32)
                for e in range(2):
                    mine = (s_ref[6] * 2 + e).astype(F32)
                    g = jnp.sum(jnp.where(names == mine, values, 0.0), axis=0, keepdims=True)
                    both = jnp.where(row == e, g, both)
                dealt[((a - d) & 3) * 4 + (b ^ (1 - r)) * 2 + side] = both
    for n in range(16):
        slot = jnp.broadcast_to(inv_ref[n : n + 1, :], (8, 128))
        at, of = slot & 127, slot >> 7
        got = jnp.zeros((8, 128), F32)
        for k in range(16):
            got = jnp.where(of == k, jnp.take_along_axis(dealt[k], at, axis=1), got)
        out_ref[n] = got


def given_gates(marks, own, sib, inverse):
    extra = pl.BlockSpec((4, 2, 16, D), lambda i, s: (0, 0, 8, 0))
    return pl.pallas_call(
        given_gates_kernel,
        grid_spec=pltpu.PrefetchScalarGridSpec(
            num_scalar_prefetch=1,
            grid=(1,),
            in_specs=[extra, extra, whole(16, 128)],
            out_specs=whole(16, 8, 128),
            scratch_shapes=[pltpu.VMEM((16, 8, 128), F32)],
        ),
        out_shape=sds((16, 8, 128), F32),
        compiler_params=params(56),
        cost_estimate=cost(2),
        name="given_gates",
    )(marks, own, sib, inverse)


def inner_kernel(own_ref, sib_ref, w_ref, po_ref, ps_ref, co_ref, cs_ref):
    w = w_ref[...]
    for ref, p_ref, c_ref in ((own_ref, po_ref, co_ref), (sib_ref, ps_ref, cs_ref)):
        up = ref[0, :, :128]
        c_ref[0] = up
        p_ref[0] = dot(up.reshape(256, D), w).astype(BF).reshape(2, 128, D)


def inner_products(own, sib, w):
    side = pl.BlockSpec((1, 2, 144, D), lambda i: (i, 0, 0, 0))
    spec = pl.BlockSpec((1, 2, 128, D), lambda i: (i, 0, 0, 0))
    return pl.pallas_call(
        inner_kernel,
        grid=(4,),
        in_specs=[side, side, pl.BlockSpec((D, 2 * FF), lambda i: (0, 2))],
        out_specs=[spec] * 4,
        out_shape=[sds((4, 2, 128, D), BF)] * 4,
        compiler_params=params(56),
        cost_estimate=cost(8),
        name="inner_products",
    )(own, sib, w)


def experts_kernel(s_ref, mid_ref, pre_ref, g_ref, w_ref, *refs):
    entry_ref, gg_ref, ug_ref, in_ref = refs[-4:]
    mid = mid_ref[...].reshape(256, D)
    b = s_ref[2]
    gates = jnp.concatenate([g_ref[0, b ^ 1, 0].T, g_ref[0, b, 0].T], 0)
    entry = None
    for e in range(2):
        cg = slice(e * FF, e * FF + FF)
        cu = slice(1024 + e * FF, 1024 + e * FF + FF)
        gp = dot(mid, w_ref[:, cg])
        u = dot(mid, w_ref[:, cu])
        g = gates[:, e : e + 1]
        ig = pre_ref[0, :, :, cg].reshape(256, FF).astype(F32) * g
        sig = 0.5 * jnp.tanh(0.5 * gp) + 0.5
        act = gp * sig
        inner = (g * act * u).astype(BF)
        gg = (ig * u * (sig + act * (1.0 - sig))).astype(BF)
        ug = (ig * act).astype(BF)
        part = dot(gg, w_ref[:, cg], NT) + dot(ug, w_ref[:, cu], NT)
        entry = part if entry is None else entry + part
        for ref, v in ((in_ref, inner), (gg_ref, gg), (ug_ref, ug)):
            ref[0, :, :, cg] = v.reshape(2, 128, FF)
    entry = entry.astype(BF)
    entry_ref[0, b ^ 1] = entry[:128]
    entry_ref[0, b] = entry[128:]


def run_experts(marks, which, mid, pre, gates, w, pick=lambda i: i, before=()):
    hid = pl.BlockSpec((1, 2, 128, D), lambda i, s: (pick(i), 0, 0, 0))
    n = mid.shape[0]
    return pl.pallas_call(
        experts_kernel,
        grid_spec=pltpu.PrefetchScalarGridSpec(
            num_scalar_prefetch=1,
            grid=(n,),
            in_specs=[pl.BlockSpec((1, 2, 128, D), lambda i, s: (i, 0, 0, 0)), hid,
                      pl.BlockSpec((1, 2, 1, 8, 128), lambda i, s: (s[16 + pick(i)], 0, s[which], 0, 0)),
                      whole(D, 4 * FF)] + [pl.BlockSpec(memory_space=pl.ANY)] * len(before),
            out_specs=[pl.BlockSpec((1, 2, 128, D), lambda i, s: (s[16 + pick(i)], 0, 0, 0))] + [hid] * 3,
        ),
        out_shape=[sds((4, 2, 128, D), BF)] * 4,
        input_output_aliases={5 + k: k for k in range(len(before))},
        compiler_params=params(56),
        cost_estimate=cost(4 * n),
        name="run_experts",
    )(marks, mid, pre, gates, w, *before)


def add_pair_kernel(a_ref, b_ref, out_ref):
    out_ref[...] = (a_ref[...].astype(F32) + b_ref[...].astype(F32)).astype(BF)


def add_pair(a, b):
    spec = pl.BlockSpec((2, 128, D), lambda i: (i, 0, 0))
    return pl.pallas_call(
        add_pair_kernel,
        grid=(4,),
        in_specs=[spec, spec],
        out_specs=spec,
        out_shape=sds((8, 128, D), BF),
        compiler_params=params(8),
        cost_estimate=cost(2),
        name="add_pair",
    )(a.reshape(8, 128, D), b.reshape(8, 128, D))


def results_kernel(s_ref, in_ref, w_ref, *refs):
    b = s_ref[2]
    o = dot(in_ref[...].reshape(256, 2 * FF), w_ref[...], NT)
    for r in range(2):
        at = b ^ (1 - r)
        v = o[r * 128 : r * 128 + 128]
        if len(refs) == 2:
            v = v + refs[0][0, at].astype(F32)
        refs[-1][0, at] = v.astype(BF)


def results(marks, inner, w, got=None):
    hid = pl.BlockSpec((1, 2, 128, 2 * FF), lambda i, s: (i, 0, 0, 0))
    there = pl.BlockSpec((1, 2, 128, D), lambda i, s: (s[16 + i], 0, 0, 0))
    more = [] if got is None else [got]
    return pl.pallas_call(
        results_kernel,
        grid_spec=pltpu.PrefetchScalarGridSpec(
            num_scalar_prefetch=1,
            grid=(4,),
            in_specs=[hid, pl.BlockSpec((D, 2 * FF), lambda i, s: (0, 2))] + [there] * len(more),
            out_specs=there,
        ),
        out_shape=sds((4, 2, 128, D), BF),
        compiler_params=params(56),
        cost_estimate=cost(4),
        name="results",
    )(marks, inner, w, *more)


def add_up_kernel(h_ref, m_ref, out_ref):
    t = h_ref[...]
    for j in range(8):
        t = t + m_ref[j].astype(F32)
    out_ref[...] = t.astype(BF)


def add_up(hidden, chunks):
    return pl.pallas_call(
        add_up_kernel,
        out_shape=sds((128, D), BF),
        compiler_params=params(8),
        cost_estimate=cost(2),
        name="add_up",
    )(hidden, chunks)


def weights_kernel(*refs):
    out_ref = refs[-1]
    for n in range(len(refs) // 4):
        l0, l1, r0, r1 = refs[4 * n : 4 * n + 4]
        o = dot(l0[...].reshape(PLANE, 256), r0[...].reshape(PLANE, 1024), TN)
        o = o + dot(l1[...].reshape(PLANE, 256), r1[...].reshape(PLANE, 1024), TN)
        out_ref[:, n * 1024 : n * 1024 + 1024] = o.astype(BF)


def weight_grads(*sides):
    side = pl.BlockSpec((4, 2, 128, 256), lambda i: (0, 0, 0, i))
    hid = whole(4, 2, 128, 2 * FF)
    n = len(sides)
    return pl.pallas_call(
        weights_kernel,
        grid=(4,),
        in_specs=[side, side, hid, hid] * n,
        out_specs=pl.BlockSpec((256, n * 2 * FF), lambda i: (i, 0)),
        out_shape=sds((D, n * 2 * FF), BF),
        compiler_params=params(56),
        cost_estimate=cost(8 * n),
        name="weight_grads",
    )(*[v for left, right in sides for v in (*left, *right)])


def unpack_kernel(a_ref, g_ref, u_ref, d_ref):
    t = a_ref[...].astype(F32)
    for e in range(2):
        at = e * FF
        g_ref[:, e, :] = t[:, at : at + FF]
        u_ref[:, e, :] = t[:, 1024 + at : 1024 + at + FF]
        d_ref[:, e, :] = t[:, 2048 + at : 2048 + at + FF]


def unpack(*parts):
    return pl.pallas_call(
        unpack_kernel,
        out_shape=[sds((128, 2, FF), F32)] * 3,
        compiler_params=params(12),
        cost_estimate=cost(2),
        name="unpack",
    )(*parts)


def qkv_grads_kernel(s_ref, x0, x1, x2, x3, r_ref, w_ref, g_ref, second_ref, heads_ref,
                     own_ref, other_ref, gains_ref):
    core = s_ref[0]
    i = pl.program_id(0)

    @pl.when(i == 0)
    def _():
        gains_ref[...] = jnp.zeros_like(gains_ref)
        gains_ref[8:9, :] = heads_ref[...]

    gains_ref[pl.ds(4 + i, 1), :] = second_ref[...]
    a, b = s_ref[1], s_ref[2]
    o = jnp.zeros((256, 256), F32)
    for ref, d in zip((x0, x1, x2, x3), (1, 3, 2, 0)):
        at = ((a - d) & 3) * 2
        both = jnp.concatenate([r_ref[at + (b ^ 1)], r_ref[at + b]], 0)
        o = o + dot(ref[...].reshape(256, 256), both, TN)
    first = jnp.sum(o * w_ref[...].astype(F32), axis=1, keepdims=True)
    gains_ref[pl.ds(i, 1), :] = jnp.broadcast_to(first, (256, 128)).T[:1]
    o = o * g_ref[...]
    own_ref[...] = jnp.where(core == 0, o[:, :128], o[:, 128:])
    other_ref[...] = jnp.where(core == 0, o[:, 128:], o[:, :128]).astype(BF)


def qkv_grads(marks, x, r, w, gain, second, heads):
    rows = lambda m: pl.BlockSpec((256, m), lambda i, s: (i, 0))
    return pl.pallas_call(
        qkv_grads_kernel,
        grid_spec=pltpu.PrefetchScalarGridSpec(
            num_scalar_prefetch=1,
            grid=(4,),
            in_specs=[pl.BlockSpec((2, 128, 256), lambda i, s: (0, 0, i))] * 4 + [whole(8, 128, 256),
                      rows(256), rows(1), pl.BlockSpec((1, 256), lambda i, s: (0, i)), whole(1, 256)],
            out_specs=[rows(128), rows(128), whole(16, 256)],
        ),
        out_shape=[sds((D, 128), F32), sds((D, 128), BF), sds((16, 256), F32)],
        compiler_params=params(56),
        cost_estimate=cost(4),
        name="qkv_grads",
    )(marks, *x, r, w, gain, second, heads)


def add_gains_kernel(own_ref, got_ref, raw_ref, out_ref):
    parts = three(own_ref[...] + got_ref[...])
    k = pl.program_id(0)
    part = jnp.where(k == 0, parts[0], jnp.where(k == 1, parts[1], parts[2]))
    for j in range(8):
        out_ref[j] = part.astype(BF)


def add_gains(own, got, raw):
    return pl.pallas_call(
        add_gains_kernel,
        grid=(3,),
        in_specs=[whole(16, 256), whole(16, 256), pl.BlockSpec(memory_space=pl.ANY)],
        out_specs=pl.BlockSpec((8, 16, 256), lambda i: (0, 8 + i, 0)),
        out_shape=sds((8, 176, 256), BF),
        input_output_aliases={2: 0},
        compiler_params=params(56),
        cost_estimate=cost(1),
        name="add_gains",
    )(own, got, raw)


def write_gains(ref, at, gains):
    for k, part in enumerate(three(gains)):
        ref[at + 16 * k : at + 16 * k + 16, :] = part.astype(BF)


def read_gains(ref, at):
    g = ref[at : at + 16, :].astype(F32) + ref[at + 16 : at + 32, :].astype(F32)
    return g + ref[at + 32 : at + 48, :].astype(F32)


def out_grads_kernel(s_ref, h0, h1, h2, h3, j_ref, own_ref, other_ref):
    core, a, b = s_ref[0], s_ref[1], s_ref[2]
    acc = jnp.zeros((D, 128), F32)
    for ref, d in zip((h0, h1, h2, h3), (1, 3, 2, 0)):
        at = ((a - d) & 3) * 2
        both = jnp.concatenate([j_ref[at + (b ^ 1)], j_ref[at + b]], 0)
        acc = acc + dot(ref[...].reshape(256, D), both, TN)
    swapped = pltpu.roll(acc, 64, 1)
    low = lax.broadcasted_iota(jnp.int32, (D, 128), 1) < 64
    own_ref[...] = jnp.where(low, jnp.where(core == 0, acc, swapped), 0.0)
    other_ref[...] = jnp.where(low, jnp.where(core == 0, swapped, acc), 0.0).astype(BF)


def out_grads(marks, pieces, joined):
    return pl.pallas_call(
        out_grads_kernel,
        grid_spec=pltpu.PrefetchScalarGridSpec(
            num_scalar_prefetch=1,
            grid=(1,),
            in_specs=[whole(2, 128, D)] * 4 + [whole(8, 128, 128)],
            out_specs=[whole(D, 128), whole(D, 128)],
        ),
        out_shape=[sds((D, 128), F32), sds((D, 128), BF)],
        compiler_params=params(56),
        cost_estimate=cost(3),
        name="out_grads",
    )(marks, *pieces, joined)


def pair_parts_kernel(s_ref, q_ref, o_ref, got_ref, keep_ref, msg_ref):
    a, b = s_ref[3], s_ref[4]

    def rows(chunk):
        at = pl.ds(pl.multiple_of(chunk * 128, 128), 128)
        return jnp.concatenate([q_ref[at, :], o_ref[at, :]], 1) + got_ref[at, :].astype(F32)

    for i, d in enumerate((1, 3, 2, 0)):
        at = ((a + d) & 3) * 2
        keep_ref[i] = rows(at + b)
        msg_ref[i] = rows(at + (b ^ 1)).astype(BF)


def pair_parts(marks, own_q, own_o, got):
    return pl.pallas_call(
        pair_parts_kernel,
        grid_spec=pltpu.PrefetchScalarGridSpec(
            num_scalar_prefetch=1,
            grid=(1,),
            in_specs=[whole(D, 128), whole(D, 128), whole(D, 256)],
            out_specs=[whole(4, 128, 256)] * 2,
        ),
        out_shape=[sds((4, 128, 256), F32), sds((4, 128, 256), BF)],
        compiler_params=params(56),
        cost_estimate=cost(2),
        name="pair_parts",
    )(marks, own_q, own_o, got)


def sum_gains_kernel(raw_ref, out_ref):
    @pl.when(pl.program_id(0) == 0)
    def _():
        out_ref[...] = jnp.zeros_like(out_ref)

    t = raw_ref[0].astype(F32)
    for j in range(1, 8):
        t = t + raw_ref[j].astype(F32)
    out_ref[...] += t


def sum_gains(raw):
    return pl.pallas_call(
        sum_gains_kernel,
        grid=(3,),
        in_specs=[pl.BlockSpec((8, 16, 256), lambda i: (0, 8 + i, 0))],
        out_specs=whole(16, 256),
        out_shape=sds((16, 256), F32),
        compiler_params=params(56),
        cost_estimate=cost(1),
        name="sum_gains",
    )(raw)


def ring_parts_kernel(keep_ref, got_ref, gains_ref, more_ref, own_ref, out_ref, m1, m3, m2):
    gains = gains_ref[...] + more_ref[...]
    out_ref[...] = gains
    for i, ref in enumerate((m1, m3, m2)):
        ref[:128, :] = (keep_ref[i] + got_ref[i].astype(F32)).astype(BF)
        write_gains(ref, 128, gains)
    own_ref[...] = keep_ref[3] + got_ref[3].astype(F32)


def ring_parts(keep, got, gains, more):
    return pl.pallas_call(
        ring_parts_kernel,
        out_shape=[sds((128, 256), F32), sds((16, 256), F32)] + [sds((176, 256), BF)] * 3,
        compiler_params=params(56),
        cost_estimate=cost(2),
        name="ring_parts",
    )(keep, got, gains, more)


def last_parts_kernel(own_ref, gains_ref, m1, m3, m2, qkv_ref, out_ref, sum_ref):
    t = own_ref[...]
    gains = gains_ref[...]
    for ref in (m1, m3, m2):
        t = t + ref[:128, :].astype(F32)
        gains = gains + read_gains(ref, 128)
    sum_ref[...] = gains
    qkv_ref[...] = t[:, :128]
    out_ref[...] = t[:, 128:].T[:64]


def last_parts(own, gains, got):
    return pl.pallas_call(
        last_parts_kernel,
        out_shape=[sds((128, 128), F32), sds((64, 128), F32), sds((16, 256), F32)],
        compiler_params=params(56),
        cost_estimate=cost(2),
        name="last_parts",
    )(own, gains, *got)


def body(tokens, cotangent, deal_order, lengths, routes, route_gates, gain_first, gain_second, gain_query, gain_key,
         weight_qkv, weight_out, weight_gate, weight_up, weight_down):
    col = lax.axis_index("col")
    core = col % 2
    a, b = place("col")
    ra, rb = place("row")
    order = [(a + d) % 4 for d in (1, 3, 2, 0)]
    row_order = [(ra + d) % 4 for d in (1, 3, 2, 0)]
    back = [(a - d) % 4 for d in (1, 3, 2, 0)]
    marks = jnp.stack([core, a, b, ra, rb, 1 - core, col, core] + order + row_order + back).astype(jnp.int32)
    planes = [[i for i in range(16) if i % 2 == k] for k in range(2)]
    swap_all = partial(lax.all_to_all, axis_name="col", split_axis=0, concat_axis=0, tiled=True,
                       axis_index_groups=planes)

    extra = jnp.concatenate([routes.T.astype(BF)] + [p.T.astype(BF) for p in three(route_gates)], 1)
    cot = jnp.concatenate([cotangent, jnp.pad(extra, ((0, 8), (0, 512)))], 0)
    wide = jnp.concatenate([w.reshape(128, 2 * FF) for w in (weight_gate, weight_up, weight_down)], 1).astype(BF)

    qkv_low = weight_qkv.astype(BF)
    near, qkv_pair, wide, cot = together(step_pair(tokens, "col"), step_core(qkv_low), wide, cot)
    small = jnp.concatenate([qkv_low, qkv_pair, weight_out.astype(BF), jnp.zeros((128, 64), BF)], 1)
    small_pair = step_pair(small, "row")
    cot_near = step_pair(cot, "col")
    x_pieces = gather_rest(near, tokens, "col")
    w_all = lax.all_gather(wide, "row", axis=0, tiled=True)
    w_chip, w_scaled, qkv_t, out_t = place_small(marks, gather_rest(small_pair, small, "row"), gain_first[None])
    out_near = step_pair(out_t, "col")

    inverse, segment, offset = places(marks, lengths, deal_order.reshape(16, 128))
    frequency = THETA ** (-(jnp.arange(128) % 32).astype(F32) * 2.0 / HEAD)
    angles = offset * frequency[None, None, :]
    cos, sin = jnp.cos(angles), jnp.sin(angles)
    gains = jnp.concatenate([gain_query, gain_query, gain_key, jnp.ones((HEAD,), F32)])[None, :]

    out_near, w_scaled, cos, sin, segment, gain_column, *x_pieces = together(
        out_near, w_scaled, cos, sin, segment, gain_first[:, None], *x_pieces)
    both = gather_rest(jnp.concatenate([cot_near, out_near], 0), jnp.concatenate([cot, out_t], 0), "col")
    q0, q1, kv, raw, f1_all = project_heads(
        marks, x_pieces, w_scaled, gains, cos, sin, segment)
    kv_sib = step_core(kv)
    joined, logs = attend(q0, q1, kv, kv_sib)
    joined_got = swap_all(joined)
    joined_got, *both = together(joined_got, *both)
    out_own = [v[:, 144:] for v in both]
    out_sib = step_core(jnp.stack(out_own))
    hidden, middle, wout_t = after_attention(marks, joined_got, out_own, out_sib, tokens, gain_second[None])
    mid_pair = step_pair(middle, "col")
    hidden, *both = together(hidden, *both)
    cot_own = jnp.stack([v[:, :144] for v in both])
    cot_sib = step_core(cot_own)
    gates = given_gates(marks, cot_own, cot_sib, inverse).reshape(4, 2, 2, 8, 128)
    pre0, pre1, cot0, cot1 = inner_products(cot_own, cot_sib, w_all)
    own0 = jnp.stack([mid_pair, middle])
    near0, far0 = step_ring(own0, "col", 1), step_ring(own0, "col", 3)
    near0, far0, own0, gates, pre0 = together(near0, far0, own0, gates, pre0)
    last0 = step_ring(own0, "col", 2)
    part = run_experts(marks, 0, jnp.stack([near0, far0, own0]), pre0, gates, w_all, lambda i: i + i // 2)
    last0, *part = together(last0, *part)
    mid0 = jnp.stack([near0, far0, last0, own0])
    mid1 = step_core(mid0)
    qkv_t, mid0 = together(qkv_t, mid0)
    wqkv_t = lax.all_gather(qkv_t, "col", axis=0, tiled=True)

    mid1, *part = together(mid1, *part)
    e_other, gg1, ug1, in1 = run_experts(marks, 5, mid1, pre1, gates, w_all)
    last0, e_other = together(last0, e_other)
    e_own, gg0, ug0, in0 = run_experts(marks, 0, last0[None], pre0, gates, w_all, lambda i: i + 2, part)
    entry = add_pair(e_own, step_core(e_other))
    entry, gg0 = together(entry, gg0)
    entry_got = swap_all(entry)
    in1, entry = together(in1, entry)
    r_other = results(marks, in1, w_all)
    grads = weight_grads(((mid0, mid1), (gg0, gg1)), ((mid0, mid1), (ug0, ug1)), ((cot0, cot1), (in0, in1)))

    entry_got, grads, r_other = together(entry_got, grads, r_other)
    r_got = step_core(r_other)
    grads = lax.psum_scatter(grads, "row", scatter_dimension=0, tiled=True)
    hidden_grad, hidden_low, joined_grad, second = second_back(entry_got, hidden, cotangent, gain_second[None], wout_t)
    joined_grad, in0 = together(joined_grad, in0)
    joined_grad = swap_all(joined_grad)
    r_sum = results(marks, in0, w_all, r_got).reshape(8, 128, D)
    hidden_near, r_sum = together(step_pair(hidden_low, "col"), r_sum)
    hidden_pair = jnp.stack([hidden_near, hidden_low])
    joined_grad, r_sum, hidden_pair = together(joined_grad, r_sum, hidden_pair)
    hidden_pieces = [step_ring(hidden_pair, "col", d) for d in AHEAD] + [hidden_pair]
    dq, dkv_own, dkv_other = attend_back(q0, q1, kv, kv_sib, joined, logs, joined_grad)
    dkv_got = step_core(dkv_other)
    raw_grad, raw_scaled, gain_heads = heads_back(dq, dkv_own, dkv_got, raw, f1_all, gains, cos, sin)
    raw_scaled, *hidden_pieces = together(raw_scaled, *hidden_pieces)
    own_q, other_q, sums = qkv_grads(
        marks, x_pieces, raw_scaled, w_chip, gain_column, second, gain_heads)
    sums_got = step_core(sums)
    own_o, other_o = out_grads(marks, hidden_pieces, joined)
    raw_got = swap_all(add_gains(sums, sums_got, raw_grad))
    keep, msg = pair_parts(marks, own_q, own_o, step_core(jnp.concatenate([other_q, other_o], 1)))
    msg_got = step_pair(msg, "row")
    sums = sum_gains(raw_got)
    raw_got, r_sum, msg_got, sums_got = together(raw_got, r_sum, msg_got, step_pair(sums, "row"))
    out_got = swap_all(r_sum)
    own, sums, *msgs = ring_parts(keep, msg_got, sums, sums_got)
    input_grad = first_back(raw_got, wqkv_t, tokens, gain_first[None], hidden_grad)
    input_grad, grads, *msgs = together(
        input_grad, grads, *[step_ring(m, "row", d) for m, d in zip(msgs, AHEAD)])
    grads_w = unpack(grads)
    grad_qkv, grad_out, sums = last_parts(own, sums, msgs)
    out_got, grad_qkv = together(out_got, grad_qkv)
    block_out = add_up(hidden, out_got)
    heads = sums[8]
    return (
        block_out,
        input_grad,
        sums[:4].reshape(-1),
        sums[4:8].reshape(-1),
        heads[:64] + heads[64:128],
        heads[128:192],
        grad_qkv,
        grad_out.T,
        *grads_w,
    )


def solution(mesh):
    both = P(("row", "col"), None)
    return jax.shard_map(
        body,
        mesh=mesh,
        in_specs=(both, both, P("row", None), P("row", None), both, both, P(), P(), P(), P(),
                  P("row", "col"), P("row", "col"), P("row", "col", None), P("row", "col", None),
                  P("row", "col", None)),
        out_specs=(both, both, P(), P(), P(), P(), P("row", "col"), P("row", "col"), P("row", "col", None),
                   P("row", "col", None), P("row", "col", None)),
        check_vma=False,
    )
```

```python
from functools import partial

import jax
import jax.numpy as jnp
import numpy as np
from jax import lax
from jax.experimental import pallas as pl
from jax.experimental.pallas import tpu as pltpu
from jax.sharding import PartitionSpec as P

D = 1024
HEAD = 64
EXPERTS = 32
FF = 512
TOP = 8
TOK = 128
GROUP = 2048
PLANE = 1024
EPS_WIDE = 1e-05
EPS_HEAD = 1e-06
THETA = 10000.0
LOG2E = 1.4426950408889634
LN2 = 0.6931471805599453
QSCALE = LOG2E * HEAD**-0.5
APART = -256.0
BF = jnp.bfloat16
F32 = jnp.float32
NT = (((1,), (1,)), ((), ()))
TN = (((0,), (0,)), ((), ()))
HIGH = lax.Precision.HIGHEST


def params(mib=56):
    return pltpu.CompilerParams(vmem_limit_bytes=mib * 2**20)


def cost(us, scale=0.02):
    us = us * scale
    return pl.CostEstimate(flops=int(us * 1e9), bytes_accessed=int(us * 1e6), transcendentals=0)


def dot(a, b, dims=None):
    if dims is None:
        dims = (((1,), (0,)), ((), ()))
    return lax.dot_general(a, b, dims, preferred_element_type=F32)


def sds(shape, kind):
    return jax.ShapeDtypeStruct(shape, kind)


def whole(*shape):
    return pl.BlockSpec(shape, lambda *_: (0,) * len(shape))


def together(*values):
    return lax.optimization_barrier(values)


AHEAD = (1, 3, 2)


def step_pair(v, axis):
    if axis == "row":
        route = [(i, i ^ 1) for i in range(8)]
    else:
        route = [(i, i ^ 2) for i in range(16)]
    return lax.ppermute(v, axis, route)


def step_ring(v, axis, d):
    if axis == "row":
        route = [(i, (i + 2 * d) % 8) for i in range(8)]
    else:
        route = [(i, (i + 4 * d) % 16) for i in range(16)]
    return lax.ppermute(v, axis, route)


def step_core(v):
    return lax.ppermute(v, "col", [(i, i ^ 1) for i in range(16)])


def place(axis):
    i = lax.axis_index(axis)
    if axis == "col":
        i = i // 2
    return i // 2, i % 2


def gather_rest(pair, v, axis):
    pair = jnp.stack([pair, v])
    return [step_ring(pair, axis, d) for d in AHEAD] + [pair]


def gather_plain(v, axis):
    return gather_rest(step_pair(v, axis), v, axis)


def added(terms):
    t = terms[0].astype(F32)
    for r in terms[1:]:
        t = t + r.astype(F32)
    return t


def places_kernel(s_ref, l_ref, deal_ref, inv_ref, seg_ref, off_ref):
    core = s_ref[0]
    row = lax.broadcasted_iota(jnp.int32, (128, 128), 0)
    lane = lax.broadcasted_iota(jnp.int32, (128, 128), 1)
    ends = [l_ref[0, 0]]
    for n in range(1, 4):
        ends.append(ends[-1] + l_ref[0, n])
    for k in range(16):
        found = jnp.zeros((128, 128), jnp.int32)
        for n in range(16):
            deal = jnp.broadcast_to(deal_ref[n : n + 1, :], (128, 128))
            found = jnp.where(deal == row + k * 128, lane + n * 128, found)
        slot = jnp.sum(found.astype(F32), axis=1, keepdims=True)
        inv_ref[k : k + 1, :] = jnp.broadcast_to(slot, (128, 128)).T[:1].astype(jnp.int32)
        slot = slot.astype(jnp.int32)
        seg = jnp.zeros((128, 1), jnp.int32)
        start = jnp.zeros((128, 1), jnp.int32)
        for end in ends:
            seg = seg + jnp.where(slot >= end, 1, 0)
            start = jnp.where(slot >= end, end, start)

        @pl.when(core == k % 2)
        def _():
            seg_ref[k // 2] = seg
            off_ref[k // 2] = (slot - start).astype(F32)


def places(marks, lengths, deal):
    return pl.pallas_call(
        places_kernel,
        grid_spec=pltpu.PrefetchScalarGridSpec(
            num_scalar_prefetch=2,
            grid=(1,),
            in_specs=[whole(16, 128)],
            out_specs=[whole(16, 128), whole(8, 128, 1), whole(8, 128, 1)],
        ),
        out_shape=[sds((16, 128), jnp.int32), sds((8, 128, 1), jnp.int32), sds((8, 128, 1), F32)],
        compiler_params=params(56),
        cost_estimate=cost(3),
        name="places",
    )(marks, lengths, deal)


def head_sums():
    i = np.arange(256) // HEAD
    return jnp.asarray((i[:, None] == i[None, :]) / HEAD, BF)


def spread():
    s = np.zeros((256, 512), np.float32)
    for h in range(4):
        for i in range(64):
            s[h * 64 + i, h * 128 + i] = 1.0
    return jnp.asarray(s, BF)


def exact_sums(v, sums):
    hi = v.astype(BF)
    lo = (v - hi.astype(F32)).astype(BF)
    return dot(hi, sums) + dot(lo, sums)


def half_turn(v, lane):
    back = jnp.concatenate([pltpu.roll(v[:, :128], 96, 1), pltpu.roll(v[:, 128:], 96, 1)], 1)
    ahead = jnp.concatenate([pltpu.roll(v[:, :128], 32, 1), pltpu.roll(v[:, 128:], 32, 1)], 1)
    return jnp.where(lane % 64 < 32, -back, ahead)


def wide_tables(c, s, lane):
    c = jnp.where(lane < 192, jnp.concatenate([c, c], 1), 1.0)
    s = jnp.where(lane < 192, jnp.concatenate([s, s], 1), 0.0)
    return c, s


def heads_kernel(s_ref, x0, x1, x2, x3, w_ref, g_ref, c_ref, s_tab_ref, seg_ref, bd_ref, sp_ref,
                 q0_ref, q1_ref, kv_ref, raw_ref, f_ref):
    a, b = s_ref[1], s_ref[2]
    lane = lax.broadcasted_iota(jnp.int32, (256, 256), 1)
    l1 = lax.broadcasted_iota(jnp.int32, (256, 128), 1)
    inseg = (l1 >= 64) & (l1 < 68)
    aug_v = jnp.where((l1 >= 64) & (l1 < 67), 1.0, 0.0)
    for ref, d in zip((x0, x1, x2, x3), (1, 3, 2, 0)):
        at = ((a - d) & 3) * 2
        blocks = (at + (b ^ 1), at + b)

        def both(r):
            return jnp.concatenate([r[blocks[0]], r[blocks[1]]], 0)

        def put(r, v):
            r[blocks[0]] = v[:128]
            r[blocks[1]] = v[128:]

        x = ref[...].reshape(256, D)
        xf = x.astype(F32)
        f = lax.rsqrt(jnp.mean(xf * xf, axis=1, keepdims=True) + EPS_WIDE)
        raw = dot(x, w_ref[...]) * f
        put(raw_ref, raw)
        put(f_ref, f)
        fac = jnp.where(lane < 192, lax.rsqrt(exact_sums(raw * raw, bd_ref[...]) + EPS_HEAD), 1.0)
        h = raw * fac * g_ref[...]
        c, s = wide_tables(both(c_ref), both(s_tab_ref), lane)
        t = h * c + half_turn(h, lane) * s
        t = jnp.where(lane < 128, t * QSCALE, t).astype(BF)
        wide = dot(t, sp_ref[...])
        same = (l1 - 64) == both(seg_ref)
        aug_q = jnp.where(inseg & jnp.logical_not(same), APART, 0.0)
        aug_k = jnp.where((inseg & same) | ((l1 >= 68) & (l1 < 71)), 1.0, 0.0)
        put(q0_ref, (wide[:, 0:128] + aug_q).astype(BF))
        put(q1_ref, (wide[:, 128:256] + aug_q).astype(BF))
        put(kv_ref.at[0], (wide[:, 256:384] + aug_k).astype(BF))
        put(kv_ref.at[1], (wide[:, 384:512] + aug_v).astype(BF))


def project_heads(marks, pieces, w, gains, cos, sin, seg):
    return pl.pallas_call(
        heads_kernel,
        grid_spec=pltpu.PrefetchScalarGridSpec(
            num_scalar_prefetch=1,
            grid=(1,),
            in_specs=[whole(2, 128, D)] * 4 + [whole(D, 256), whole(1, 256), whole(8, 128, 128), whole(8, 128, 128),
                                               whole(8, 128, 1), whole(256, 256), whole(256, 512)],
            out_specs=[whole(8, 128, 128)] * 2 + [whole(2, 8, 128, 128), whole(8, 128, 256), whole(8, 128, 1)],
        ),
        out_shape=[sds((8, 128, 128), BF)] * 2 + [sds((2, 8, 128, 128), BF), sds((8, 128, 256), F32),
                                                  sds((8, 128, 1), F32)],
        compiler_params=params(32),
        cost_estimate=cost(7),
        name="project_heads",
    )(marks, *pieces, w, gains, cos, sin, seg, head_sums(), spread())


WIDE = 512


def attend_kernel(q0_ref, q1_ref, own_ref, sib_ref, o_ref, l_ref):
    q = jnp.concatenate([q0_ref[...].reshape(WIDE, 128), q1_ref[...].reshape(WIDE, 128)], 0)
    acc = jnp.zeros((128, 2 * WIDE), F32)
    for ref in (own_ref, sib_ref):
        p = jnp.exp2(dot(ref[0], q, NT)).astype(BF)
        acc = acc + dot(ref[1], p, TN)
    acc = acc.T
    total = acc[:, 64:65]
    o = acc / total
    l_ref[...] = jnp.log2(total).reshape(2, 4, 128, 1)
    lane = lax.broadcasted_iota(jnp.int32, (WIDE, 128), 1)
    o = jnp.where(lane < 64, o[:WIDE], pltpu.roll(o[WIDE:], 64, 1))
    o_ref[...] = o.astype(BF).reshape(4, 128, 128)


def four(n, m):
    return pl.BlockSpec((4, n, m), lambda j: (j, 0, 0))


def two_four(n, m):
    return pl.BlockSpec((2, 4, n, m), lambda j: (0, j, 0, 0))


def attend(q0, q1, own, sib):
    return pl.pallas_call(
        attend_kernel,
        grid=(2,),
        in_specs=[four(128, 128), four(128, 128), whole(2, PLANE, 128), whole(2, PLANE, 128)],
        out_specs=[four(128, 128), two_four(128, 1)],
        out_shape=[sds((8, 128, 128), BF), sds((2, 8, 128, 1), F32)],
        compiler_params=params(24),
        cost_estimate=cost(7),
        name="attend",
    )(q0, q1, own.reshape(2, PLANE, 128), sib.reshape(2, PLANE, 128))


def three(v):
    hi = v.astype(BF).astype(F32)
    mid = (v - hi).astype(BF).astype(F32)
    return hi, mid, v - hi - mid


def attend_back_kernel(q0_ref, q1_ref, kvo_ref, kvs_ref, o_ref, l_ref, g_ref,
                       dq_ref, own_ref, other_ref, dk_ref, dv_ref):
    @pl.when(pl.program_id(0) == 0)
    def _():
        dk_ref[...] = jnp.zeros_like(dk_ref)
        dv_ref[...] = jnp.zeros_like(dv_ref)

    lane = lax.broadcasted_iota(jnp.int32, (2 * WIDE, 128), 1)
    q = jnp.concatenate([q0_ref[...].reshape(WIDE, 128), q1_ref[...].reshape(WIDE, 128)], 0)
    h0, h1, h2 = three(l_ref[...].reshape(2 * WIDE, 1))
    ql = jnp.where(lane == 68, -h0, jnp.where(lane == 69, -h1, jnp.where(lane == 70, -h2, q.astype(F32))))
    ql = ql.astype(BF)
    g = g_ref[...].reshape(WIDE, 128).astype(F32)
    o = o_ref[...].reshape(WIDE, 128).astype(F32)
    g = jnp.concatenate([g, pltpu.roll(g, 64, 1)], 0)
    o = jnp.concatenate([o, pltpu.roll(o, 64, 1)], 0)
    g = jnp.where(lane < 64, g, 0.0)
    centre = jnp.sum(g * o, axis=1, keepdims=True)
    c0, c1, c2 = three(centre)
    gl = jnp.where(lane == 64, -c0, jnp.where(lane == 65, -c1, jnp.where(lane == 66, -c2, g)))
    gl = gl.astype(BF)
    gb = g.astype(BF)
    dq = jnp.zeros((128, 2 * WIDE), F32)
    for j in range(GROUP // WIDE):
        rows = pl.ds(j * WIDE, WIDE)
        ref = kvo_ref if j * WIDE < PLANE else kvs_ref
        part = pl.ds(j * WIDE % PLANE, WIDE)
        k = ref[0, part, :]
        pt = jnp.exp2(dot(k, ql, NT))
        ds = (pt * dot(ref[1, part, :], gl, NT)).astype(BF)
        dv_ref[rows, :] += dot(pt.astype(BF), gb)
        dk_ref[rows, :] += dot(ds, q)
        dq = dq + dot(k, ds, TN)
    dq_ref[...] = dq.T.reshape(2, 4, 128, 128)

    @pl.when(pl.program_id(0) == 1)
    def _():
        low = lax.broadcasted_iota(jnp.int32, (128, 128), 1) < 64

        def block(j):
            rows = pl.ds(j * 128, 128)
            return jnp.where(low, dk_ref[rows, :] * LN2, pltpu.roll(dv_ref[rows, :], 64, 1))

        for j in range(8):
            own_ref[j] = block(j)
            other_ref[j] = block(8 + j).astype(BF)


def attend_back(q0, q1, own, sib, o, l, g):
    kv = whole(2, PLANE, 128)
    return pl.pallas_call(
        attend_back_kernel,
        grid=(2,),
        in_specs=[four(128, 128), four(128, 128), kv, kv, four(128, 128), two_four(128, 1), four(128, 128)],
        out_specs=[two_four(128, 128), whole(8, 128, 128), whole(8, 128, 128)],
        out_shape=[sds((2, 8, 128, 128), F32), sds((8, 128, 128), F32), sds((8, 128, 128), BF)],
        scratch_shapes=[pltpu.VMEM((GROUP, 128), F32)] * 2,
        compiler_params=params(56),
        cost_estimate=cost(17),
        name="attend_back",
    )(q0, q1, own.reshape(2, PLANE, 128), sib.reshape(2, PLANE, 128), o, l, g)


def heads_back_kernel(dq_ref, own_ref, got_ref, raw_ref, f_ref, g_ref, c_ref, sin_ref, bd_ref,
                      out_ref, scaled_ref, gain_ref):
    @pl.when(pl.program_id(0) == 0)
    def _():
        gain_ref[...] = jnp.zeros_like(gain_ref)

    rows = WIDE
    lane1 = lax.broadcasted_iota(jnp.int32, (rows, 128), 1)
    dq = dq_ref[...].reshape(2 * rows, 128) * HEAD**-0.5
    dq = jnp.where(lane1 < 64, dq[:rows], pltpu.roll(dq[rows:], 64, 1))
    dkv = own_ref[...] + got_ref[...].astype(F32)
    d = jnp.concatenate([dq, dkv.reshape(rows, 128)], 1)
    raw = raw_ref[...].reshape(rows, 256)
    lane = lax.broadcasted_iota(jnp.int32, (rows, 256), 1)
    bd = bd_ref[...]
    fac = jnp.where(lane < 192, lax.rsqrt(exact_sums(raw * raw, bd) + EPS_HEAD), 1.0)
    hat = raw * fac
    c, s = wide_tables(c_ref[...].reshape(rows, 128), sin_ref[...].reshape(rows, 128), lane)
    dh = d * c - half_turn(d * s, lane)
    gain_ref[...] += jnp.sum(dh * hat, axis=0, keepdims=True)
    dn = dh * g_ref[...]
    back = fac * (dn - hat * exact_sums(dn * hat, bd))
    res = jnp.where(lane < 192, back, d)
    out_ref[:, :128] = res.astype(BF).reshape(4, 128, 256)
    scaled_ref[...] = (res * f_ref[...].reshape(rows, 1)).astype(BF).reshape(4, 128, 256)


def heads_back(dq, own, got, raw, f, gains, cos, sin):
    return pl.pallas_call(
        heads_back_kernel,
        grid=(2,),
        in_specs=[two_four(128, 128), four(128, 128), four(128, 128), four(128, 256), four(128, 1),
                  whole(1, 256), four(128, 128), four(128, 128), whole(256, 256)],
        out_specs=[four(128, 256), four(128, 256), whole(1, 256)],
        out_shape=[sds((8, 176, 256), BF), sds((8, 128, 256), BF), sds((1, 256), F32)],
        compiler_params=params(56),
        cost_estimate=cost(6),
        name="heads_back",
    )(dq, own, got, raw, f, gains, cos, sin, head_sums())


def norm_factor(v):
    return lax.rsqrt(jnp.mean(v * v, axis=1, keepdims=True) + EPS_WIDE)


def after_attention_kernel(s_ref, j_ref, *refs):
    own, sib = refs[0:4], refs[4]
    x_ref, g_ref, hidden_ref, middle_ref, w_ref = refs[5:]
    core, a, b = s_ref[0], s_ref[1], s_ref[2]
    for i, d in enumerate((1, 3, 2, 0)):
        for r in range(2):
            chip = ((a - d) & 3) * 2 + (b ^ (1 - r))
            at = chip * 128 + core * 64
            w_ref[pl.ds(pl.multiple_of(at, 64), 64), :] = own[i][r]
            at = chip * 128 + (1 - core) * 64
            w_ref[pl.ds(pl.multiple_of(at, 64), 64), :] = sib[i, r]
    hidden = x_ref[...].astype(F32)
    for j in range(8):
        hidden = hidden + dot(j_ref[j], w_ref[j * 128 : j * 128 + 128, :])
    hidden_ref[...] = hidden
    middle_ref[...] = (hidden * norm_factor(hidden) * g_ref[...]).astype(BF)


def after_attention(marks, joined, own, sib, x, gain):
    return pl.pallas_call(
        after_attention_kernel,
        grid_spec=pltpu.PrefetchScalarGridSpec(
            num_scalar_prefetch=1,
            grid=(1,),
            in_specs=[whole(8, 128, 128)] + [whole(2, 64, D)] * 4 + [whole(4, 2, 64, D), whole(128, D), whole(1, D)],
            out_specs=[whole(128, D), whole(128, D), whole(D, D)],
        ),
        out_shape=[sds((128, D), F32), sds((128, D), BF), sds((D, D), BF)],
        compiler_params=params(24),
        cost_estimate=cost(3),
        name="after_attention",
    )(marks, joined, *own, sib, x, gain)


def second_back_kernel(m_ref, hidden_ref, cot_ref, g_ref, w_ref, grad_ref, low_ref, joined_ref, gain_ref):
    mg = m_ref[0].astype(F32)
    for j in range(1, 8):
        mg = mg + m_ref[j].astype(F32)
    hidden = hidden_ref[...]
    f = norm_factor(hidden)
    hat = hidden * f
    gain_ref[...] = jnp.sum(mg * hat, axis=0, keepdims=True)
    dn = mg * g_ref[...]
    grad = cot_ref[...].astype(F32) + f * (dn - hat * jnp.mean(dn * hat, axis=1, keepdims=True))
    grad_ref[...] = grad
    low = grad.astype(BF)
    low_ref[...] = low
    joined = dot(low, w_ref[...], NT).astype(BF)
    for j in range(8):
        joined_ref[j] = joined[:, j * 128 : j * 128 + 128]


def second_back(chunks, hidden, cot, gain, w):
    return pl.pallas_call(
        second_back_kernel,
        out_shape=[sds((128, D), F32), sds((128, D), BF), sds((8, 128, 128), BF), sds((1, D), F32)],
        compiler_params=params(20),
        cost_estimate=cost(2),
        name="second_back",
    )(chunks, hidden, cot, gain, w)


def first_back_kernel(raw_ref, w_ref, x_ref, g_ref, grad_ref, out_ref):
    ng = dot(raw_ref[0, :128], w_ref[0:256, :])
    for j in range(1, 8):
        ng = ng + dot(raw_ref[j, :128], w_ref[j * 256 : j * 256 + 256, :])
    x = x_ref[...].astype(F32)
    f = norm_factor(x)
    hat = x * f
    dn = ng * g_ref[...]
    out_ref[...] = (grad_ref[...] + f * (dn - hat * jnp.mean(dn * hat, axis=1, keepdims=True))).astype(BF)


def first_back(raw, w, x, gain, grad):
    return pl.pallas_call(
        first_back_kernel,
        out_shape=sds((128, D), BF),
        compiler_params=params(24),
        cost_estimate=cost(2),
        name="first_back",
    )(raw, w, x, gain, grad)


def place_small_kernel(s_ref, p0, p1, p2, p3, g_ref, chip_ref, scaled_ref, qkv_ref, out_ref):
    core, a, b = s_ref[0], s_ref[3], s_ref[4]
    for ref, d in zip((p0, p1, p2, p3), (1, 3, 2, 0)):
        for r in range(2):
            at = pl.multiple_of((((a - d) & 3) * 2 + (b ^ (1 - r))) * 128, 128)
            v = ref[r]
            own, other = v[:, :128], v[:, 128:256]
            chip = jnp.where(core == 0, jnp.concatenate([own, other], 1), jnp.concatenate([other, own], 1))
            chip_ref[pl.ds(at, 128), :] = chip
            gain = jnp.broadcast_to(g_ref[:, pl.ds(at, 128)], (128, 128)).T
            gain = jnp.concatenate([gain, gain], 1)
            scaled_ref[pl.ds(at, 128), :] = (chip.astype(F32) * gain).astype(BF)
            qkv_ref[:, pl.ds(at, 128)] = own.astype(F32).T.astype(BF)
            out_ref[:, pl.ds(at, 128)] = v[:, 256:].astype(F32).T[:64].astype(BF)


def place_small(marks, pieces, gain):
    return pl.pallas_call(
        place_small_kernel,
        grid_spec=pltpu.PrefetchScalarGridSpec(
            num_scalar_prefetch=1,
            grid=(1,),
            in_specs=[whole(2, 128, 384)] * 4 + [whole(1, D)],
            out_specs=[whole(D, 256), whole(D, 256), whole(128, D), whole(64, D)],
        ),
        out_shape=[sds((D, 256), BF), sds((D, 256), BF), sds((128, D), BF), sds((64, D), BF)],
        compiler_params=params(56),
        cost_estimate=cost(2),
        name="place_small",
    )(marks, *pieces, gain)


def given_gates_kernel(s_ref, own_ref, sib_ref, inv_ref, out_ref, dealt):
    core, a, b = s_ref[0], s_ref[1], s_ref[2]
    row = lax.broadcasted_iota(jnp.int32, (8, 128), 0)
    for ref, side in ((own_ref, core), (sib_ref, 1 - core)):
        for i, d in enumerate((1, 3, 2, 0)):
            for r in range(2):
                ex = ref[i, r].astype(F32)
                names = ex[:8, 0:128]
                values = ex[:8, 128:256] + ex[:8, 256:384] + ex[:8, 384:512]
                both = jnp.zeros((8, 128), F32)
                for e in range(2):
                    mine = (s_ref[6] * 2 + e).astype(F32)
                    g = jnp.sum(jnp.where(names == mine, values, 0.0), axis=0, keepdims=True)
                    both = jnp.where(row == e, g, both)
                dealt[((a - d) & 3) * 4 + (b ^ (1 - r)) * 2 + side] = both
    for n in range(16):
        slot = jnp.broadcast_to(inv_ref[n : n + 1, :], (8, 128))
        at, of = slot & 127, slot >> 7
        got = jnp.zeros((8, 128), F32)
        for k in range(16):
            got = jnp.where(of == k, jnp.take_along_axis(dealt[k], at, axis=1), got)
        out_ref[n] = got


def given_gates(marks, own, sib, inverse):
    extra = pl.BlockSpec((4, 2, 16, D), lambda i, s: (0, 0, 8, 0))
    return pl.pallas_call(
        given_gates_kernel,
        grid_spec=pltpu.PrefetchScalarGridSpec(
            num_scalar_prefetch=1,
            grid=(1,),
            in_specs=[extra, extra, whole(16, 128)],
            out_specs=whole(16, 8, 128),
            scratch_shapes=[pltpu.VMEM((16, 8, 128), F32)],
        ),
        out_shape=sds((16, 8, 128), F32),
        compiler_params=params(56),
        cost_estimate=cost(2),
        name="given_gates",
    )(marks, own, sib, inverse)


def inner_kernel(own_ref, sib_ref, w_ref, po_ref, ps_ref, co_ref, cs_ref):
    w = w_ref[...]
    for ref, p_ref, c_ref in ((own_ref, po_ref, co_ref), (sib_ref, ps_ref, cs_ref)):
        up = ref[0, :, :128]
        c_ref[0] = up
        p_ref[0] = dot(up.reshape(256, D), w).astype(BF).reshape(2, 128, D)


def inner_products(own, sib, w):
    side = pl.BlockSpec((1, 2, 144, D), lambda i: (i, 0, 0, 0))
    spec = pl.BlockSpec((1, 2, 128, D), lambda i: (i, 0, 0, 0))
    return pl.pallas_call(
        inner_kernel,
        grid=(4,),
        in_specs=[side, side, pl.BlockSpec((D, 2 * FF), lambda i: (0, 2))],
        out_specs=[spec] * 4,
        out_shape=[sds((4, 2, 128, D), BF)] * 4,
        compiler_params=params(56),
        cost_estimate=cost(8),
        name="inner_products",
    )(own, sib, w)


def experts_kernel(s_ref, mid_ref, pre_ref, g_ref, w_ref, *refs):
    entry_ref, gg_ref, ug_ref, in_ref = refs[-4:]
    mid = mid_ref[...].reshape(256, D)
    b = s_ref[2]
    gates = jnp.concatenate([g_ref[0, b ^ 1, 0].T, g_ref[0, b, 0].T], 0)
    entry = None
    for e in range(2):
        cg = slice(e * FF, e * FF + FF)
        cu = slice(1024 + e * FF, 1024 + e * FF + FF)
        gp = dot(mid, w_ref[:, cg])
        u = dot(mid, w_ref[:, cu])
        g = gates[:, e : e + 1]
        ig = pre_ref[0, :, :, cg].reshape(256, FF).astype(F32) * g
        sig = 0.5 * jnp.tanh(0.5 * gp) + 0.5
        act = gp * sig
        inner = (g * act * u).astype(BF)
        gg = (ig * u * (sig + act * (1.0 - sig))).astype(BF)
        ug = (ig * act).astype(BF)
        part = dot(gg, w_ref[:, cg], NT) + dot(ug, w_ref[:, cu], NT)
        entry = part if entry is None else entry + part
        for ref, v in ((in_ref, inner), (gg_ref, gg), (ug_ref, ug)):
            ref[0, :, :, cg] = v.reshape(2, 128, FF)
    entry = entry.astype(BF)
    entry_ref[0, b ^ 1] = entry[:128]
    entry_ref[0, b] = entry[128:]


def run_experts(marks, which, mid, pre, gates, w, pick=lambda i: i, before=()):
    hid = pl.BlockSpec((1, 2, 128, D), lambda i, s: (pick(i), 0, 0, 0))
    n = mid.shape[0]
    return pl.pallas_call(
        experts_kernel,
        grid_spec=pltpu.PrefetchScalarGridSpec(
            num_scalar_prefetch=1,
            grid=(n,),
            in_specs=[pl.BlockSpec((1, 2, 128, D), lambda i, s: (i, 0, 0, 0)), hid,
                      pl.BlockSpec((1, 2, 1, 8, 128), lambda i, s: (s[16 + pick(i)], 0, s[which], 0, 0)),
                      whole(D, 4 * FF)] + [pl.BlockSpec(memory_space=pl.ANY)] * len(before),
            out_specs=[pl.BlockSpec((1, 2, 128, D), lambda i, s: (s[16 + pick(i)], 0, 0, 0))] + [hid] * 3,
        ),
        out_shape=[sds((4, 2, 128, D), BF)] * 4,
        input_output_aliases={5 + k: k for k in range(len(before))},
        compiler_params=params(56),
        cost_estimate=cost(4 * n),
        name="run_experts",
    )(marks, mid, pre, gates, w, *before)


def add_pair_kernel(a_ref, b_ref, out_ref):
    out_ref[...] = (a_ref[...].astype(F32) + b_ref[...].astype(F32)).astype(BF)


def add_pair(a, b):
    spec = pl.BlockSpec((2, 128, D), lambda i: (i, 0, 0))
    return pl.pallas_call(
        add_pair_kernel,
        grid=(4,),
        in_specs=[spec, spec],
        out_specs=spec,
        out_shape=sds((8, 128, D), BF),
        compiler_params=params(8),
        cost_estimate=cost(2),
        name="add_pair",
    )(a.reshape(8, 128, D), b.reshape(8, 128, D))


def results_kernel(s_ref, in_ref, w_ref, *refs):
    b = s_ref[2]
    o = dot(in_ref[...].reshape(256, 2 * FF), w_ref[...], NT)
    for r in range(2):
        at = b ^ (1 - r)
        v = o[r * 128 : r * 128 + 128]
        if len(refs) == 2:
            v = v + refs[0][0, at].astype(F32)
        refs[-1][0, at] = v.astype(BF)


def results(marks, inner, w, got=None):
    hid = pl.BlockSpec((1, 2, 128, 2 * FF), lambda i, s: (i, 0, 0, 0))
    there = pl.BlockSpec((1, 2, 128, D), lambda i, s: (s[16 + i], 0, 0, 0))
    more = [] if got is None else [got]
    return pl.pallas_call(
        results_kernel,
        grid_spec=pltpu.PrefetchScalarGridSpec(
            num_scalar_prefetch=1,
            grid=(4,),
            in_specs=[hid, pl.BlockSpec((D, 2 * FF), lambda i, s: (0, 2))] + [there] * len(more),
            out_specs=there,
        ),
        out_shape=sds((4, 2, 128, D), BF),
        compiler_params=params(56),
        cost_estimate=cost(4),
        name="results",
    )(marks, inner, w, *more)


def add_up_kernel(h_ref, m_ref, out_ref):
    t = h_ref[...]
    for j in range(8):
        t = t + m_ref[j].astype(F32)
    out_ref[...] = t.astype(BF)


def add_up(hidden, chunks):
    return pl.pallas_call(
        add_up_kernel,
        out_shape=sds((128, D), BF),
        compiler_params=params(8),
        cost_estimate=cost(2),
        name="add_up",
    )(hidden, chunks)


def weights_kernel(*refs):
    out_ref = refs[-1]
    for n in range(len(refs) // 4):
        l0, l1, r0, r1 = refs[4 * n : 4 * n + 4]
        o = dot(l0[...].reshape(PLANE, 256), r0[...].reshape(PLANE, 1024), TN)
        o = o + dot(l1[...].reshape(PLANE, 256), r1[...].reshape(PLANE, 1024), TN)
        out_ref[:, n * 1024 : n * 1024 + 1024] = o.astype(BF)


def weight_grads(*sides):
    side = pl.BlockSpec((4, 2, 128, 256), lambda i: (0, 0, 0, i))
    hid = whole(4, 2, 128, 2 * FF)
    n = len(sides)
    return pl.pallas_call(
        weights_kernel,
        grid=(4,),
        in_specs=[side, side, hid, hid] * n,
        out_specs=pl.BlockSpec((256, n * 2 * FF), lambda i: (i, 0)),
        out_shape=sds((D, n * 2 * FF), BF),
        compiler_params=params(56),
        cost_estimate=cost(8 * n),
        name="weight_grads",
    )(*[v for left, right in sides for v in (*left, *right)])


def unpack_kernel(a_ref, g_ref, u_ref, d_ref):
    t = a_ref[...].astype(F32)
    for e in range(2):
        at = e * FF
        g_ref[:, e, :] = t[:, at : at + FF]
        u_ref[:, e, :] = t[:, 1024 + at : 1024 + at + FF]
        d_ref[:, e, :] = t[:, 2048 + at : 2048 + at + FF]


def unpack(*parts):
    return pl.pallas_call(
        unpack_kernel,
        out_shape=[sds((128, 2, FF), F32)] * 3,
        compiler_params=params(12),
        cost_estimate=cost(2),
        name="unpack",
    )(*parts)


def qkv_grads_kernel(s_ref, x0, x1, x2, x3, r_ref, w_ref, g_ref, second_ref, heads_ref,
                     own_ref, other_ref, gains_ref):
    core = s_ref[0]
    i = pl.program_id(0)

    @pl.when(i == 0)
    def _():
        gains_ref[...] = jnp.zeros_like(gains_ref)
        gains_ref[8:9, :] = heads_ref[...]

    gains_ref[pl.ds(4 + i, 1), :] = second_ref[...]
    a, b = s_ref[1], s_ref[2]
    o = jnp.zeros((256, 256), F32)
    for ref, d in zip((x0, x1, x2, x3), (1, 3, 2, 0)):
        at = ((a - d) & 3) * 2
        both = jnp.concatenate([r_ref[at + (b ^ 1)], r_ref[at + b]], 0)
        o = o + dot(ref[...].reshape(256, 256), both, TN)
    first = jnp.sum(o * w_ref[...].astype(F32), axis=1, keepdims=True)
    gains_ref[pl.ds(i, 1), :] = jnp.broadcast_to(first, (256, 128)).T[:1]
    o = o * g_ref[...]
    own_ref[...] = jnp.where(core == 0, o[:, :128], o[:, 128:])
    other_ref[...] = jnp.where(core == 0, o[:, 128:], o[:, :128]).astype(BF)


def qkv_grads(marks, x, r, w, gain, second, heads):
    rows = lambda m: pl.BlockSpec((256, m), lambda i, s: (i, 0))
    return pl.pallas_call(
        qkv_grads_kernel,
        grid_spec=pltpu.PrefetchScalarGridSpec(
            num_scalar_prefetch=1,
            grid=(4,),
            in_specs=[pl.BlockSpec((2, 128, 256), lambda i, s: (0, 0, i))] * 4 + [whole(8, 128, 256),
                      rows(256), rows(1), pl.BlockSpec((1, 256), lambda i, s: (0, i)), whole(1, 256)],
            out_specs=[rows(128), rows(128), whole(16, 256)],
        ),
        out_shape=[sds((D, 128), F32), sds((D, 128), BF), sds((16, 256), F32)],
        compiler_params=params(56),
        cost_estimate=cost(4),
        name="qkv_grads",
    )(marks, *x, r, w, gain, second, heads)


def add_gains_kernel(own_ref, got_ref, raw_ref, out_ref):
    parts = three(own_ref[...] + got_ref[...])
    k = pl.program_id(0)
    part = jnp.where(k == 0, parts[0], jnp.where(k == 1, parts[1], parts[2]))
    for j in range(8):
        out_ref[j] = part.astype(BF)


def add_gains(own, got, raw):
    return pl.pallas_call(
        add_gains_kernel,
        grid=(3,),
        in_specs=[whole(16, 256), whole(16, 256), pl.BlockSpec(memory_space=pl.ANY)],
        out_specs=pl.BlockSpec((8, 16, 256), lambda i: (0, 8 + i, 0)),
        out_shape=sds((8, 176, 256), BF),
        input_output_aliases={2: 0},
        compiler_params=params(56),
        cost_estimate=cost(1),
        name="add_gains",
    )(own, got, raw)


def write_gains(ref, at, gains):
    for k, part in enumerate(three(gains)):
        ref[at + 16 * k : at + 16 * k + 16, :] = part.astype(BF)


def read_gains(ref, at):
    g = ref[at : at + 16, :].astype(F32) + ref[at + 16 : at + 32, :].astype(F32)
    return g + ref[at + 32 : at + 48, :].astype(F32)


def out_grads_kernel(s_ref, h0, h1, h2, h3, j_ref, own_ref, other_ref):
    core, a, b = s_ref[0], s_ref[1], s_ref[2]
    acc = jnp.zeros((D, 128), F32)
    for ref, d in zip((h0, h1, h2, h3), (1, 3, 2, 0)):
        at = ((a - d) & 3) * 2
        both = jnp.concatenate([j_ref[at + (b ^ 1)], j_ref[at + b]], 0)
        acc = acc + dot(ref[...].reshape(256, D), both, TN)
    swapped = pltpu.roll(acc, 64, 1)
    low = lax.broadcasted_iota(jnp.int32, (D, 128), 1) < 64
    own_ref[...] = jnp.where(low, jnp.where(core == 0, acc, swapped), 0.0)
    other_ref[...] = jnp.where(low, jnp.where(core == 0, swapped, acc), 0.0).astype(BF)


def out_grads(marks, pieces, joined):
    return pl.pallas_call(
        out_grads_kernel,
        grid_spec=pltpu.PrefetchScalarGridSpec(
            num_scalar_prefetch=1,
            grid=(1,),
            in_specs=[whole(2, 128, D)] * 4 + [whole(8, 128, 128)],
            out_specs=[whole(D, 128), whole(D, 128)],
        ),
        out_shape=[sds((D, 128), F32), sds((D, 128), BF)],
        compiler_params=params(56),
        cost_estimate=cost(3),
        name="out_grads",
    )(marks, *pieces, joined)


def pair_parts_kernel(s_ref, q_ref, o_ref, got_ref, keep_ref, msg_ref):
    a, b = s_ref[3], s_ref[4]

    def rows(chunk):
        at = pl.ds(pl.multiple_of(chunk * 128, 128), 128)
        return jnp.concatenate([q_ref[at, :], o_ref[at, :]], 1) + got_ref[at, :].astype(F32)

    for i, d in enumerate((1, 3, 2, 0)):
        at = ((a + d) & 3) * 2
        keep_ref[i] = rows(at + b)
        msg_ref[i] = rows(at + (b ^ 1)).astype(BF)


def pair_parts(marks, own_q, own_o, got):
    return pl.pallas_call(
        pair_parts_kernel,
        grid_spec=pltpu.PrefetchScalarGridSpec(
            num_scalar_prefetch=1,
            grid=(1,),
            in_specs=[whole(D, 128), whole(D, 128), whole(D, 256)],
            out_specs=[whole(4, 128, 256)] * 2,
        ),
        out_shape=[sds((4, 128, 256), F32), sds((4, 128, 256), BF)],
        compiler_params=params(56),
        cost_estimate=cost(2),
        name="pair_parts",
    )(marks, own_q, own_o, got)


def sum_gains_kernel(raw_ref, out_ref):
    @pl.when(pl.program_id(0) == 0)
    def _():
        out_ref[...] = jnp.zeros_like(out_ref)

    t = raw_ref[0].astype(F32)
    for j in range(1, 8):
        t = t + raw_ref[j].astype(F32)
    out_ref[...] += t


def sum_gains(raw):
    return pl.pallas_call(
        sum_gains_kernel,
        grid=(3,),
        in_specs=[pl.BlockSpec((8, 16, 256), lambda i: (0, 8 + i, 0))],
        out_specs=whole(16, 256),
        out_shape=sds((16, 256), F32),
        compiler_params=params(56),
        cost_estimate=cost(1),
        name="sum_gains",
    )(raw)


def ring_parts_kernel(keep_ref, got_ref, gains_ref, more_ref, own_ref, out_ref, m1, m3, m2):
    gains = gains_ref[...] + more_ref[...]
    out_ref[...] = gains
    for i, ref in enumerate((m1, m3, m2)):
        ref[:128, :] = (keep_ref[i] + got_ref[i].astype(F32)).astype(BF)
        write_gains(ref, 128, gains)
    own_ref[...] = keep_ref[3] + got_ref[3].astype(F32)


def ring_parts(keep, got, gains, more):
    return pl.pallas_call(
        ring_parts_kernel,
        out_shape=[sds((128, 256), F32), sds((16, 256), F32)] + [sds((176, 256), BF)] * 3,
        compiler_params=params(56),
        cost_estimate=cost(2),
        name="ring_parts",
    )(keep, got, gains, more)


def last_parts_kernel(own_ref, gains_ref, m1, m3, m2, qkv_ref, out_ref, sum_ref):
    t = own_ref[...]
    gains = gains_ref[...]
    for ref in (m1, m3, m2):
        t = t + ref[:128, :].astype(F32)
        gains = gains + read_gains(ref, 128)
    sum_ref[...] = gains
    qkv_ref[...] = t[:, :128]
    out_ref[...] = t[:, 128:].T[:64]


def last_parts(own, gains, got):
    return pl.pallas_call(
        last_parts_kernel,
        out_shape=[sds((128, 128), F32), sds((64, 128), F32), sds((16, 256), F32)],
        compiler_params=params(56),
        cost_estimate=cost(2),
        name="last_parts",
    )(own, gains, *got)


def body(tokens, cotangent, deal_order, lengths, routes, route_gates, gain_first, gain_second, gain_query, gain_key,
         weight_qkv, weight_out, weight_gate, weight_up, weight_down):
    col = lax.axis_index("col")
    core = col % 2
    a, b = place("col")
    ra, rb = place("row")
    order = [(a + d) % 4 for d in (1, 3, 2, 0)]
    row_order = [(ra + d) % 4 for d in (1, 3, 2, 0)]
    back = [(a - d) % 4 for d in (1, 3, 2, 0)]
    marks = jnp.stack([core, a, b, ra, rb, 1 - core, col, core] + order + row_order + back).astype(jnp.int32)
    planes = [[i for i in range(16) if i % 2 == k] for k in range(2)]
    swap_all = partial(lax.all_to_all, axis_name="col", split_axis=0, concat_axis=0, tiled=True,
                       axis_index_groups=planes)

    extra = jnp.concatenate([routes.T.astype(BF)] + [p.T.astype(BF) for p in three(route_gates)], 1)
    cot = jnp.concatenate([cotangent, jnp.pad(extra, ((0, 8), (0, 512)))], 0)
    wide = jnp.concatenate([w.reshape(128, 2 * FF) for w in (weight_gate, weight_up, weight_down)], 1).astype(BF)

    qkv_low = weight_qkv.astype(BF)
    near, qkv_pair, wide, cot = together(step_pair(tokens, "col"), step_core(qkv_low), wide, cot)
    small = jnp.concatenate([qkv_low, qkv_pair, weight_out.astype(BF), jnp.zeros((128, 64), BF)], 1)
    small_pair = step_pair(small, "row")
    cot_near = step_pair(cot, "col")
    x_pieces = gather_rest(near, tokens, "col")
    w_all = lax.all_gather(wide, "row", axis=0, tiled=True)
    w_chip, w_scaled, qkv_t, out_t = place_small(marks, gather_rest(small_pair, small, "row"), gain_first[None])
    out_near = step_pair(out_t, "col")

    inverse, segment, offset = places(marks, lengths, deal_order.reshape(16, 128))
    frequency = THETA ** (-(jnp.arange(128) % 32).astype(F32) * 2.0 / HEAD)
    angles = offset * frequency[None, None, :]
    cos, sin = jnp.cos(angles), jnp.sin(angles)
    gains = jnp.concatenate([gain_query, gain_query, gain_key, jnp.ones((HEAD,), F32)])[None, :]

    out_near, w_scaled, cos, sin, segment, gain_column, *x_pieces = together(
        out_near, w_scaled, cos, sin, segment, gain_first[:, None], *x_pieces)
    both = gather_rest(jnp.concatenate([cot_near, out_near], 0), jnp.concatenate([cot, out_t], 0), "col")
    q0, q1, kv, raw, f1_all = project_heads(
        marks, x_pieces, w_scaled, gains, cos, sin, segment)
    kv_sib = step_core(kv)
    joined, logs = attend(q0, q1, kv, kv_sib)
    joined_got = swap_all(joined)
    joined_got, *both = together(joined_got, *both)
    out_own = [v[:, 144:] for v in both]
    out_sib = step_core(jnp.stack(out_own))
    hidden, middle, wout_t = after_attention(marks, joined_got, out_own, out_sib, tokens, gain_second[None])
    mid_pair = step_pair(middle, "col")
    hidden, *both = together(hidden, *both)
    cot_own = jnp.stack([v[:, :144] for v in both])
    cot_sib = step_core(cot_own)
    gates = given_gates(marks, cot_own, cot_sib, inverse).reshape(4, 2, 2, 8, 128)
    pre0, pre1, cot0, cot1 = inner_products(cot_own, cot_sib, w_all)
    own0 = jnp.stack([mid_pair, middle])
    near0, far0 = step_ring(own0, "col", 1), step_ring(own0, "col", 3)
    near0, far0, own0, gates, pre0 = together(near0, far0, own0, gates, pre0)
    last0 = step_ring(own0, "col", 2)
    part = run_experts(marks, 0, jnp.stack([near0, far0, own0]), pre0, gates, w_all, lambda i: i + i // 2)
    last0, *part = together(last0, *part)
    mid0 = jnp.stack([near0, far0, last0, own0])
    mid1 = step_core(mid0)
    qkv_t, mid0 = together(qkv_t, mid0)
    wqkv_t = lax.all_gather(qkv_t, "col", axis=0, tiled=True)

    mid1, *part = together(mid1, *part)
    e_other, gg1, ug1, in1 = run_experts(marks, 5, mid1, pre1, gates, w_all)
    last0, e_other = together(last0, e_other)
    e_own, gg0, ug0, in0 = run_experts(marks, 0, last0[None], pre0, gates, w_all, lambda i: i + 2, part)
    entry = add_pair(e_own, step_core(e_other))
    entry, gg0 = together(entry, gg0)
    entry_got = swap_all(entry)
    in1, entry = together(in1, entry)
    r_other = results(marks, in1, w_all)
    grads = weight_grads(((mid0, mid1), (gg0, gg1)), ((mid0, mid1), (ug0, ug1)), ((cot0, cot1), (in0, in1)))

    entry_got, grads, r_other = together(entry_got, grads, r_other)
    r_got = step_core(r_other)
    grads = lax.psum_scatter(grads, "row", scatter_dimension=0, tiled=True)
    hidden_grad, hidden_low, joined_grad, second = second_back(entry_got, hidden, cotangent, gain_second[None], wout_t)
    joined_grad, in0 = together(joined_grad, in0)
    joined_grad = swap_all(joined_grad)
    r_sum = results(marks, in0, w_all, r_got).reshape(8, 128, D)
    hidden_near, r_sum = together(step_pair(hidden_low, "col"), r_sum)
    hidden_pair = jnp.stack([hidden_near, hidden_low])
    joined_grad, r_sum, hidden_pair = together(joined_grad, r_sum, hidden_pair)
    hidden_pieces = [step_ring(hidden_pair, "col", d) for d in AHEAD] + [hidden_pair]
    dq, dkv_own, dkv_other = attend_back(q0, q1, kv, kv_sib, joined, logs, joined_grad)
    dkv_got = step_core(dkv_other)
    raw_grad, raw_scaled, gain_heads = heads_back(dq, dkv_own, dkv_got, raw, f1_all, gains, cos, sin)
    raw_scaled, *hidden_pieces = together(raw_scaled, *hidden_pieces)
    own_q, other_q, sums = qkv_grads(
        marks, x_pieces, raw_scaled, w_chip, gain_column, second, gain_heads)
    sums_got = step_core(sums)
    own_o, other_o = out_grads(marks, hidden_pieces, joined)
    raw_got = swap_all(add_gains(sums, sums_got, raw_grad))
    keep, msg = pair_parts(marks, own_q, own_o, step_core(jnp.concatenate([other_q, other_o], 1)))
    msg_got = step_pair(msg, "row")
    sums = sum_gains(raw_got)
    raw_got, r_sum, msg_got, sums_got = together(raw_got, r_sum, msg_got, step_pair(sums, "row"))
    out_got = swap_all(r_sum)
    own, sums, *msgs = ring_parts(keep, msg_got, sums, sums_got)
    input_grad = first_back(raw_got, wqkv_t, tokens, gain_first[None], hidden_grad)
    input_grad, grads, *msgs = together(
        input_grad, grads, *[step_ring(m, "row", d) for m, d in zip(msgs, AHEAD)])
    grads_w = unpack(grads)
    grad_qkv, grad_out, sums = last_parts(own, sums, msgs)
    out_got, grad_qkv = together(out_got, grad_qkv)
    block_out = add_up(hidden, out_got)
    heads = sums[8]
    return (
        block_out,
        input_grad,
        sums[:4].reshape(-1),
        sums[4:8].reshape(-1),
        heads[:64] + heads[64:128],
        heads[128:192],
        grad_qkv,
        grad_out.T,
        *grads_w,
    )


def solution(mesh):
    both = P(("row", "col"), None)
    return jax.shard_map(
        body,
        mesh=mesh,
        in_specs=(both, both, P("row", None), P("row", None), both, both, P(), P(), P(), P(),
                  P("row", "col"), P("row", "col"), P("row", "col", None), P("row", "col", None),
                  P("row", "col", None)),
        out_specs=(both, both, P(), P(), P(), P(), P("row", "col"), P("row", "col"), P("row", "col", None),
                   P("row", "col", None), P("row", "col", None)),
        check_vma=False,
    )
```
